32 devices in a mesh: ws: 4 (over y, x), ctx: 8 (over z, core).
Axes of the slice: x: 2, y: 2, z: 4, core: 2. Of those that a mesh axis runs over, the one named last changes fastest.
Arguments:
- inputs: bfloat16 [8, 8192, 1600], P('ws', 'ctx'), may hold values from -6 to 6
- cotangent: bfloat16 [8, 8192, 1600], P('ws', 'ctx'), may hold values from -6 to 6
- block_ids: int32 [8, 8192], P('ws', 'ctx'), may hold values from 0 to 63, never falling along the last dimension, each value on 1 to 256 neighbouring positions
- first_gain: bfloat16 [1600], P('ws'), may hold values from 0.5 to 1.5
- first_shift: bfloat16 [1600], P('ws'), may hold values from -2 to 2
- weight_in: bfloat16 [1600, 800], P('ws'), may hold values from -0.15625 to 0.15625
- second_gain: bfloat16 [800], P('ws'), may hold values from 0.5 to 1.5
- second_shift: bfloat16 [800], P('ws'), may hold values from -2 to 2
- weight_conv: bfloat16 [5, 800, 800], P(None, 'ws'), may hold values from -0.09375 to 0.09375
- third_gain: bfloat16 [800], P('ws'), may hold values from 0.5 to 1.5
- third_shift: bfloat16 [800], P('ws'), may hold values from -2 to 2
- weight_out: bfloat16 [800, 1600], P('ws'), may hold values from -0.3125 to 0.3125
- output_bias: bfloat16 [1600], P('ws'), may hold values from -2 to 2
Outputs:
- block_output: bfloat16 [8, 8192, 1600], P('ws', 'ctx')
- input_grad: bfloat16 [8, 8192, 1600], P('ws', 'ctx')
- first_gain_grad: float32 [1600], P('ws')
- first_shift_grad: float32 [1600], P('ws')
- weight_in_grad: float32 [1600, 800], P('ws')
- second_gain_grad: float32 [800], P('ws')
- second_shift_grad: float32 [800], P('ws')
- weight_conv_grad: float32 [5, 800, 800], P(None, 'ws')
- third_gain_grad: float32 [800], P('ws')
- third_shift_grad: float32 [800], P('ws')
- weight_out_grad: float32 [800, 1600], P('ws')
- output_bias_grad: float32 [1600], P('ws')
The draws below stay inside these ranges and needn't reach their ends.
Inputs may be any that keep to these rules, and one draw needn't show every extreme that they name: `block_ids`: within a sequence the ids never fall, start at 0 and take every value up to 63; a block holds 1 to 256 tokens, and some block exactly 256.
All inputs are finite; a program needn't handle non-finite values.
Results may differ from the reference program's by a relative error of at most 0.017.
Values may be sent and summed in bfloat16 or wider, within the bound.
No kernel may reach another device: no remote copies, remote signals or barrier semaphores. Data moves between devices by JAX's collectives and lax.ppermute only.
A program may use at most 256 MiB of HBM per device.

```python
import math
import jax
import jax.numpy as jnp
import numpy as np
from jax import lax

D = 1600
INNER = 800
KERNEL_TAPS = 5
DILATION_STEP = 16
BLOCK = 256
LENGTH = 8192
SEQS = 8
COUNT = 64


def level_of(key, dims, cuts, low, largest):
    level, own = 1.0, jax.random.fold_in(key, 6)
    for dim, parts in cuts:
        draws = jnp.exp(jax.random.uniform(jax.random.fold_in(own, dim), (parts,), jnp.float32, low / len(cuts), largest / len(cuts)))
        level = level * jnp.repeat(draws, dims[dim] // parts).reshape([-1 if axis == dim else 1 for axis in range(len(dims))])
    return level


def profile(count, total, most, skew):
    portions = [(1 << 20) // math.isqrt(rank ** skew) + 1 for rank in range(2, count + 1)]
    spare, counts = total - most - (count - 1), [1] * (count - 1)
    while spare > 0:
        movable = [i for i in range(count - 1) if counts[i] < most]
        pool, budget = sum([portions[i] for i in movable]), spare
        for i in movable:
            more = min(most - counts[i], max(1, budget * portions[i] // pool), spare)
            counts[i] = counts[i] + more
            spare = spare - more
    return np.array([most] + counts)


def ragged_sizes(key, amount, total, reach, slope):
    if amount == 2:
        one = jax.random.randint(key, (), max(1, total - reach), min(reach, total - 1) + 1)
        return jnp.stack([one, total - one])
    lengths = jnp.asarray(profile(amount, total, reach, slope), jnp.int32)
    couples = (amount - 1) // 2
    giver, receiver = lengths[1:1 + 2 * couples:2], lengths[2:2 + 2 * couples:2]
    slack = jnp.minimum(giver - 1, reach - receiver)
    moved = jax.random.randint(jax.random.fold_in(key, 1), (couples,), 0, 1 << 20) % (slack + 1)
    lengths = lengths.at[1:1 + 2 * couples:2].set(giver - moved).at[2:2 + 2 * couples:2].set(receiver + moved)
    return lengths[jax.random.permutation(jax.random.fold_in(key, 2), amount)]


def noise(key, shape, scale, reach, split=(), dtype=jnp.bfloat16):
    values = scale * jax.random.normal(key, shape, jnp.float32)
    if split:
        values = values * level_of(key, shape, split, -0.22, 0.18)
    return jnp.clip(values, -reach, reach).astype(dtype)


def setup_inputs(seed: int = 0) -> dict:
    key_list = jax.random.split(jax.random.key(seed), 14)
    return {
        "inputs": noise(key_list[0], (SEQS, LENGTH, D), 1.0, 6.0, ((0, 4), (1, 8))),
        "cotangent": noise(key_list[1], (SEQS, LENGTH, D), 1.0, 6.0, ((0, 4), (1, 8))),
        "block_ids": jax.vmap(lambda own: jnp.searchsorted(jnp.cumsum(ragged_sizes(own, COUNT, LENGTH, BLOCK, 1)), jnp.arange(LENGTH), side="right"))(jax.random.split(key_list[2], SEQS)).reshape((SEQS, LENGTH)).astype(jnp.int32),
        "first_gain": jnp.clip(1.0 + 0.1 * jax.random.normal(key_list[3], (D,), jnp.float32), 0.5, 1.5).astype(jnp.bfloat16),
        "first_shift": noise(key_list[4], (D,), 0.5, 2.0, ((0, 4),)),
        "weight_in": noise(key_list[5], (D, INNER), D ** -0.5, 0.15625, ((0, 4),)),
        "second_gain": jnp.clip(1.0 + 0.1 * jax.random.normal(key_list[6], (INNER,), jnp.float32), 0.5, 1.5).astype(jnp.bfloat16),
        "second_shift": noise(key_list[7], (INNER,), 0.5, 2.0, ((0, 4),)),
        "weight_conv": noise(key_list[8], (KERNEL_TAPS, INNER, INNER), (KERNEL_TAPS * INNER) ** -0.5, 0.09375, ((1, 4),)),
        "third_gain": jnp.clip(1.0 + 0.1 * jax.random.normal(key_list[9], (INNER,), jnp.float32), 0.5, 1.5).astype(jnp.bfloat16),
        "third_shift": noise(key_list[10], (INNER,), 0.5, 2.0, ((0, 4),)),
        "weight_out": noise(key_list[11], (INNER, D), (INNER // 2) ** -0.5, 0.3125, ((0, 4),)),
        "output_bias": noise(key_list[12], (D,), 0.5, 2.0, ((0, 4),)),
    }


EPS = 1e-05

@jax.custom_vjp
def low(v):
    return lax.optimization_barrier(v.astype(jnp.bfloat16)).astype(jnp.float32)

@jax.custom_vjp
def low_back(v):
    return v

def low_keep(v):
    return (low(v), None)

def low_pass(kept, grad):
    return (grad,)

def back_keep(v):
    return (v, None)

def back_low(kept, grad):
    return (low(grad),)
low.defvjp(low_keep, low_pass)
low_back.defvjp(back_keep, back_low)

def matmul_high(left, right):
    return jnp.dot(left, right, precision=lax.Precision.HIGHEST)

def norm_silu(values, gain, shift):
    middle = lax.optimization_barrier(jnp.mean(values, axis=-1, keepdims=True))
    centred = values - middle
    spread = lax.optimization_barrier(jnp.mean(centred * centred, axis=-1, keepdims=True))
    return jax.nn.silu(centred * lax.rsqrt(spread + EPS) * gain + shift)

def residual_block_forward(params, seq_rows, own_ids):
    first_gain, first_shift, weight_in, second_gain, second_shift, weight_conv, third_gain, third_shift, weight_out, output_bias = params
    first_activation = low(norm_silu(seq_rows, first_gain, first_shift))
    proj_one = low_back(matmul_high(first_activation, weight_in))
    act_two = low(norm_silu(proj_one, second_gain, second_shift))
    length = act_two.shape[0]
    border_width = KERNEL_TAPS // 2 * DILATION_STEP
    padded = jnp.pad(act_two, ((border_width, border_width), (0, 0)))
    padded_ids = jnp.pad(own_ids, (border_width, border_width), constant_values=-1)
    conv = jnp.zeros((length, weight_conv.shape[2]), jnp.float32)
    for kernel_tap_index in range(KERNEL_TAPS):
        tap_displacement = (kernel_tap_index - KERNEL_TAPS // 2) * DILATION_STEP
        tap_rows = padded[border_width + tap_displacement:border_width + tap_displacement + length]
        if tap_displacement > 0:
            keep_mask = (padded_ids[border_width + tap_displacement:border_width + tap_displacement + length] == own_ids).astype(jnp.float32)
            tap_rows = tap_rows * keep_mask[:, None]
        conv = conv + matmul_high(tap_rows, weight_conv[kernel_tap_index])
    conv = low_back(conv)
    act_three = low(norm_silu(conv, third_gain, third_shift))
    proj_two = low_back(matmul_high(act_three, weight_out))
    return seq_rows + proj_two + output_bias

def reference(inputs, cotangent, block_ids, first_gain, first_shift, weight_in, second_gain, second_shift, weight_conv, third_gain, third_shift, weight_out, output_bias):
    params = tuple((value.astype(jnp.float32) for value in (first_gain, first_shift, weight_in, second_gain, second_shift, weight_conv, third_gain, third_shift, weight_out, output_bias)))

    def per_sequence(running, sequence_item):
        seq_rows, seq_grad, own_ids = sequence_item

        def forward_of(param_set, rows_in):
            return residual_block_forward(param_set, rows_in, own_ids)
        result, pullback = jax.vjp(forward_of, params, seq_rows.astype(jnp.float32))
        param_grads, rows_grad = pullback(seq_grad.astype(jnp.float32))
        running = tuple((total + extra for total, extra in zip(running, param_grads)))
        return (running, (result.astype(jnp.bfloat16), rows_grad.astype(jnp.bfloat16)))
    zeros = tuple((jnp.zeros_like(value) for value in params))
    totals, (outputs, in_grads) = lax.scan(per_sequence, zeros, (inputs, cotangent, block_ids))
    return (outputs, in_grads, totals[0], totals[1], totals[2], totals[3], totals[4], totals[5], totals[6], totals[7], totals[8], totals[9])
```

```python
import functools
import jax
import jax.numpy as jnp
from jax import lax
from jax.experimental import pallas as pl
from jax.experimental.pallas import tpu as pltpu
from jax.sharding import PartitionSpec as P

KERNEL_TAPS = 5
DILATION_STEP = 16
EPS = 1e-05
LANES = 128
BORDER = KERNEL_TAPS // 2 * DILATION_STEP
F32 = jnp.float32
BF16 = jnp.bfloat16
VMEM_BYTES = 60 * 2**20

NN = (((1,), (0,)), ((), ()))
NT = (((1,), (1,)), ((), ()))


def params(steps=0):
    return pltpu.CompilerParams(
        dimension_semantics=("arbitrary",) * steps or None, vmem_limit_bytes=VMEM_BYTES
    )


def cost(flops, bytes_accessed):
    return pl.CostEstimate(flops=flops, bytes_accessed=bytes_accessed, transcendentals=0)


def shape(dims, dtype=BF16):
    return jax.ShapeDtypeStruct(dims, dtype)


def dot(left, right, dims=NN):
    return lax.dot_general(left, right, dims, preferred_element_type=F32)


def wide(column, lanes):
    return jnp.concatenate([column] * (lanes // LANES), axis=1)


def folded(values):
    total = values[:, :LANES]
    for at in range(LANES, values.shape[1], LANES):
        total = total + values[:, at : at + LANES]
    return total


def logistic(x):
    return 0.5 * jnp.tanh(0.5 * x) + 0.5


def vector(rows, block):
    return pl.BlockSpec((rows, LANES), lambda *_: (block, 0))


def here(rows, lanes, seq=0):
    return pl.BlockSpec((1, rows, lanes), lambda s, t: (s + seq, 0, t))


def held(dims):
    return pl.BlockSpec(dims, lambda *_: (0,) * len(dims))


def each(count, body, init, unroll=5):
    return lax.fori_loop(0, count, body, init, unroll=unroll)


def rows_at(index, size):
    return pl.ds(pl.multiple_of(index * size, size), size)


def row_stats(load, channels, chunk, lanes):
    steps = channels // chunk
    zero = jnp.zeros((chunk, lanes), F32)
    total = each(steps, lambda i, t: t + load(i), zero)
    mean = jnp.sum(total, axis=0, keepdims=True) * (1.0 / channels)

    def square(i, t):
        centred = load(i) - mean
        return t + centred * centred

    squares = each(steps, square, zero)
    spread = jnp.sum(squares, axis=0, keepdims=True) * (1.0 / channels)
    return mean, lax.rsqrt(spread + EPS)


def back_first(u, normed, gain, shift):
    pre = normed * gain + shift
    sigma = logistic(pre)
    p = u * (sigma * (1.0 + pre * (1.0 - sigma)))
    return pre, sigma, p, p * gain


def first_step():
    return (pl.program_id(0) == 0) & (pl.program_id(1) == 0)


def last_step():
    return (pl.program_id(0) == pl.num_programs(0) - 1) & (
        pl.program_id(1) == pl.num_programs(1) - 1
    )


def cleared(sums):
    @pl.when(first_step())
    def _():
        sums[...] = jnp.zeros_like(sums)


def handed(sums, out):
    @pl.when(last_step())
    def _():
        out[...] = sums[...]


def open_kernel(x, gain, shift, act1, stats, *, chunk):
    lanes, width = x.shape[2], x.shape[1]
    load = lambda i: x[0, rows_at(i, chunk), :].astype(F32)
    mean, scale = row_stats(load, width, chunk, lanes)

    def activate(i, carry):
        at = rows_at(i, chunk)
        normed = (load(i) - mean) * scale
        pre = normed * wide(gain[at, :], lanes) + wide(shift[at, :], lanes)
        act1[0, at, :] = (pre * logistic(pre)).astype(BF16)
        return carry

    each(width // chunk, activate, 0)
    stats[0] = jnp.concatenate([mean, scale, jnp.zeros((6, lanes), F32)], axis=0)


def open_block(x, vectors, lanes=512, chunk=32):
    seqs, width, length = x.shape
    return pl.pallas_call(
        functools.partial(open_kernel, chunk=chunk),
        grid=(seqs, length // lanes),
        in_specs=[here(width, lanes), vector(width, 0), vector(width, 1)],
        out_specs=[here(width, lanes), here(8, lanes)],
        out_shape=[shape(x.shape), shape((seqs, 8, length), F32)],
        compiler_params=params(2),
        cost_estimate=cost(40 * x.size, 4 * x.size),
        name="open_block",
    )(x, vectors, vectors)


def enter_kernel(act1, w_in, gain, shift, act2, turned, normed2, stats, proj, *, chunk):
    lanes, inner = act1.shape[2], act2.shape[1]
    proj[...] = dot(w_in[...], act1[0])
    load = lambda i: proj[rows_at(i, chunk), :]
    mean, scale = row_stats(load, inner, chunk, lanes)

    def activate(i, carry):
        at = rows_at(i, chunk)
        normed = (load(i) - mean) * scale
        normed2[0, at, :] = normed
        pre = normed * wide(gain[at, :], lanes) + wide(shift[at, :], lanes)
        act2[0, at, :] = (pre * logistic(pre)).astype(BF16)
        return carry

    each(inner // chunk, activate, 0)
    turned[0] = act2[0].T
    stats[0] = jnp.concatenate([scale, jnp.zeros((7, lanes), F32)], axis=0)


def enter(act1, w_in_t, vectors, lanes=512, chunk=32):
    seqs, width, length = act1.shape
    inner = w_in_t.shape[0]
    return pl.pallas_call(
        functools.partial(enter_kernel, chunk=chunk),
        grid=(seqs, length // lanes),
        in_specs=[here(width, lanes), held((inner, width)), vector(inner, 6), vector(inner, 7)],
        out_specs=[
            here(inner, lanes),
            pl.BlockSpec((1, lanes, inner), lambda s, t: (s, t, 0)),
            here(inner, lanes),
            here(8, lanes),
        ],
        out_shape=[
            shape((seqs, inner, length)),
            shape((seqs, length, inner)),
            shape((seqs, inner, length), F32),
            shape((seqs, 8, length), F32),
        ],
        scratch_shapes=[pltpu.VMEM((inner, lanes), F32)],
        compiler_params=params(2),
        cost_estimate=cost(2 * act1.size * inner, seqs * length * (2 * width + 8 * inner)),
        name="enter",
    )(act1, w_in_t, vectors, vectors)


def project_kernel(weight, columns, out, grads, sums, *, chunk):
    cleared(sums)
    out[0] = dot(weight[...], columns[0])

    def body(i, carry):
        at = rows_at(i, chunk)
        sums[at, :] += folded(columns[0, at, :].astype(F32))
        return carry

    each(columns.shape[1] // chunk, body, 0)
    handed(sums, grads)


def project(weight, columns, lanes=512, chunk=32):
    seqs, depth, length = columns.shape
    rows = weight.shape[0]
    return pl.pallas_call(
        functools.partial(project_kernel, chunk=chunk),
        grid=(seqs, length // lanes),
        in_specs=[held((rows, depth)), here(depth, lanes)],
        out_specs=[here(rows, lanes), held((depth, LANES))],
        out_shape=[shape((seqs, rows, length), F32), shape((depth, LANES), F32)],
        scratch_shapes=[pltpu.VMEM((depth, LANES), F32)],
        compiler_params=params(2),
        cost_estimate=cost(2 * columns.size * rows, seqs * length * (2 * depth + 4 * rows)),
        name="project",
    )(weight, columns)


def extend(rows, before, after, mask, whole, masked, seq, sign):
    length = rows.shape[1]
    whole[:BORDER, :] = before[seq]
    whole[BORDER : BORDER + length, :] = rows[seq]
    whole[BORDER + length :, :] = after[seq]
    inner = rows.shape[2]
    chunk = 128
    for later in range(KERNEL_TAPS // 2):
        by = sign * (later + 1) * DILATION_STEP

        def body(i, carry, later=later, by=by):
            kept = mask[seq, later, rows_at(i, chunk), :]
            kept = jnp.concatenate([kept] * -(-inner // LANES), axis=1)[:, :inner]
            start = pl.multiple_of(i * chunk + BORDER + by, DILATION_STEP)
            masked[later, rows_at(i, chunk), :] = whole[pl.ds(start, chunk), :] * kept
            return carry

        each(length // chunk, body, 0, 1)


def tap_rows(whole, masked, tap, sign, start, count):
    by = (tap - KERNEL_TAPS // 2) * DILATION_STEP
    if by > 0:
        return masked[tap - KERNEL_TAPS // 2 - 1, pl.ds(start, count), :]
    return whole[pl.ds(start + (BORDER + sign * by), count), :]


def conv_kernel(rows, before, after, mask, w_conv, gain, shift, upstream, act3, turned, grads, whole, masked, conv, scaled, low, sums, *, chunk):
    tile = pl.program_id(1)
    lanes, inner = act3.shape[2], act3.shape[1]
    cleared(sums)

    @pl.when(tile == 0)
    def _():
        extend(rows, before, after, mask, whole, masked, 0, 1)

    start = pl.multiple_of(tile * lanes, lanes)
    total = None
    for tap in range(KERNEL_TAPS):
        part = dot(w_conv[tap], tap_rows(whole, masked, tap, 1, start, lanes), NT)
        total = part if total is None else total + part
    conv[...] = total
    load = lambda i: conv[rows_at(i, chunk), :]
    mean, scale = row_stats(load, inner, chunk, lanes)

    def first(i, carry):
        at = rows_at(i, chunk)
        normed = (load(i) - mean) * scale
        gains = wide(gain[at, :], lanes)
        pre, sigma, p, q = back_first(upstream[0, at, :], normed, gains, wide(shift[at, :], lanes))
        act3[0, at, :] = (pre * sigma).astype(BF16)
        conv[at, :] = normed
        scaled[at, :] = q
        sums[0, at, :] += folded(p * normed)
        sums[1, at, :] += folded(p)
        return carry[0] + q, carry[1] + q * normed

    zero = jnp.zeros((chunk, lanes), F32)
    one, two = each(inner // chunk, first, (zero, zero))
    one = jnp.sum(one, axis=0, keepdims=True) * (1.0 / inner)
    two = jnp.sum(two, axis=0, keepdims=True) * (1.0 / inner)

    def second(i, carry):
        at = rows_at(i, chunk)
        low[at, :] = (scale * (scaled[at, :] - one - conv[at, :] * two)).astype(BF16)
        return carry

    each(inner // chunk, second, 0)
    turned[0] = low[...].T
    handed(sums, grads)


def conv_block(rows, before, after, mask, w_conv_t, vectors, upstream, lanes=512, chunk=16):
    seqs, length, inner = rows.shape
    seq = lambda *dims: pl.BlockSpec((1, *dims), lambda s, t: (s,) + (0,) * len(dims))
    return pl.pallas_call(
        functools.partial(conv_kernel, chunk=chunk),
        grid=(seqs, length // lanes),
        in_specs=[
            seq(length, inner),
            seq(BORDER, inner),
            seq(BORDER, inner),
            seq(2, length, LANES),
            held(w_conv_t.shape),
            vector(inner, 8),
            vector(inner, 9),
            here(inner, lanes),
        ],
        out_specs=[
            here(inner, lanes),
            pl.BlockSpec((1, lanes, inner), lambda s, t: (s, t, 0)),
            held((2, inner, LANES)),
        ],
        out_shape=[
            shape((seqs, inner, length)),
            shape((seqs, length, inner)),
            shape((2, inner, LANES), F32),
        ],
        scratch_shapes=[
            pltpu.VMEM((length + 2 * BORDER, inner), BF16),
            pltpu.VMEM((KERNEL_TAPS // 2, length, inner), BF16),
            pltpu.VMEM((inner, lanes), F32),
            pltpu.VMEM((inner, lanes), F32),
            pltpu.VMEM((inner, lanes), BF16),
            pltpu.VMEM((2, inner, LANES), F32),
        ],
        compiler_params=params(2),
        cost_estimate=cost(2 * rows.size * w_conv_t.size // inner, 12 * rows.size),
        name="conv_block",
    )(rows, before, after, mask, w_conv_t, vectors, vectors, upstream)


def conv_back_kernel(rows, before, after, mask, w_conv, gain, shift, normed2, stats, *rest, chunk):
    out, grads, whole, masked, grad, scaled, sums = rest[-7:]
    tile = pl.program_id(1)
    lanes, inner = out.shape[2], out.shape[1]
    cleared(sums)

    @pl.when(tile == 0)
    def _():
        extend(rows, before, after, mask, whole, masked, 0, -1)

    start = pl.multiple_of(tile * lanes, lanes)
    total = None
    for tap in range(KERNEL_TAPS):
        part = dot(w_conv[tap], tap_rows(whole, masked, tap, -1, start, lanes), NT)
        total = part if total is None else total + part
    grad[...] = total
    scale = stats[0, 0:1, :]

    def first(i, carry):
        at = rows_at(i, chunk)
        normed = normed2[0, at, :]
        _, _, p, q = back_first(
            grad[at, :], normed, wide(gain[at, :], lanes), wide(shift[at, :], lanes)
        )
        scaled[at, :] = q
        sums[0, at, :] += folded(p * normed)
        sums[1, at, :] += folded(p)
        return carry[0] + q, carry[1] + q * normed

    zero = jnp.zeros((chunk, lanes), F32)
    one, two = each(inner // chunk, first, (zero, zero))
    one = jnp.sum(one, axis=0, keepdims=True) * (1.0 / inner)
    two = jnp.sum(two, axis=0, keepdims=True) * (1.0 / inner)

    def second(i, carry):
        at = rows_at(i, chunk)
        out[0, at, :] = (scale * (scaled[at, :] - one - normed2[0, at, :] * two)).astype(BF16)
        return carry

    each(inner // chunk, second, 0)
    handed(sums, grads)


def conv_back(rows, before, after, mask, w_conv, vectors, normed2, stats, first, count, into=None, lanes=512, chunk=16):
    seqs, length, inner = rows.shape
    seq = lambda *dims: pl.BlockSpec((1, *dims), lambda s, t: (s + first,) + (0,) * len(dims))
    more = () if into is None else (into,)
    return pl.pallas_call(
        functools.partial(conv_back_kernel, chunk=chunk),
        grid=(count, length // lanes),
        in_specs=[
            seq(length, inner),
            seq(BORDER, inner),
            seq(BORDER, inner),
            seq(2, length, LANES),
            held(w_conv.shape),
            vector(inner, 6),
            vector(inner, 7),
            here(inner, lanes, first),
            here(8, lanes, first),
        ]
        + [pl.BlockSpec(memory_space=pl.ANY)] * len(more),
        out_specs=[here(inner, lanes, first), held((2, inner, LANES))],
        input_output_aliases={9: 0} if more else {},
        out_shape=[shape((seqs, inner, length)), shape((2, inner, LANES), F32)],
        scratch_shapes=[
            pltpu.VMEM((length + 2 * BORDER, inner), BF16),
            pltpu.VMEM((KERNEL_TAPS // 2, length, inner), BF16),
            pltpu.VMEM((inner, lanes), F32),
            pltpu.VMEM((inner, lanes), F32),
            pltpu.VMEM((2, inner, LANES), F32),
        ],
        compiler_params=params(2),
        cost_estimate=cost(2 * rows.size * w_conv.size * count // (seqs * inner), 10 * rows.size * count // seqs),
        name="conv_back",
    )(rows, before, after, mask, w_conv, vectors, vectors, normed2, stats, *more)


def leave_kernel(low, w_in, x, g, gain, shift, stats, *rest, chunk):
    out, grads, grad, sums = rest[-4:]
    lanes, width = out.shape[2], out.shape[1]
    cleared(sums)
    grad[...] = dot(w_in[...], low[0])
    mean = stats[0, 0:1, :]
    scale = stats[0, 1:2, :]
    norm = lambda at: (x[0, at, :].astype(F32) - mean) * scale

    def first(i, carry):
        at = rows_at(i, chunk)
        normed = norm(at)
        _, _, p, q = back_first(
            grad[at, :], normed, wide(gain[at, :], lanes), wide(shift[at, :], lanes)
        )
        grad[at, :] = q
        sums[0, at, :] += folded(p * normed)
        sums[1, at, :] += folded(p)
        return carry[0] + q, carry[1] + q * normed

    zero = jnp.zeros((chunk, lanes), F32)
    one, two = each(width // chunk, first, (zero, zero))
    one = jnp.sum(one, axis=0, keepdims=True) * (1.0 / width)
    two = jnp.sum(two, axis=0, keepdims=True) * (1.0 / width)

    def second(i, carry):
        at = rows_at(i, chunk)
        branch = scale * (grad[at, :] - one - norm(at) * two)
        out[0, at, :] = (g[0, at, :].astype(F32) + branch).astype(BF16)
        return carry

    each(width // chunk, second, 0)
    handed(sums, grads)


def leave(low, w_in, x, g, vectors, stats, first, count, into=None, lanes=512, chunk=16):
    seqs, inner, length = low.shape
    width = x.shape[1]
    more = () if into is None else (into,)
    return pl.pallas_call(
        functools.partial(leave_kernel, chunk=chunk),
        grid=(count, length // lanes),
        in_specs=[
            here(inner, lanes, first),
            held((width, inner)),
            here(width, lanes, first),
            here(width, lanes, first),
            vector(width, 0),
            vector(width, 1),
            here(8, lanes, first),
        ]
        + [pl.BlockSpec(memory_space=pl.ANY)] * len(more),
        input_output_aliases={7: 0} if more else {},
        out_specs=[here(width, lanes, first), held((2, width, LANES))],
        out_shape=[shape(x.shape), shape((2, width, LANES), F32)],
        scratch_shapes=[pltpu.VMEM((width, lanes), F32), pltpu.VMEM((2, width, LANES), F32)],
        compiler_params=params(2),
        cost_estimate=cost(2 * low.size * width * count // seqs, (2 * low.size + 6 * x.size) * count // seqs),
        name="leave",
    )(low, w_in, x, g, vectors, vectors, stats, *more)


def finish_kernel(w_out, act3, x, bias, *rest, chunk):
    out, proj = rest[-2:]
    lanes, width = out.shape[2], out.shape[1]
    proj[...] = dot(w_out[...], act3[0])

    def body(i, carry):
        at = rows_at(i, chunk)
        out[0, at, :] = (x[0, at, :].astype(F32) + proj[at, :] + wide(bias[at, :], lanes)).astype(BF16)
        return carry

    each(width // chunk, body, 0)


def finish(w_out_t, act3, x, vectors, first, count, into=None, lanes=512, chunk=32):
    more = () if into is None else (into,)
    seqs, inner, length = act3.shape
    width = x.shape[1]
    return pl.pallas_call(
        functools.partial(finish_kernel, chunk=chunk),
        grid=(count, length // lanes),
        in_specs=[held((width, inner)), here(inner, lanes, first), here(width, lanes, first), vector(width, 2)]
        + [pl.BlockSpec(memory_space=pl.ANY)] * len(more),
        input_output_aliases={4: 0} if more else {},
        out_specs=here(width, lanes, first),
        out_shape=shape(x.shape),
        scratch_shapes=[pltpu.VMEM((width, lanes), F32)],
        compiler_params=params(2),
        cost_estimate=cost(2 * act3.size * width * count // seqs, (2 * act3.size + 4 * x.size) * count // seqs),
        name="finish",
    )(w_out_t, act3, x, vectors, *more)


def outer_kernel(at, left, right, *rest, count):
    got, outs, total = rest[:-3] if count else (), rest[-3:-1] if count else rest[-2:-1], rest[-1]
    value = None
    for s in range(left.shape[0]):
        part = dot(left[s], right[s], NT)
        value = part if value is None else value + part
    if not count:
        outs[0][...] = value.astype(BF16)
        return
    total[...] = value + got[0][...].astype(F32)
    rows = outs[0].shape[0]
    for step, out in enumerate(outs):
        start = pl.multiple_of((at[1] ^ step) * rows, 8)
        out[...] = total[pl.ds(start, rows), :].astype(BF16)


def outer(at, left, right, got=None):
    seqs, height, length = left.shape
    width = right.shape[1]
    half = height // 2
    specs = [
        pl.BlockSpec((seqs, half, length), lambda i, at: (0, at[0], 0)),
        pl.BlockSpec((seqs, width, length), lambda i, at: (0, 0, 0)),
    ]
    if got is None:
        outs, out_specs = shape((half, width)), held((half, width))
    else:
        specs.append(held((half, width)))
        outs = [shape((half // 2, width))] * 2
        out_specs = [held((half // 2, width))] * 2
    return pl.pallas_call(
        functools.partial(outer_kernel, count=0 if got is None else 2),
        grid_spec=pltpu.PrefetchScalarGridSpec(
            num_scalar_prefetch=1,
            grid=(1,),
            in_specs=specs,
            out_specs=out_specs,
            scratch_shapes=[pltpu.VMEM((half, width) if got is not None else (8, LANES), F32)],
        ),
        out_shape=outs,
        compiler_params=params(1),
        cost_estimate=cost(seqs * length * height * width, 2 * seqs * length * (height + width)),
        name="outer",
    )(at, left, right, *(() if got is None else (got,)))


def outer_taps_kernel(at, left, rows, before, after, mask, *rest, first, groups, keep):
    got = rest[0] if keep else None
    outs = rest[1:3] if keep else rest[: len(groups)]
    whole, masked, total = rest[-3:]
    seqs, length = rows.shape[0], rows.shape[1]
    for seq in range(seqs):
        extend(rows, before, after, mask, whole.at[seq], masked.at[seq], seq, -1)
    places = [(group, i) for group, size in enumerate(groups) for i in range(size)]
    for step, (group, i) in enumerate(places):
        value = None
        for seq in range(seqs):
            right = tap_rows(whole.at[seq], masked.at[seq], first + step, -1, 0, length)
            part = dot(left[seq], right)
            value = part if value is None else value + part
        if not keep:
            outs[group][i] = value.astype(BF16)
            continue
        total[...] = value + got[i].astype(F32)
        size = outs[0].shape[1]
        for place, out in enumerate(outs):
            start = pl.multiple_of((at[1] ^ place) * size, 8)
            out[i] = total[pl.ds(start, size), :].astype(BF16)


def outer_taps(at, left, rows, before, after, mask, first, groups, got=None):
    seqs, length, inner = rows.shape
    half = inner // 2
    keep = got is not None
    specs = [
        pl.BlockSpec((seqs, half, length), lambda i, at: (0, at[0], 0)),
        held(rows.shape),
        held(before.shape),
        held(after.shape),
        held(mask.shape),
    ]
    if keep:
        specs.append(held((groups[0], half, inner)))
        dims = [(groups[0], half // 2, inner)] * 2
    else:
        dims = [(count, half, inner) for count in groups]
    return pl.pallas_call(
        functools.partial(outer_taps_kernel, first=first, groups=groups, keep=keep),
        grid_spec=pltpu.PrefetchScalarGridSpec(
            num_scalar_prefetch=1,
            grid=(1,),
            in_specs=specs,
            out_specs=[held(d) for d in dims],
            scratch_shapes=[
                pltpu.VMEM((seqs, length + 2 * BORDER, inner), BF16),
                pltpu.VMEM((seqs, KERNEL_TAPS // 2, length, inner), BF16),
                pltpu.VMEM((half, inner), F32),
            ],
        ),
        out_shape=[shape(d) for d in dims],
        compiler_params=params(1),
        cost_estimate=cost(rows.size * inner * sum(groups), 4 * rows.size),
        name="outer_taps",
    )(at, left, rows, before, after, mask, *((got,) if keep else ()))


def flip_kernel(w, out):
    for tap in range(w.shape[0]):
        out[tap] = w[tap].T


def flip(w):
    taps, rows, columns = w.shape
    return pl.pallas_call(
        flip_kernel,
        out_shape=shape((taps, columns, rows)),
        compiler_params=params(),
        cost_estimate=cost(0, 4 * w.size),
        name="flip",
    )(w)


def assemble_kernel(at, own, mine, other, natural, turned, whole, *, gap):
    rows, half = own.shape[0], mine.shape[1]
    whole[pl.ds(pl.multiple_of(at[0] * rows, 8), rows), :] = own[...].astype(F32)
    for step in range(mine.shape[0]):
        for pieces, core in ((mine, at[1]), (other, 1 - at[1])):
            start = (at[0] ^ (step + 1)) * rows + core * (rows - half)
            whole[pl.ds(pl.multiple_of(start, 8), half), :] = pieces[step].astype(F32)
    natural[...] = whole[...].astype(BF16)
    turned[...] = natural[...].T


def assemble(at, own, mine, other):
    rows, columns = own.shape
    full = rows * (mine.shape[0] + 1)
    dims = [(full, columns), (columns, full)]
    return pl.pallas_call(
        functools.partial(assemble_kernel, gap=0),
        grid_spec=pltpu.PrefetchScalarGridSpec(
            num_scalar_prefetch=1,
            grid=(1,),
            in_specs=[held(own.shape), held(mine.shape), held(other.shape)],
            out_specs=[held(d) for d in dims],
            scratch_shapes=[pltpu.VMEM((full, columns), F32)],
        ),
        out_shape=[shape(d) for d in dims],
        compiler_params=params(1),
        cost_estimate=cost(0, 6 * full * columns),
        name="assemble",
    )(at, own, mine, other)


def join_kernel(pieces, natural, turned, whole, *, rows):
    count, half = pieces.shape[0], pieces.shape[3]
    for shard in range(count):
        for core in range(2):
            start = shard * rows + core * (rows - half)
            whole[start : start + half, :] = pieces[shard, core, 0].astype(F32)
    natural[0] = whole[...].astype(BF16)
    turned[0] = natural[0].T


def join(pieces, rows):
    count, cores, taps, half, columns = pieces.shape
    full = count * rows
    dims = [(taps, full, columns), (taps, columns, full)]
    return pl.pallas_call(
        functools.partial(join_kernel, rows=rows),
        grid=(taps,),
        in_specs=[pl.BlockSpec((count, cores, 1, half, columns), lambda t: (0, 0, t, 0, 0))],
        out_specs=[pl.BlockSpec((1, *d[1:]), lambda t: (t, 0, 0)) for d in dims],
        out_shape=[shape(d) for d in dims],
        scratch_shapes=[pltpu.VMEM((full, columns), F32)],
        compiler_params=params(1),
        cost_estimate=cost(0, 6 * taps * full * columns),
        name="join",
    )(pieces)


def spread_kernel(at, parts, out, rows, *, sizes):
    count = parts.shape[0]
    for i in range(count):
        rows[pl.ds(at[0] ^ i, 1), :] = parts[i : i + 1, :]
    start, base = 0, 0
    for size in sizes:
        for shard in range(count):
            row = rows[shard : shard + 1, start : start + size]
            out[base : base + size, :] = jnp.broadcast_to(row, (LANES, size)).T
            base += size
        start += size


def spread(at, parts, sizes):
    total = parts.size
    return pl.pallas_call(
        functools.partial(spread_kernel, sizes=sizes),
        grid_spec=pltpu.PrefetchScalarGridSpec(
            num_scalar_prefetch=1,
            grid=(1,),
            in_specs=[held(parts.shape)],
            out_specs=held((total, LANES)),
            scratch_shapes=[pltpu.VMEM(parts.shape, F32)],
        ),
        out_shape=shape((total, LANES), F32),
        compiler_params=params(1),
        cost_estimate=cost(0, 4 * LANES * total),
        name="spread",
    )(at, parts)


def after(value, *others):
    return lax.optimization_barrier((value, *others))[0] if others else value


def swapped(x):
    return lax.ppermute(x, "core", [(0, 1), (1, 0)])


def from_ws(x, bit):
    return lax.ppermute(x, "ws", [(i, i ^ bit) for i in range(lax.axis_size("ws"))])


def neighbours(first, last):
    runs = lax.axis_size("run") * 2
    up = [(i, i + 1) for i in range(runs - 1)]
    down = [(i + 1, i) for i in range(runs - 1)]
    return lax.ppermute(last, ("run", "core"), up), lax.ppermute(first, ("run", "core"), down)


def square():
    return lax.axis_size("ws") == 4 and lax.axis_size("run") == 4


def halved(rows):
    return -(-rows // 16) * 8


def fetched(shard):
    rows = shard.shape[0]
    half = halved(rows)
    own = lax.dynamic_slice_in_dim(shard, lax.axis_index("core") * (rows - half), half, axis=0)
    return [from_ws(own, bit) for bit in (1, 2, 3)]


def whole_weight(at, shard, pieces):
    if pieces is None:
        natural = lax.all_gather(shard, "ws", axis=0, tiled=True)
        return natural, flip(natural[None])[0]
    mine = jnp.stack(pieces)
    return assemble(at, shard, mine, swapped(mine))


def conv_weights(shard):
    taps, rows, columns = shard.shape
    half = halved(rows)
    own = lax.dynamic_slice_in_dim(shard, lax.axis_index("core") * (rows - half), half, axis=1)
    pieces = lax.all_gather(own, ("ws", "core"), axis=0)
    return pieces.reshape(-1, 2, taps, half, columns)


def summed(*terms):
    total = terms[0].astype(F32)
    for term in terms[1:]:
        total = total + term.astype(F32)
    return total.astype(BF16)


def active(shard):
    return shard >> 1


class Share:
    def __init__(self, first, second):
        self.sum, self.second, self.came = first, second, ()

    def land(self, *kernels):
        came = after(self.came, *kernels)
        if self.second is None and self.last:
            run = lax.axis_index("run")
            self.sum = jnp.where((run == 1) | (run == 2), self.sum, came[0])
        else:
            self.sum = summed(self.sum, *came)
        self.second = None
        return self.sum

    def spread(self):
        near = [(2 * i + active(i), 2 * (i ^ 1) + active(i)) for i in range(4)]
        far = lambda bit: [(2 * i + 1 - active(i), 2 * (i ^ bit) + 1 - active(i)) for i in range(4)]
        move = lambda x, pairs: lax.ppermute(x, ("ws", "core"), pairs)
        self.came = (move(self.second, near), move(self.sum, far(2)), move(self.second, far(3)))

    def along(self, *pairs):
        every = []
        for shard in range(4):
            every += [((shard * 4 + i) * 2 + active(shard), (shard * 4 + j) * 2 + active(shard)) for i, j in pairs]
        self.came = (lax.ppermute(self.sum, ("ws", "run", "core"), every),)

    def inward(self):
        self.along((0, 1), (3, 2))
        self.last = False

    def middle(self):
        self.along((1, 2), (2, 1))

    def outward(self):
        self.along((1, 0), (2, 3))
        self.last = True

    def both(self):
        shard, core = lax.axis_index("ws"), lax.axis_index("core")
        pairs = [(2 * i + active(i), 2 * i + 1 - active(i)) for i in range(4)]
        other = lax.ppermute(self.sum, ("ws", "core"), pairs)
        return jnp.where(core == active(shard), self.sum, other).astype(F32)


def plain(low, high, axis):
    whole = jnp.concatenate([low, high], axis=axis)
    owned = lax.psum_scatter(whole, "ws", scatter_dimension=axis, tiled=True)
    return lax.psum(owned, ("run", "core")).astype(F32)


def small_sums(sums):
    if not square():
        return lax.psum(sums, ("ws", "run", "core"))
    sums = sums + swapped(sums)
    for axis, bit in (("ws", 1), ("ws", 2), ("run", 1), ("run", 2)):
        sums = sums + lax.ppermute(sums, axis, [(i, i ^ bit) for i in range(4)])
    return sums


def shards(
    inputs,
    cotangent,
    block_ids,
    first_gain,
    first_shift,
    weight_in,
    second_gain,
    second_shift,
    weight_conv,
    third_gain,
    third_shift,
    weight_out,
    output_bias,
):
    x = inputs.transpose(0, 2, 1)
    g = cotangent.transpose(0, 2, 1)
    count, shard, core = lax.axis_size("ws"), lax.axis_index("ws"), lax.axis_index("core")
    easy = square()
    place = jnp.stack([shard, core])
    owned_vectors = (first_gain, first_shift, output_bias, second_gain, second_shift, third_gain, third_shift)
    sizes = tuple(own.size for own in owned_vectors)
    flat = jnp.concatenate(owned_vectors)
    if easy:
        parts = jnp.stack([flat, *[from_ws(flat, bit) for bit in (1, 2, 3)]]).astype(F32)
        vectors = spread(place, parts, sizes)
    else:
        parts = lax.all_gather(flat, "ws", axis=0).astype(F32)
        vectors = spread(jnp.zeros_like(place), parts, sizes)
    in_pieces = fetched(weight_in) if easy else None
    own_conv = conv_weights(weight_conv) if easy else None
    length = block_ids.shape[1]
    ids_before, ids_after = neighbours(block_ids[:, :BORDER], block_ids[:, -BORDER:])
    ids = jnp.concatenate([ids_before, block_ids, ids_after], axis=1)
    same = lambda by: ids[:, BORDER + by : BORDER + by + length] == block_ids
    steps = [DILATION_STEP * (i + 1) for i in range(KERNEL_TAPS // 2)]

    def masks(sign):
        both = jnp.stack([same(sign * by) for by in steps], axis=1)
        return jnp.broadcast_to(both[..., None], (*both.shape, LANES)).astype(BF16)

    mask, mask_back = masks(1), masks(-1)
    act1, stats1 = open_block(x, vectors)
    if easy:
        in_pieces = after(in_pieces, act1)
        out_pieces = fetched(after(weight_out, *in_pieces))
    else:
        out_pieces = None
    w_in, w_in_t = whole_weight(place, weight_in, in_pieces)
    act2, rows2, normed2, stats2 = enter(act1, w_in_t, vectors)
    halo2 = neighbours(rows2[:, :BORDER], rows2[:, -BORDER:])
    if easy:
        out_pieces = after(out_pieces, act2)
    w_out, w_out_t = whole_weight(place, weight_out, out_pieces)
    grad_act3, bias_sums = project(w_out, g)
    if easy:
        w_conv, w_conv_t = join(after(own_conv, grad_act3), weight_conv.shape[1])
    else:
        w_conv = lax.all_gather(weight_conv, "ws", axis=1, tiled=True)
        w_conv_t = flip(w_conv)
    halo2 = after(halo2, grad_act3)
    act3, rows3, sums3 = conv_block(rows2, *halo2, mask, w_conv_t, vectors, grad_act3)
    halo = neighbours(rows3[:, :BORDER], rows3[:, -BORDER:])
    bit = shard & 1
    give, keep = jnp.stack([1 - core, bit]), jnp.stack([core, bit])
    if not easy:
        give, keep = jnp.zeros_like(give), jnp.ones_like(keep)
    seqs = x.shape[0]
    back = lambda rows, seq, number, into: conv_back(
        rows, *halo, mask_back, w_conv, vectors, normed2, stats2, seq, number, into
    )
    close = lambda low, seq, number, into: leave(low, w_in, x, g, vectors, stats1, seq, number, into)
    if not easy:
        taps = (act2, rows3, *halo, mask_back)
        out_grad = plain(outer(give, act3, g), outer(keep, act3, g), 0)
        (low,), (high,) = outer_taps(give, *taps, 0, (5,)), outer_taps(keep, *taps, 0, (5,))
        conv_grad = plain(low, high, 1)
        low2, sums2 = back(rows3, 0, seqs, None)
        in_grad = plain(outer(give, act1, low2), outer(keep, act1, low2), 0)
        input_grad, sums1 = close(low2, 0, seqs, None)
        block_output = finish(w_out_t, act3, x, vectors, 0, seqs)
    else:
        out_send = outer(give, act3, g)
        halo = after(halo, out_send)
        taps = (act2, rows3, *halo, mask_back)
        send_a, send_b = outer_taps(give, *taps, 0, (3, 2))
        got_out = swapped(out_send)
        got_a, got_b = swapped(send_a), swapped(send_b)
        out = Share(*outer(keep, act3, g, after(got_out, send_a)))
        out.spread()
        got_a, got_b = after((got_a, got_b), out.sum)
        tap_a = Share(*outer_taps(keep, *taps, 0, (3,), got_a))
        tap_a.spread()
        tap_b = Share(*outer_taps(keep, *after(taps, tap_a.sum), 3, (2,), got_b))
        tap_b.spread()
        out.land(tap_b.sum)
        out.inward()
        low2, sums2a = back(after(rows3, tap_b.sum, out.sum), 0, 1, None)
        out.land(sums2a)
        out.middle()
        tap_a.land(sums2a)
        tap_a.inward()
        low2, sums2b = back(after(rows3, sums2a, out.sum, tap_a.sum), 1, seqs - 1, low2)
        sums2 = sums2a + sums2b
        tap_b.land(sums2b)
        tap_b.inward()
        in_send = outer(give, *after((act1, low2), tap_b.sum))
        got_in = swapped(in_send)
        out.land(in_send)
        out.outward()
        tap_a.land(in_send)
        tap_a.middle()
        block_output = finish(*after((w_out_t, act3), in_send, out.sum, tap_a.sum), x, vectors, 0, 1)
        inner = Share(*outer(keep, act1, low2, after(got_in, block_output)))
        inner.spread()
        tap_b.land(inner.sum)
        tap_b.middle()
        out.land(inner.sum)
        input_grad, sums1a = close(after(low2, inner.sum, tap_b.sum), 0, 1, None)
        inner.land(sums1a)
        inner.inward()
        tap_a.land(sums1a)
        tap_a.outward()
        input_grad, sums1b = close(after(low2, inner.sum, tap_a.sum), 1, seqs - 1, input_grad)
        sums1 = sums1a + sums1b
        inner.land(sums1b)
        inner.middle()
        tap_b.land(sums1b)
        tap_b.outward()
        tap_a.land(sums1b)
        block_output = finish(
            *after((w_out_t, act3), sums1b, inner.sum, tap_b.sum), x, vectors, 1, seqs - 1, block_output
        )
        inner.land(block_output)
        inner.outward()
        tap_b.land(block_output)
        out_grad = out.both()
        conv_grad = jnp.concatenate([tap_a.both(), tap_b.both()], axis=0)
        inner.land()
        in_grad = inner.both()

    totals = [s.sum(axis=-1) for s in (sums1[0], sums1[1], bias_sums, sums2[0], sums2[1], sums3[0], sums3[1])]
    small = small_sums(jnp.concatenate([t.reshape(count, -1) for t in totals], axis=1))
    small = lax.dynamic_index_in_dim(small, shard, axis=0, keepdims=False)
    at, vector_grads = 0, []
    for size in sizes:
        vector_grads.append(small[at : at + size])
        at += size
    gain1, shift1, bias, gain2, shift2, gain3, shift3 = vector_grads
    return (
        block_output.transpose(0, 2, 1),
        input_grad.transpose(0, 2, 1),
        gain1,
        shift1,
        in_grad,
        gain2,
        shift2,
        conv_grad,
        gain3,
        shift3,
        out_grad,
        bias,
    )


def solution(mesh):
    count, runs = mesh.devices.shape
    split = jax.sharding.Mesh(mesh.devices.reshape(count, runs // 2, 2), ("ws", "run", "core"))
    tokens = P("ws", ("run", "core"), None)
    rows = P("ws", None)
    taps = P(None, "ws", None)
    placed = (tokens, tokens, P("ws", ("run", "core")), P("ws"), P("ws"), rows, P("ws"), P("ws"), taps)
    placed += (P("ws"), P("ws"), rows, P("ws"))
    given = (tokens, tokens, P("ws"), P("ws"), rows, P("ws"), P("ws"), taps, P("ws"), P("ws"), rows, P("ws"))
    return jax.shard_map(shards, mesh=split, in_specs=placed, out_specs=given, check_vma=False)
```

```python
import functools
import jax
import jax.numpy as jnp
from jax import lax
from jax.experimental import pallas as pl
from jax.experimental.pallas import tpu as pltpu
from jax.sharding import PartitionSpec as P

KERNEL_TAPS = 5
DILATION_STEP = 16
EPS = 1e-05
LANES = 128
BORDER = KERNEL_TAPS // 2 * DILATION_STEP
F32 = jnp.float32
BF16 = jnp.bfloat16
VMEM_BYTES = 60 * 2**20

NN = (((1,), (0,)), ((), ()))
NT = (((1,), (1,)), ((), ()))


def params(steps=0):
    return pltpu.CompilerParams(
        dimension_semantics=("arbitrary",) * steps or None, vmem_limit_bytes=VMEM_BYTES
    )


def cost(flops, bytes_accessed):
    return pl.CostEstimate(flops=flops // 16, bytes_accessed=bytes_accessed // 16, transcendentals=0)


def shape(dims, dtype=BF16):
    return jax.ShapeDtypeStruct(dims, dtype)


def dot(left, right, dims=NN):
    return lax.dot_general(left, right, dims, preferred_element_type=F32)


def wide(column, lanes):
    return jnp.concatenate([column] * (lanes // LANES), axis=1)


def folded(values):
    total = values[:, :LANES]
    for at in range(LANES, values.shape[1], LANES):
        total = total + values[:, at : at + LANES]
    return total


def logistic(x):
    return 0.5 * jnp.tanh(0.5 * x) + 0.5


def vector(rows, block):
    return pl.BlockSpec((rows, LANES), lambda *_: (block, 0))


def here(rows, lanes, seq=0):
    return pl.BlockSpec((1, rows, lanes), lambda s, t: (s + seq, 0, t))


def held(dims):
    return pl.BlockSpec(dims, lambda *_: (0,) * len(dims))


def each(count, body, init, unroll=5):
    return lax.fori_loop(0, count, body, init, unroll=unroll)


def rows_at(index, size):
    return pl.ds(pl.multiple_of(index * size, size), size)


def row_stats(load, channels, chunk, lanes):
    steps = channels // chunk
    zero = jnp.zeros((chunk, lanes), F32)
    total = each(steps, lambda i, t: t + load(i), zero)
    mean = jnp.sum(total, axis=0, keepdims=True) * (1.0 / channels)

    def square(i, t):
        centred = load(i) - mean
        return t + centred * centred

    squares = each(steps, square, zero)
    spread = jnp.sum(squares, axis=0, keepdims=True) * (1.0 / channels)
    return mean, lax.rsqrt(spread + EPS)


def back_first(u, normed, gain, shift):
    pre = normed * gain + shift
    sigma = logistic(pre)
    p = u * (sigma * (1.0 + pre * (1.0 - sigma)))
    return pre, sigma, p, p * gain


def first_step():
    return (pl.program_id(0) == 0) & (pl.program_id(1) == 0)


def last_step():
    return (pl.program_id(0) == pl.num_programs(0) - 1) & (
        pl.program_id(1) == pl.num_programs(1) - 1
    )


def cleared(sums):
    @pl.when(first_step())
    def _():
        sums[...] = jnp.zeros_like(sums)


def handed(sums, out):
    @pl.when(last_step())
    def _():
        out[...] = sums[...]


def open_kernel(x, gain, shift, act1, stats, *, chunk):
    lanes, width = x.shape[2], x.shape[1]
    load = lambda i: x[0, rows_at(i, chunk), :].astype(F32)
    mean, scale = row_stats(load, width, chunk, lanes)

    def activate(i, carry):
        at = rows_at(i, chunk)
        normed = (load(i) - mean) * scale
        pre = normed * wide(gain[at, :], lanes) + wide(shift[at, :], lanes)
        act1[0, at, :] = (pre * logistic(pre)).astype(BF16)
        return carry

    each(width // chunk, activate, 0)
    stats[0] = jnp.concatenate([mean, scale, jnp.zeros((6, lanes), F32)], axis=0)


def open_block(x, vectors, lanes=512, chunk=32):
    seqs, width, length = x.shape
    return pl.pallas_call(
        functools.partial(open_kernel, chunk=chunk),
        grid=(seqs, length // lanes),
        in_specs=[here(width, lanes), vector(width, 0), vector(width, 1)],
        out_specs=[here(width, lanes), here(8, lanes)],
        out_shape=[shape(x.shape), shape((seqs, 8, length), F32)],
        compiler_params=params(2),
        cost_estimate=cost(40 * x.size, 4 * x.size),
        name="open_block",
    )(x, vectors, vectors)


def enter_kernel(act1, w_in, gain, shift, act2, turned, normed2, stats, proj, *, chunk):
    lanes, inner = act1.shape[2], act2.shape[1]
    proj[...] = dot(w_in[...], act1[0])
    load = lambda i: proj[rows_at(i, chunk), :]
    mean, scale = row_stats(load, inner, chunk, lanes)

    def activate(i, carry):
        at = rows_at(i, chunk)
        normed = (load(i) - mean) * scale
        normed2[0, at, :] = normed
        pre = normed * wide(gain[at, :], lanes) + wide(shift[at, :], lanes)
        act2[0, at, :] = (pre * logistic(pre)).astype(BF16)
        return carry

    each(inner // chunk, activate, 0)
    turned[0] = act2[0].T
    stats[0] = jnp.concatenate([scale, jnp.zeros((7, lanes), F32)], axis=0)


def enter(act1, w_in_t, vectors, lanes=512, chunk=32):
    seqs, width, length = act1.shape
    inner = w_in_t.shape[0]
    return pl.pallas_call(
        functools.partial(enter_kernel, chunk=chunk),
        grid=(seqs, length // lanes),
        in_specs=[here(width, lanes), held((inner, width)), vector(inner, 6), vector(inner, 7)],
        out_specs=[
            here(inner, lanes),
            pl.BlockSpec((1, lanes, inner), lambda s, t: (s, t, 0)),
            here(inner, lanes),
            here(8, lanes),
        ],
        out_shape=[
            shape((seqs, inner, length)),
            shape((seqs, length, inner)),
            shape((seqs, inner, length), F32),
            shape((seqs, 8, length), F32),
        ],
        scratch_shapes=[pltpu.VMEM((inner, lanes), F32)],
        compiler_params=params(2),
        cost_estimate=cost(2 * act1.size * inner, seqs * length * (2 * width + 8 * inner)),
        name="enter",
    )(act1, w_in_t, vectors, vectors)


def project_kernel(weight, columns, out, grads, sums, *, chunk):
    cleared(sums)
    out[0] = dot(weight[...], columns[0])

    def body(i, carry):
        at = rows_at(i, chunk)
        sums[at, :] += folded(columns[0, at, :].astype(F32))
        return carry

    each(columns.shape[1] // chunk, body, 0)
    handed(sums, grads)


def project(weight, columns, lanes=512, chunk=32):
    seqs, depth, length = columns.shape
    rows = weight.shape[0]
    return pl.pallas_call(
        functools.partial(project_kernel, chunk=chunk),
        grid=(seqs, length // lanes),
        in_specs=[held((rows, depth)), here(depth, lanes)],
        out_specs=[here(rows, lanes), held((depth, LANES))],
        out_shape=[shape((seqs, rows, length), F32), shape((depth, LANES), F32)],
        scratch_shapes=[pltpu.VMEM((depth, LANES), F32)],
        compiler_params=params(2),
        cost_estimate=cost(2 * columns.size * rows, seqs * length * (2 * depth + 4 * rows)),
        name="project",
    )(weight, columns)


def extend(rows, before, after, mask, whole, masked, seq, sign):
    length = rows.shape[1]
    whole[:BORDER, :] = before[seq]
    whole[BORDER : BORDER + length, :] = rows[seq]
    whole[BORDER + length :, :] = after[seq]
    inner = rows.shape[2]
    chunk = 128
    for later in range(KERNEL_TAPS // 2):
        by = sign * (later + 1) * DILATION_STEP

        def body(i, carry, later=later, by=by):
            kept = mask[seq, later, rows_at(i, chunk), :]
            kept = jnp.concatenate([kept] * -(-inner // LANES), axis=1)[:, :inner]
            start = pl.multiple_of(i * chunk + BORDER + by, DILATION_STEP)
            masked[later, rows_at(i, chunk), :] = whole[pl.ds(start, chunk), :] * kept
            return carry

        each(length // chunk, body, 0, 1)


def tap_rows(whole, masked, tap, sign, start, count):
    by = (tap - KERNEL_TAPS // 2) * DILATION_STEP
    if by > 0:
        return masked[tap - KERNEL_TAPS // 2 - 1, pl.ds(start, count), :]
    return whole[pl.ds(start + (BORDER + sign * by), count), :]


def conv_kernel(rows, before, after, mask, w_conv, gain, shift, upstream, act3, turned, grads, whole, masked, conv, scaled, low, sums, *, chunk):
    tile = pl.program_id(1)
    lanes, inner = act3.shape[2], act3.shape[1]
    cleared(sums)

    @pl.when(tile == 0)
    def _():
        extend(rows, before, after, mask, whole, masked, 0, 1)

    start = pl.multiple_of(tile * lanes, lanes)
    total = None
    for tap in range(KERNEL_TAPS):
        part = dot(w_conv[tap], tap_rows(whole, masked, tap, 1, start, lanes), NT)
        total = part if total is None else total + part
    conv[...] = total
    load = lambda i: conv[rows_at(i, chunk), :]
    mean, scale = row_stats(load, inner, chunk, lanes)

    def first(i, carry):
        at = rows_at(i, chunk)
        normed = (load(i) - mean) * scale
        gains = wide(gain[at, :], lanes)
        pre, sigma, p, q = back_first(upstream[0, at, :], normed, gains, wide(shift[at, :], lanes))
        act3[0, at, :] = (pre * sigma).astype(BF16)
        conv[at, :] = normed
        scaled[at, :] = q
        sums[0, at, :] += folded(p * normed)
        sums[1, at, :] += folded(p)
        return carry[0] + q, carry[1] + q * normed

    zero = jnp.zeros((chunk, lanes), F32)
    one, two = each(inner // chunk, first, (zero, zero))
    one = jnp.sum(one, axis=0, keepdims=True) * (1.0 / inner)
    two = jnp.sum(two, axis=0, keepdims=True) * (1.0 / inner)

    def second(i, carry):
        at = rows_at(i, chunk)
        low[at, :] = (scale * (scaled[at, :] - one - conv[at, :] * two)).astype(BF16)
        return carry

    each(inner // chunk, second, 0)
    turned[0] = low[...].T
    handed(sums, grads)


def conv_block(rows, before, after, mask, w_conv_t, vectors, upstream, lanes=512, chunk=16):
    seqs, length, inner = rows.shape
    seq = lambda *dims: pl.BlockSpec((1, *dims), lambda s, t: (s,) + (0,) * len(dims))
    return pl.pallas_call(
        functools.partial(conv_kernel, chunk=chunk),
        grid=(seqs, length // lanes),
        in_specs=[
            seq(length, inner),
            seq(BORDER, inner),
            seq(BORDER, inner),
            seq(2, length, LANES),
            held(w_conv_t.shape),
            vector(inner, 8),
            vector(inner, 9),
            here(inner, lanes),
        ],
        out_specs=[
            here(inner, lanes),
            pl.BlockSpec((1, lanes, inner), lambda s, t: (s, t, 0)),
            held((2, inner, LANES)),
        ],
        out_shape=[
            shape((seqs, inner, length)),
            shape((seqs, length, inner)),
            shape((2, inner, LANES), F32),
        ],
        scratch_shapes=[
            pltpu.VMEM((length + 2 * BORDER, inner), BF16),
            pltpu.VMEM((KERNEL_TAPS // 2, length, inner), BF16),
            pltpu.VMEM((inner, lanes), F32),
            pltpu.VMEM((inner, lanes), F32),
            pltpu.VMEM((inner, lanes), BF16),
            pltpu.VMEM((2, inner, LANES), F32),
        ],
        compiler_params=params(2),
        cost_estimate=cost(2 * rows.size * w_conv_t.size // inner, 12 * rows.size),
        name="conv_block",
    )(rows, before, after, mask, w_conv_t, vectors, vectors, upstream)


def conv_back_kernel(rows, before, after, mask, w_conv, gain, shift, normed2, stats, *rest, chunk):
    out, grads, whole, masked, grad, scaled, sums = rest[-7:]
    tile = pl.program_id(1)
    lanes, inner = out.shape[2], out.shape[1]
    cleared(sums)

    @pl.when(tile == 0)
    def _():
        extend(rows, before, after, mask, whole, masked, 0, -1)

    start = pl.multiple_of(tile * lanes, lanes)
    total = None
    for tap in range(KERNEL_TAPS):
        part = dot(w_conv[tap], tap_rows(whole, masked, tap, -1, start, lanes), NT)
        total = part if total is None else total + part
    grad[...] = total
    scale = stats[0, 0:1, :]

    def first(i, carry):
        at = rows_at(i, chunk)
        normed = normed2[0, at, :]
        _, _, p, q = back_first(
            grad[at, :], normed, wide(gain[at, :], lanes), wide(shift[at, :], lanes)
        )
        scaled[at, :] = q
        sums[0, at, :] += folded(p * normed)
        sums[1, at, :] += folded(p)
        return carry[0] + q, carry[1] + q * normed

    zero = jnp.zeros((chunk, lanes), F32)
    one, two = each(inner // chunk, first, (zero, zero))
    one = jnp.sum(one, axis=0, keepdims=True) * (1.0 / inner)
    two = jnp.sum(two, axis=0, keepdims=True) * (1.0 / inner)

    def second(i, carry):
        at = rows_at(i, chunk)
        out[0, at, :] = (scale * (scaled[at, :] - one - normed2[0, at, :] * two)).astype(BF16)
        return carry

    each(inner // chunk, second, 0)
    handed(sums, grads)


def conv_back(rows, before, after, mask, w_conv, vectors, normed2, stats, first, count, into=None, lanes=512, chunk=16):
    seqs, length, inner = rows.shape
    seq = lambda *dims: pl.BlockSpec((1, *dims), lambda s, t: (s + first,) + (0,) * len(dims))
    more = () if into is None else (into,)
    return pl.pallas_call(
        functools.partial(conv_back_kernel, chunk=chunk),
        grid=(count, length // lanes),
        in_specs=[
            seq(length, inner),
            seq(BORDER, inner),
            seq(BORDER, inner),
            seq(2, length, LANES),
            held(w_conv.shape),
            vector(inner, 6),
            vector(inner, 7),
            here(inner, lanes, first),
            here(8, lanes, first),
        ]
        + [pl.BlockSpec(memory_space=pl.ANY)] * len(more),
        out_specs=[here(inner, lanes, first), held((2, inner, LANES))],
        input_output_aliases={9: 0} if more else {},
        out_shape=[shape((seqs, inner, length)), shape((2, inner, LANES), F32)],
        scratch_shapes=[
            pltpu.VMEM((length + 2 * BORDER, inner), BF16),
            pltpu.VMEM((KERNEL_TAPS // 2, length, inner), BF16),
            pltpu.VMEM((inner, lanes), F32),
            pltpu.VMEM((inner, lanes), F32),
            pltpu.VMEM((2, inner, LANES), F32),
        ],
        compiler_params=params(2),
        cost_estimate=cost(2 * rows.size * w_conv.size * count // (seqs * inner), 10 * rows.size * count // seqs),
        name="conv_back",
    )(rows, before, after, mask, w_conv, vectors, vectors, normed2, stats, *more)


def leave_kernel(low, w_in, x, g, gain, shift, stats, *rest, chunk):
    out, grads, grad, sums = rest[-4:]
    lanes, width = out.shape[2], out.shape[1]
    cleared(sums)
    grad[...] = dot(w_in[...], low[0])
    mean = stats[0, 0:1, :]
    scale = stats[0, 1:2, :]
    norm = lambda at: (x[0, at, :].astype(F32) - mean) * scale

    def first(i, carry):
        at = rows_at(i, chunk)
        normed = norm(at)
        _, _, p, q = back_first(
            grad[at, :], normed, wide(gain[at, :], lanes), wide(shift[at, :], lanes)
        )
        grad[at, :] = q
        sums[0, at, :] += folded(p * normed)
        sums[1, at, :] += folded(p)
        return carry[0] + q, carry[1] + q * normed

    zero = jnp.zeros((chunk, lanes), F32)
    one, two = each(width // chunk, first, (zero, zero))
    one = jnp.sum(one, axis=0, keepdims=True) * (1.0 / width)
    two = jnp.sum(two, axis=0, keepdims=True) * (1.0 / width)

    def second(i, carry):
        at = rows_at(i, chunk)
        branch = scale * (grad[at, :] - one - norm(at) * two)
        out[0, at, :] = (g[0, at, :].astype(F32) + branch).astype(BF16)
        return carry

    each(width // chunk, second, 0)
    handed(sums, grads)


def leave(low, w_in, x, g, vectors, stats, first, count, into=None, lanes=512, chunk=16):
    seqs, inner, length = low.shape
    width = x.shape[1]
    more = () if into is None else (into,)
    return pl.pallas_call(
        functools.partial(leave_kernel, chunk=chunk),
        grid=(count, length // lanes),
        in_specs=[
            here(inner, lanes, first),
            held((width, inner)),
            here(width, lanes, first),
            here(width, lanes, first),
            vector(width, 0),
            vector(width, 1),
            here(8, lanes, first),
        ]
        + [pl.BlockSpec(memory_space=pl.ANY)] * len(more),
        input_output_aliases={7: 0} if more else {},
        out_specs=[here(width, lanes, first), held((2, width, LANES))],
        out_shape=[shape(x.shape), shape((2, width, LANES), F32)],
        scratch_shapes=[pltpu.VMEM((width, lanes), F32), pltpu.VMEM((2, width, LANES), F32)],
        compiler_params=params(2),
        cost_estimate=cost(2 * low.size * width * count // seqs, (2 * low.size + 6 * x.size) * count // seqs),
        name="leave",
    )(low, w_in, x, g, vectors, vectors, stats, *more)


def finish_kernel(w_out, act3, x, bias, *rest, chunk):
    out, proj = rest[-2:]
    lanes, width = out.shape[2], out.shape[1]
    proj[...] = dot(w_out[...], act3[0])

    def body(i, carry):
        at = rows_at(i, chunk)
        out[0, at, :] = (x[0, at, :].astype(F32) + proj[at, :] + wide(bias[at, :], lanes)).astype(BF16)
        return carry

    each(width // chunk, body, 0)


def finish(w_out_t, act3, x, vectors, first, count, into=None, lanes=512, chunk=32):
    more = () if into is None else (into,)
    seqs, inner, length = act3.shape
    width = x.shape[1]
    return pl.pallas_call(
        functools.partial(finish_kernel, chunk=chunk),
        grid=(count, length // lanes),
        in_specs=[held((width, inner)), here(inner, lanes, first), here(width, lanes, first), vector(width, 2)]
        + [pl.BlockSpec(memory_space=pl.ANY)] * len(more),
        input_output_aliases={4: 0} if more else {},
        out_specs=here(width, lanes, first),
        out_shape=shape(x.shape),
        scratch_shapes=[pltpu.VMEM((width, lanes), F32)],
        compiler_params=params(2),
        cost_estimate=cost(0, 0),
        name="finish",
    )(w_out_t, act3, x, vectors, *more)


def grads_kernel(at, *refs, pair, taps, keep, units):
    refs = list(refs)
    take = lambda n: [refs.pop(0) for _ in range(n)]
    sources = []
    left = right = act2 = rows3 = before = after = mask = got = None
    if pair:
        left, right = take(2)
    if taps:
        act2, rows3, before, after, mask = take(5)
    if keep:
        (got,) = take(1)
    outs = take(2 if keep else len(units))
    sems = refs.pop(-1)
    loads = []

    def load(source, target):
        copy = pltpu.make_async_copy(source, target, sems.at[len(loads)])
        copy.start()
        loads.append(copy)
        return copy

    if pair:
        left_here, right_here = take(2)
        half = left_here.shape[1]
        columns = right_here.shape[1] // pair
        first = [load(left.at[:, pl.ds(pl.multiple_of(at[0] * half, half), half), :], left_here)]
        blocks = []
        for i in range(pair):
            span = pl.ds(i * columns, columns)
            blocks.append(load(right.at[:, span, :], right_here.at[:, span, :]))
    if taps:
        act2_here, whole, mask_here, masked = take(4)
        seqs, length = rows3.shape[0], rows3.shape[1]
        half2 = act2_here.shape[1]
        ready = [load(act2.at[:, pl.ds(pl.multiple_of(at[0] * half2, half2), half2), :], act2_here)]
        for seq in range(seqs):
            ready.append(load(rows3.at[seq], whole.at[seq, pl.ds(BORDER, length), :]))
        ready.append(load(before, whole.at[:, pl.ds(0, BORDER), :]))
        ready.append(load(after, whole.at[:, pl.ds(BORDER + length, BORDER), :]))
        ready.append(load(mask, mask_here))
    if keep:
        got_here, total = take(2)
        got_load = load(got, got_here)

    def give(step, value):
        if not keep:
            place = step
            for out, size in zip(outs, units):
                if place < size:
                    out[place] = value.astype(BF16)
                    return
                place -= size
        if step == 0:
            got_load.wait()
        total[...] = value + got_here[step].astype(F32)
        rows = outs[0].shape[1]
        for place, out in enumerate(outs):
            start = pl.multiple_of((at[1] ^ place) * rows, 8)
            out[step] = total[pl.ds(start, rows), :].astype(BF16)

    for i in range(pair):
        if i == 0:
            first[0].wait()
        blocks[i].wait()
        value = None
        for seq in range(left_here.shape[0]):
            part = dot(left_here[seq], right_here[seq, i * columns : (i + 1) * columns, :], NT)
            value = part if value is None else value + part
        give(i, value)
    for step, tap in enumerate(taps):
        by = (tap - KERNEL_TAPS // 2) * DILATION_STEP
        if step == 0:
            for copy in ready:
                copy.wait()
        value = None
        for seq in range(seqs):
            if by > 0:
                mask_rows(whole.at[seq], mask_here, masked, seq, by)
                rows = masked[...]
            else:
                rows = whole[seq, BORDER - by : BORDER - by + length, :]
            part = dot(act2_here[seq], rows)
            value = part if value is None else value + part
        give(pair + step, value)


def tap_grads_kernel(left, rows3, before, after, mask, out, left_here, whole, mask_here, masked, total, done, sems):
    seqs, length = rows3.shape[0], rows3.shape[1]
    count, size = out.shape[0], left.shape[1] // out.shape[0]

    def copy(place, source, target):
        moving = pltpu.make_async_copy(source, target, sems.at[place])
        moving.start()
        return moving

    loads = [copy(0, left, left_here), copy(1, mask, mask_here)]
    loads.append(copy(2, before, whole.at[:, pl.ds(0, BORDER), :]))
    loads.append(copy(3, after, whole.at[:, pl.ds(BORDER + length, BORDER), :]))
    for seq in range(seqs):
        loads.append(copy(4 + seq, rows3.at[seq], whole.at[seq, pl.ds(BORDER, length), :]))
    for load in loads:
        load.wait()
    stores = []
    for tap in range(KERNEL_TAPS):
        by = (tap - KERNEL_TAPS // 2) * DILATION_STEP
        value = None
        for seq in range(seqs):
            if by > 0:
                mask_rows(whole.at[seq], mask_here, masked, seq, by)
                rows = masked[...]
            else:
                rows = whole[seq, BORDER - by : BORDER - by + length, :]
            part = dot(left_here[seq], rows)
            value = part if value is None else value + part
        total[tap % 2] = value
        last = tap == KERNEL_TAPS - 1
        if tap % 2 == 0 and not last:
            continue
        start = tap // 2 * 2 * size
        height = out.shape[1] - start if last else 2 * size
        fill = jnp.zeros((height - size, total.shape[2]), F32)
        for shard in range(count):
            span = slice(shard * size, (shard + 1) * size)
            below = fill if last else total[1, span, :]
            done[tap // 2, shard, :height, :] = jnp.concatenate([total[0, span, :], below], axis=0).astype(BF16)
            place = 4 + seqs + tap // 2 * count + shard
            stores.append(copy(place, done.at[tap // 2, shard, pl.ds(0, height), :], out.at[shard, pl.ds(start, height), :]))
    for store in stores:
        store.wait()


def tap_grads(count, padded, left, rows3, before, after, mask):
    seqs, length, inner = rows3.shape
    steps = -(-KERNEL_TAPS // 2)
    operands = (left, rows3, before, after, mask)
    return pl.pallas_call(
        tap_grads_kernel,
        in_specs=[pl.BlockSpec(memory_space=pl.ANY)] * len(operands),
        out_specs=pl.BlockSpec(memory_space=pl.ANY),
        out_shape=shape((count, padded, inner)),
        scratch_shapes=[
            pltpu.VMEM(left.shape, BF16),
            pltpu.VMEM((seqs, length + 2 * BORDER, inner), BF16),
            pltpu.VMEM(mask.shape, BF16),
            pltpu.VMEM((length, inner), BF16),
            pltpu.VMEM((2, inner, inner), F32),
            pltpu.VMEM((steps, count, 2 * inner // count, inner), BF16),
            pltpu.SemaphoreType.DMA((4 + seqs + steps * count,)),
        ],
        compiler_params=params(),
        cost_estimate=cost(2 * KERNEL_TAPS * left.size * inner, 4 * left.size + 10 * inner * inner),
        name="tap_grads",
    )(*operands)


def mask_rows(whole, mask, masked, seq, by):
    length, inner = masked.shape
    chunk = 128

    def body(i, carry):
        kept = mask[seq, by // DILATION_STEP - 1, rows_at(i, chunk), :]
        kept = jnp.concatenate([kept] * -(-inner // LANES), axis=1)[:, :inner]
        start = pl.multiple_of(i * chunk + BORDER - by, DILATION_STEP)
        masked[rows_at(i, chunk), :] = whole[pl.ds(start, chunk), :] * kept
        return carry

    each(length // chunk, body, 0, 1)


def grads(at, columns, pair=None, taps=(), conv=(), got=None, units=None):
    operands, scratch = [], []
    count, flops, copies = 0, 0, 0
    if pair is not None:
        left, right = pair
        half = left.shape[1] // 2
        count = right.shape[1] // columns
        operands += [left, right]
        scratch += [pltpu.VMEM((left.shape[0], half, left.shape[2]), BF16), pltpu.VMEM(right.shape, BF16)]
        copies += 1 + count
        flops += left.size * right.shape[1]
    if taps:
        act2, rows3, _, _, mask = conv
        seqs, length, inner = rows3.shape
        half = inner // 2
        operands += conv
        scratch += [
            pltpu.VMEM((seqs, half, length), BF16),
            pltpu.VMEM((seqs, length + 2 * BORDER, inner), BF16),
            pltpu.VMEM(mask.shape, BF16),
            pltpu.VMEM((length, inner), BF16),
        ]
        copies += 4 + seqs
        flops += act2.size * inner * len(taps)
    total = count + len(taps)
    if got is None:
        units = units or (total,)
        dims = [(size, half, columns) for size in units]
    else:
        operands.append(got)
        scratch += [pltpu.VMEM(got.shape, BF16), pltpu.VMEM((half, columns), F32)]
        copies += 1
        dims = [(total, half // 2, columns)] * 2
    scratch.append(pltpu.SemaphoreType.DMA((copies,)))
    return pl.pallas_call(
        functools.partial(grads_kernel, pair=count, taps=taps, keep=got is not None, units=units),
        grid_spec=pltpu.PrefetchScalarGridSpec(
            num_scalar_prefetch=1,
            grid=(1,),
            in_specs=[pl.BlockSpec(memory_space=pl.ANY)] * len(operands),
            out_specs=[held(d) for d in dims],
            scratch_shapes=scratch,
        ),
        out_shape=[shape(d) for d in dims],
        compiler_params=params(1),
        cost_estimate=cost(flops, 2 * sum(o.size for o in operands)),
        name="grads",
    )(at, *operands)


def flip_kernel(w, out):
    for tap in range(w.shape[0]):
        out[tap] = w[tap].T


def flip(w):
    taps, rows, columns = w.shape
    return pl.pallas_call(
        flip_kernel,
        out_shape=shape((taps, columns, rows)),
        compiler_params=params(),
        cost_estimate=cost(0, 4 * w.size),
        name="flip",
    )(w)


def assemble_kernel(at, own, mine, other, natural, turned, whole, *, gap):
    rows, half = own.shape[0], mine.shape[1]
    whole[pl.ds(pl.multiple_of(at[0] * rows, 8), rows), :] = own[...].astype(F32)
    for step in range(mine.shape[0]):
        for pieces, core in ((mine, at[1]), (other, 1 - at[1])):
            start = (at[0] ^ (step + 1)) * rows + core * (rows - half)
            whole[pl.ds(pl.multiple_of(start, 8), half), :] = pieces[step].astype(F32)
    natural[...] = whole[...].astype(BF16)
    turned[...] = natural[...].T


def assemble(at, own, mine, other):
    rows, columns = own.shape
    full = rows * (mine.shape[0] + 1)
    dims = [(full, columns), (columns, full)]
    return pl.pallas_call(
        functools.partial(assemble_kernel, gap=0),
        grid_spec=pltpu.PrefetchScalarGridSpec(
            num_scalar_prefetch=1,
            grid=(1,),
            in_specs=[held(own.shape), held(mine.shape), held(other.shape)],
            out_specs=[held(d) for d in dims],
            scratch_shapes=[pltpu.VMEM((full, columns), F32)],
        ),
        out_shape=[shape(d) for d in dims],
        compiler_params=params(1),
        cost_estimate=cost(0, 6 * full * columns),
        name="assemble",
    )(at, own, mine, other)


def join_kernel(pieces, natural, turned, whole, *, rows):
    count, half = pieces.shape[0], pieces.shape[3]
    for shard in range(count):
        for core in range(2):
            start = shard * rows + core * (rows - half)
            whole[start : start + half, :] = pieces[shard, core, 0].astype(F32)
    natural[0] = whole[...].astype(BF16)
    turned[0] = natural[0].T


def join(pieces, rows):
    count, cores, taps, half, columns = pieces.shape
    full = count * rows
    dims = [(taps, full, columns), (taps, columns, full)]
    return pl.pallas_call(
        functools.partial(join_kernel, rows=rows),
        grid=(taps,),
        in_specs=[pl.BlockSpec((count, cores, 1, half, columns), lambda t: (0, 0, t, 0, 0))],
        out_specs=[pl.BlockSpec((1, *d[1:]), lambda t: (t, 0, 0)) for d in dims],
        out_shape=[shape(d) for d in dims],
        scratch_shapes=[pltpu.VMEM((full, columns), F32)],
        compiler_params=params(1),
        cost_estimate=cost(0, 6 * taps * full * columns),
        name="join",
    )(pieces)


def spread_kernel(at, parts, out, rows, *, sizes):
    count = parts.shape[0]
    for i in range(count):
        rows[pl.ds(at[0] ^ i, 1), :] = parts[i : i + 1, :]
    start, base = 0, 0
    for size in sizes:
        for shard in range(count):
            row = rows[shard : shard + 1, start : start + size]
            out[base : base + size, :] = jnp.broadcast_to(row, (LANES, size)).T
            base += size
        start += size


def spread(at, parts, sizes):
    total = parts.size
    return pl.pallas_call(
        functools.partial(spread_kernel, sizes=sizes),
        grid_spec=pltpu.PrefetchScalarGridSpec(
            num_scalar_prefetch=1,
            grid=(1,),
            in_specs=[held(parts.shape)],
            out_specs=held((total, LANES)),
            scratch_shapes=[pltpu.VMEM(parts.shape, F32)],
        ),
        out_shape=shape((total, LANES), F32),
        compiler_params=params(1),
        cost_estimate=cost(0, 4 * LANES * total),
        name="spread",
    )(at, parts)


def after(value, *others):
    return lax.optimization_barrier((value, *others))[0] if others else value


def swapped(x):
    return lax.ppermute(x, "core", [(0, 1), (1, 0)])


def from_ws(x, bit):
    return lax.ppermute(x, "ws", [(i, i ^ bit) for i in range(lax.axis_size("ws"))])


def neighbours(first, last):
    runs = lax.axis_size("run") * 2
    up = [(i, i + 1) for i in range(runs - 1)]
    down = [(i + 1, i) for i in range(runs - 1)]
    return lax.ppermute(last, ("run", "core"), up), lax.ppermute(first, ("run", "core"), down)


def square():
    return lax.axis_size("ws") == 4 and lax.axis_size("run") == 4


def halved(rows):
    return -(-rows // 16) * 8


def fetched(shard):
    rows = shard.shape[0]
    half = halved(rows)
    own = lax.dynamic_slice_in_dim(shard, lax.axis_index("core") * (rows - half), half, axis=0)
    return [from_ws(own, bit) for bit in (1, 2, 3)]


def whole_weight(at, shard, pieces):
    if pieces is None:
        natural = lax.all_gather(shard, "ws", axis=0, tiled=True)
        return natural, flip(natural[None])[0]
    mine = jnp.stack(pieces)
    return assemble(at, shard, mine, swapped(mine))


def halves_of(shard, *others):
    taps, rows, columns = shard.shape
    half = halved(rows)
    own = lax.dynamic_slice_in_dim(shard, lax.axis_index("core") * (rows - half), half, axis=1)
    pieces = lax.all_gather(after(own, *others), ("ws", "core"), axis=0)
    return pieces.reshape(-1, 2, taps, half, columns)


def summed(*terms):
    total = terms[0].astype(F32)
    for term in terms[1:]:
        total = total + term.astype(F32)
    return total.astype(BF16)


def active(shard):
    return shard >> 1


class Share:
    def __init__(self, first, second):
        self.dims = first.shape
        rows = lambda x: x.reshape(-1, x.shape[-1])
        self.sum, self.second = rows(first), rows(second)
        self.rows = self.sum.shape[0]
        self.half = halved(self.rows)
        run = lax.axis_index("run")
        self.outer = (run == 0) | (run == 3)

    def land(self, *kernels):
        return self.add(after(self.came, *kernels))

    def spread(self):
        near = [(2 * i + active(i), 2 * (i ^ 1) + active(i)) for i in range(4)]
        far = lambda bit: [(2 * i + 1 - active(i), 2 * (i ^ bit) + 1 - active(i)) for i in range(4)]
        move = lambda x, pairs: lax.ppermute(x, ("ws", "core"), pairs)
        self.came = (move(self.second, near), move(self.sum, far(2)), move(self.second, far(3)))
        self.add = self.add_all

    def add_all(self, came):
        self.sum = summed(self.sum, *came)
        return self.sum

    def along(self, x, bits):
        every = []
        for shard in range(4):
            every += [((shard * 4 + i) * 2 + active(shard), (shard * 4 + (i ^ bits)) * 2 + active(shard)) for i in range(4)]
        self.came = (lax.ppermute(x, ("ws", "run", "core"), every),)

    def cut(self, low):
        start = jnp.where(low, 0, self.rows - self.half)
        return lax.dynamic_slice_in_dim(self.sum, start, self.half, axis=0)

    def inward(self):
        self.along(self.cut(~self.outer), 1)
        self.add = self.add_half

    def add_half(self, came):
        self.sum = summed(self.cut(self.outer), *came)
        return self.sum

    def middle(self):
        self.along(self.sum, 3)
        self.add = self.add_all

    def outward(self):
        self.along(self.sum, 1)
        self.add = self.join

    def join(self, came):
        low = jnp.where(self.outer, self.sum, came[0])
        high = jnp.where(self.outer, came[0], self.sum)
        self.sum = jnp.concatenate([low, high[2 * self.half - self.rows :]], axis=0)
        return self.sum

    def both(self):
        shard, core = lax.axis_index("ws"), lax.axis_index("core")
        pairs = [(2 * i + active(i), 2 * i + 1 - active(i)) for i in range(4)]
        other = lax.ppermute(self.sum, ("ws", "core"), pairs)
        return jnp.where(core == active(shard), self.sum, other).astype(F32).reshape(self.dims)


def plain(low, high, axis):
    whole = jnp.concatenate([low, high], axis=axis)
    owned = lax.psum_scatter(whole, "ws", scatter_dimension=axis, tiled=True)
    return lax.psum(owned, ("run", "core")).astype(F32)


class Small:
    def __init__(self, mine):
        self.sum = mine

    def send(self, axis, bit):
        self.came = lax.ppermute(self.sum, axis, [(i, i ^ bit) for i in range(lax.axis_size(axis))])

    def land(self, *kernels):
        self.sum = self.sum + after(self.came, *kernels)


def totals_of(count, sums1, bias, sums2, sums3):
    every = (sums1[0], sums1[1], bias, sums2[0], sums2[1], sums3[0], sums3[1])
    return jnp.concatenate([s.sum(axis=-1).reshape(count, -1) for s in every], axis=1)


def shards(
    inputs,
    cotangent,
    block_ids,
    first_gain,
    first_shift,
    weight_in,
    second_gain,
    second_shift,
    weight_conv,
    third_gain,
    third_shift,
    weight_out,
    output_bias,
):
    x = inputs.transpose(0, 2, 1)
    g = cotangent.transpose(0, 2, 1)
    count, shard, core = lax.axis_size("ws"), lax.axis_index("ws"), lax.axis_index("core")
    easy = square()
    place = jnp.stack([shard, core])
    owned_vectors = (first_gain, first_shift, output_bias, second_gain, second_shift, third_gain, third_shift)
    sizes = tuple(own.size for own in owned_vectors)
    flat = jnp.concatenate(owned_vectors)
    if easy:
        parts = jnp.stack([flat, *[from_ws(flat, bit) for bit in (1, 2, 3)]]).astype(F32)
        vectors = spread(place, parts, sizes)
    else:
        parts = lax.all_gather(flat, "ws", axis=0).astype(F32)
        vectors = spread(jnp.zeros_like(place), parts, sizes)
    in_pieces = fetched(after(weight_in, parts)) if easy else None
    conv_halves = halves_of(weight_conv) if easy else None
    length = block_ids.shape[1]
    ids_before, ids_after = neighbours(block_ids[:, :BORDER], block_ids[:, -BORDER:])
    ids = jnp.concatenate([ids_before, block_ids, ids_after], axis=1)
    same = lambda by: ids[:, BORDER + by : BORDER + by + length] == block_ids
    steps = [DILATION_STEP * (i + 1) for i in range(KERNEL_TAPS // 2)]

    def masks(sign):
        both = jnp.stack([same(sign * by) for by in steps], axis=1)
        return jnp.broadcast_to(both[..., None], (*both.shape, LANES)).astype(BF16)

    mask, mask_back = masks(1), masks(-1)
    act1, stats1 = open_block(x, vectors)
    if easy:
        in_pieces = after(in_pieces, act1)
        out_pieces = fetched(after(weight_out, *in_pieces))
    else:
        out_pieces = None
    w_in, w_in_t = whole_weight(place, weight_in, in_pieces)
    act2, rows2, normed2, stats2 = enter(act1, w_in_t, vectors)
    halo2 = neighbours(rows2[:, :BORDER], rows2[:, -BORDER:])
    if easy:
        out_pieces = after(out_pieces, act2)
    w_out, w_out_t = whole_weight(place, weight_out, out_pieces)
    grad_act3, bias_sums = project(w_out, g)
    if easy:
        w_conv, w_conv_t = join(after(conv_halves, grad_act3), weight_conv.shape[1])
    else:
        w_conv = lax.all_gather(weight_conv, "ws", axis=1, tiled=True)
        w_conv_t = flip(w_conv)
    halo2 = after(halo2, grad_act3)
    act3, rows3, sums3 = conv_block(rows2, *halo2, mask, w_conv_t, vectors, grad_act3)
    halo = neighbours(rows3[:, :BORDER], rows3[:, -BORDER:])
    bit = shard & 1
    give, keep = jnp.stack([1 - core, bit]), jnp.stack([core, bit])
    if not easy:
        give, keep = jnp.zeros_like(give), jnp.ones_like(keep)
    seqs = x.shape[0]
    back = lambda rows, seq, number, into: conv_back(
        rows, *halo, mask_back, w_conv, vectors, normed2, stats2, seq, number, into
    )
    close = lambda low, seq, number, into: leave(low, w_in, x, g, vectors, stats1, seq, number, into)
    width, inner = x.shape[1], act2.shape[1]
    if not easy:
        conv = (act2, rows3, *halo, mask_back)
        halves = lambda **kw: [grads(at, inner, **kw)[0] for at in (give, keep)]
        out_grad = plain(*halves(pair=(act3, g)), 1)
        out_grad = out_grad.transpose(1, 0, 2).reshape(-1, width)
        conv_grad = plain(*halves(taps=tuple(range(KERNEL_TAPS)), conv=conv), 1)
        low2, sums2 = back(rows3, 0, seqs, None)
        in_grad = plain(*halves(pair=(act1, low2)), 1)[0]
        input_grad, sums1 = close(low2, 0, seqs, None)
        block_output = finish(w_out_t, act3, x, vectors, 0, seqs)
    else:
        shard_rows = inner // count
        padded = -(-KERNEL_TAPS * shard_rows // LANES) * LANES
        taps = tap_grads(count, padded, act2, rows3, *halo, mask_back)
        (out_send,) = grads(give, inner, pair=(after(act3, taps), g))
        rows3, act3_late = after((rows3, act3), out_send)
        taps = lax.psum_scatter(taps.reshape(-1, inner), "ws", scatter_dimension=0, tiled=True)
        got_out = swapped(out_send)
        low2, sums2 = back(rows3, 0, seqs, None)
        (in_send,) = grads(give, inner, pair=(act1, low2))
        got_out, act3_late = after((got_out, act3_late), in_send)
        out_parts = grads(keep, inner, pair=(act3_late, g), got=got_out)
        got_in = after(swapped(in_send), *out_parts)
        in_parts = grads(keep, inner, pair=(act1, low2), got=got_in)
        flat = lambda part: part.reshape(-1, inner)
        both = Share(*[jnp.concatenate([flat(o), flat(i)], axis=0) for o, i in zip(out_parts, in_parts)])
        both.spread()
        low2, taps = after((low2, taps), *in_parts)
        taps = lax.psum_scatter(taps, ("run", "core"), scatter_dimension=0, tiled=True)
        input_grad, sums1 = close(low2, 0, seqs, None)
        small = Small(totals_of(count, sums1, bias_sums, sums2, sums3))
        small.send("core", 1)
        both.land(sums1)
        both.inward()
        (w_out_t, act3), taps = after(((w_out_t, act3), taps), both.sum, small.sum)
        taps_sum = lax.all_gather(taps, ("run", "core"), axis=0, tiled=True)
        block_output = finish(w_out_t, act3, x, vectors, 0, seqs)
        small.land(block_output)
        both.land(block_output, small.sum)
        small.send("ws", 1)
        both.middle()
        small.land(both.sum)
        small.send("ws", 2)
        small.land()
        both.land(small.sum, taps_sum)
        small.send("run", 1)
        both.outward()
        small.land(both.sum)
        small.send("run", 2)
        small.land()
        both.land(small.sum)
        rows = both.both()
        taps = taps_sum[: KERNEL_TAPS * shard_rows].astype(F32)
        conv_grad = taps.reshape(KERNEL_TAPS, shard_rows, inner)
        out_grad = jnp.concatenate([rows[:shard_rows], rows[shard_rows : 2 * shard_rows]], axis=1)
        in_grad = rows[2 * shard_rows :]
        small = small.sum

    if not easy:
        small = lax.psum(totals_of(count, sums1, bias_sums, sums2, sums3), ("ws", "run", "core"))
    small = lax.dynamic_index_in_dim(small, shard, axis=0, keepdims=False)
    at, vector_grads = 0, []
    for size in sizes:
        vector_grads.append(small[at : at + size])
        at += size
    gain1, shift1, bias, gain2, shift2, gain3, shift3 = vector_grads
    return (
        block_output.transpose(0, 2, 1),
        input_grad.transpose(0, 2, 1),
        gain1,
        shift1,
        in_grad,
        gain2,
        shift2,
        conv_grad,
        gain3,
        shift3,
        out_grad,
        bias,
    )


def solution(mesh):
    count, runs = mesh.devices.shape
    split = jax.sharding.Mesh(mesh.devices.reshape(count, runs // 2, 2), ("ws", "run", "core"))
    tokens = P("ws", ("run", "core"), None)
    rows = P("ws", None)
    taps = P(None, "ws", None)
    placed = (tokens, tokens, P("ws", ("run", "core")), P("ws"), P("ws"), rows, P("ws"), P("ws"), taps)
    placed += (P("ws"), P("ws"), rows, P("ws"))
    given = (tokens, tokens, P("ws"), P("ws"), rows, P("ws"), P("ws"), taps, P("ws"), P("ws"), rows, P("ws"))
    return jax.shard_map(shards, mesh=split, in_specs=placed, out_specs=given, check_vma=False)
```

```python
import functools
import jax
import jax.numpy as jnp
from jax import lax
from jax.experimental import pallas as pl
from jax.experimental.pallas import tpu as pltpu
from jax.sharding import PartitionSpec as P

KERNEL_TAPS = 5
DILATION_STEP = 16
EPS = 1e-05
LANES = 128
BORDER = KERNEL_TAPS // 2 * DILATION_STEP
F32 = jnp.float32
BF16 = jnp.bfloat16
VMEM_BYTES = 60 * 2**20

NN = (((1,), (0,)), ((), ()))
NT = (((1,), (1,)), ((), ()))


def params(steps=0):
    return pltpu.CompilerParams(
        dimension_semantics=("arbitrary",) * steps or None, vmem_limit_bytes=VMEM_BYTES
    )


def cost(flops, bytes_accessed):
    return pl.CostEstimate(flops=flops // 16, bytes_accessed=bytes_accessed // 16, transcendentals=0)


def shape(dims, dtype=BF16):
    return jax.ShapeDtypeStruct(dims, dtype)


def dot(left, right, dims=NN):
    return lax.dot_general(left, right, dims, preferred_element_type=F32)


def wide(column, lanes):
    return jnp.concatenate([column] * (lanes // LANES), axis=1)


def folded(values):
    total = values[:, :LANES]
    for at in range(LANES, values.shape[1], LANES):
        total = total + values[:, at : at + LANES]
    return total


def logistic(x):
    return 0.5 * jnp.tanh(0.5 * x) + 0.5


def vector(rows, block):
    return pl.BlockSpec((rows, LANES), lambda *_: (block, 0))


def here(rows, lanes, seq=0):
    return pl.BlockSpec((1, rows, lanes), lambda s, t: (s + seq, 0, t))


def held(dims):
    return pl.BlockSpec(dims, lambda *_: (0,) * len(dims))


def each(count, body, init, unroll=True):
    return lax.fori_loop(0, count, body, init, unroll=unroll)


def rows_at(index, size):
    return pl.ds(pl.multiple_of(index * size, size), size)


def row_stats(load, channels, chunk, lanes, unroll=True):
    steps = channels // chunk
    zero = jnp.zeros((chunk, lanes), F32)
    total = each(steps, lambda i, t: t + load(i), zero, unroll)
    mean = jnp.sum(total, axis=0, keepdims=True) * (1.0 / channels)

    def square(i, t):
        centred = load(i) - mean
        return t + centred * centred

    squares = each(steps, square, zero, unroll)
    spread = jnp.sum(squares, axis=0, keepdims=True) * (1.0 / channels)
    return mean, lax.rsqrt(spread + EPS)


def back_first(u, normed, gain, shift):
    pre = normed * gain + shift
    sigma = logistic(pre)
    p = u * (sigma * (1.0 + pre * (1.0 - sigma)))
    return pre, sigma, p, p * gain


def first_step():
    return (pl.program_id(0) == 0) & (pl.program_id(1) == 0)


def last_step():
    return (pl.program_id(0) == pl.num_programs(0) - 1) & (
        pl.program_id(1) == pl.num_programs(1) - 1
    )


def cleared(sums):
    @pl.when(first_step())
    def _():
        sums[...] = jnp.zeros_like(sums)


def handed(sums, out):
    @pl.when(last_step())
    def _():
        out[...] = sums[...]


def open_kernel(x, gain, shift, act1, stats, *, chunk):
    lanes, width = x.shape[2], x.shape[1]
    load = lambda i: x[0, rows_at(i, chunk), :].astype(F32)
    mean, scale = row_stats(load, width, chunk, lanes)

    def activate(i, carry):
        at = rows_at(i, chunk)
        normed = (load(i) - mean) * scale
        pre = normed * wide(gain[at, :], lanes) + wide(shift[at, :], lanes)
        act1[0, at, :] = (pre * logistic(pre)).astype(BF16)
        return carry

    each(width // chunk, activate, 0)
    stats[0] = jnp.concatenate([mean, scale, jnp.zeros((6, lanes), F32)], axis=0)


def open_block(x, vectors, lanes=512, chunk=32):
    seqs, width, length = x.shape
    return pl.pallas_call(
        functools.partial(open_kernel, chunk=chunk),
        grid=(seqs, length // lanes),
        in_specs=[here(width, lanes), vector(width, 0), vector(width, 1)],
        out_specs=[here(width, lanes), here(8, lanes)],
        out_shape=[shape(x.shape), shape((seqs, 8, length), F32)],
        compiler_params=params(2),
        cost_estimate=cost(40 * x.size, 4 * x.size),
        name="open_block",
    )(x, vectors, vectors)


def enter_kernel(act1, w_in, gain, shift, act2, turned, normed2, stats, proj, *, chunk):
    lanes, inner = act1.shape[2], act2.shape[1]
    proj[...] = dot(w_in[...], act1[0])
    load = lambda i: proj[rows_at(i, chunk), :]
    mean, scale = row_stats(load, inner, chunk, lanes, 5)

    def activate(i, carry):
        at = rows_at(i, chunk)
        normed = (load(i) - mean) * scale
        normed2[0, at, :] = normed
        pre = normed * wide(gain[at, :], lanes) + wide(shift[at, :], lanes)
        act2[0, at, :] = (pre * logistic(pre)).astype(BF16)
        return carry

    each(inner // chunk, activate, 0, 5)
    turned[0] = act2[0].T
    stats[0] = jnp.concatenate([scale, jnp.zeros((7, lanes), F32)], axis=0)


def enter(act1, w_in_t, vectors, lanes=512, chunk=32):
    seqs, width, length = act1.shape
    inner = w_in_t.shape[0]
    return pl.pallas_call(
        functools.partial(enter_kernel, chunk=chunk),
        grid=(seqs, length // lanes),
        in_specs=[here(width, lanes), held((inner, width)), vector(inner, 6), vector(inner, 7)],
        out_specs=[
            here(inner, lanes),
            pl.BlockSpec((1, lanes, inner), lambda s, t: (s, t, 0)),
            here(inner, lanes),
            here(8, lanes),
        ],
        out_shape=[
            shape((seqs, inner, length)),
            shape((seqs, length, inner)),
            shape((seqs, inner, length), F32),
            shape((seqs, 8, length), F32),
        ],
        scratch_shapes=[pltpu.VMEM((inner, lanes), F32)],
        compiler_params=params(2),
        cost_estimate=cost(2 * act1.size * inner, seqs * length * (2 * width + 8 * inner)),
        name="enter",
    )(act1, w_in_t, vectors, vectors)


def project_kernel(weight, columns, out, grads, sums, *, chunk):
    cleared(sums)
    out[0] = dot(weight[...], columns[0])

    def body(i, carry):
        at = rows_at(i, chunk)
        sums[at, :] += folded(columns[0, at, :].astype(F32))
        return carry

    each(columns.shape[1] // chunk, body, 0)
    handed(sums, grads)


def project(weight, columns, lanes=512, chunk=32):
    seqs, depth, length = columns.shape
    rows = weight.shape[0]
    return pl.pallas_call(
        functools.partial(project_kernel, chunk=chunk),
        grid=(seqs, length // lanes),
        in_specs=[held((rows, depth)), here(depth, lanes)],
        out_specs=[here(rows, lanes), held((depth, LANES))],
        out_shape=[shape((seqs, rows, length), F32), shape((depth, LANES), F32)],
        scratch_shapes=[pltpu.VMEM((depth, LANES), F32)],
        compiler_params=params(2),
        cost_estimate=cost(2 * columns.size * rows, seqs * length * (2 * depth + 4 * rows)),
        name="project",
    )(weight, columns)


def extend(rows, before, after, mask, whole, masked, seq, sign):
    length = rows.shape[1]
    whole[:BORDER, :] = before[seq]
    whole[BORDER : BORDER + length, :] = rows[seq]
    whole[BORDER + length :, :] = after[seq]
    inner = rows.shape[2]
    chunk = 128
    for later in range(KERNEL_TAPS // 2):
        by = sign * (later + 1) * DILATION_STEP

        def body(i, carry, later=later, by=by):
            kept = mask[seq, later, rows_at(i, chunk), :]
            kept = jnp.concatenate([kept] * -(-inner // LANES), axis=1)[:, :inner]
            start = pl.multiple_of(i * chunk + BORDER + by, DILATION_STEP)
            masked[later, rows_at(i, chunk), :] = whole[pl.ds(start, chunk), :] * kept
            return carry

        each(length // chunk, body, 0, 1)


def tap_rows(whole, masked, tap, sign, start, count):
    by = (tap - KERNEL_TAPS // 2) * DILATION_STEP
    if by > 0:
        return masked[tap - KERNEL_TAPS // 2 - 1, pl.ds(start, count), :]
    return whole[pl.ds(start + (BORDER + sign * by), count), :]


def conv_kernel(rows, before, after, mask, w_conv, gain, shift, upstream, act3, turned, grads, whole, masked, conv, scaled, low, sums, *, chunk):
    tile = pl.program_id(1)
    lanes, inner = act3.shape[2], act3.shape[1]
    cleared(sums)

    @pl.when(tile == 0)
    def _():
        extend(rows, before, after, mask, whole, masked, 0, 1)

    start = pl.multiple_of(tile * lanes, lanes)
    total = None
    for tap in range(KERNEL_TAPS):
        part = dot(w_conv[tap], tap_rows(whole, masked, tap, 1, start, lanes), NT)
        total = part if total is None else total + part
    conv[...] = total
    load = lambda i: conv[rows_at(i, chunk), :]
    mean, scale = row_stats(load, inner, chunk, lanes)

    def first(i, carry):
        at = rows_at(i, chunk)
        normed = (load(i) - mean) * scale
        gains = wide(gain[at, :], lanes)
        pre, sigma, p, q = back_first(upstream[0, at, :], normed, gains, wide(shift[at, :], lanes))
        act3[0, at, :] = (pre * sigma).astype(BF16)
        conv[at, :] = normed
        scaled[at, :] = q
        sums[0, at, :] += folded(p * normed)
        sums[1, at, :] += folded(p)
        return carry[0] + q, carry[1] + q * normed

    zero = jnp.zeros((chunk, lanes), F32)
    one, two = each(inner // chunk, first, (zero, zero))
    one = jnp.sum(one, axis=0, keepdims=True) * (1.0 / inner)
    two = jnp.sum(two, axis=0, keepdims=True) * (1.0 / inner)

    def second(i, carry):
        at = rows_at(i, chunk)
        low[at, :] = (scale * (scaled[at, :] - one - conv[at, :] * two)).astype(BF16)
        return carry

    each(inner // chunk, second, 0)
    turned[0] = low[...].T
    handed(sums, grads)


def conv_block(rows, before, after, mask, w_conv_t, vectors, upstream, lanes=512, chunk=16):
    seqs, length, inner = rows.shape
    seq = lambda *dims: pl.BlockSpec((1, *dims), lambda s, t: (s,) + (0,) * len(dims))
    return pl.pallas_call(
        functools.partial(conv_kernel, chunk=chunk),
        grid=(seqs, length // lanes),
        in_specs=[
            seq(length, inner),
            seq(BORDER, inner),
            seq(BORDER, inner),
            seq(2, length, LANES),
            held(w_conv_t.shape),
            vector(inner, 8),
            vector(inner, 9),
            here(inner, lanes),
        ],
        out_specs=[
            here(inner, lanes),
            pl.BlockSpec((1, lanes, inner), lambda s, t: (s, t, 0)),
            held((2, inner, LANES)),
        ],
        out_shape=[
            shape((seqs, inner, length)),
            shape((seqs, length, inner)),
            shape((2, inner, LANES), F32),
        ],
        scratch_shapes=[
            pltpu.VMEM((length + 2 * BORDER, inner), BF16),
            pltpu.VMEM((KERNEL_TAPS // 2, length, inner), BF16),
            pltpu.VMEM((inner, lanes), F32),
            pltpu.VMEM((inner, lanes), F32),
            pltpu.VMEM((inner, lanes), BF16),
            pltpu.VMEM((2, inner, LANES), F32),
        ],
        compiler_params=params(2),
        cost_estimate=cost(2 * rows.size * w_conv_t.size // inner, 12 * rows.size),
        name="conv_block",
    )(rows, before, after, mask, w_conv_t, vectors, vectors, upstream)


def conv_back_kernel(rows, before, after, mask, w_conv, gain, shift, normed2, stats, *rest, chunk):
    out, grads, whole, masked, grad, scaled, sums = rest[-7:]
    tile = pl.program_id(1)
    lanes, inner = out.shape[2], out.shape[1]
    cleared(sums)

    @pl.when(tile == 0)
    def _():
        extend(rows, before, after, mask, whole, masked, 0, -1)

    start = pl.multiple_of(tile * lanes, lanes)
    total = None
    for tap in range(KERNEL_TAPS):
        part = dot(w_conv[tap], tap_rows(whole, masked, tap, -1, start, lanes), NT)
        total = part if total is None else total + part
    grad[...] = total
    scale = stats[0, 0:1, :]

    def first(i, carry):
        at = rows_at(i, chunk)
        normed = normed2[0, at, :]
        _, _, p, q = back_first(
            grad[at, :], normed, wide(gain[at, :], lanes), wide(shift[at, :], lanes)
        )
        scaled[at, :] = q
        sums[0, at, :] += folded(p * normed)
        sums[1, at, :] += folded(p)
        return carry[0] + q, carry[1] + q * normed

    zero = jnp.zeros((chunk, lanes), F32)
    one, two = each(inner // chunk, first, (zero, zero))
    one = jnp.sum(one, axis=0, keepdims=True) * (1.0 / inner)
    two = jnp.sum(two, axis=0, keepdims=True) * (1.0 / inner)

    def second(i, carry):
        at = rows_at(i, chunk)
        out[0, at, :] = (scale * (scaled[at, :] - one - normed2[0, at, :] * two)).astype(BF16)
        return carry

    each(inner // chunk, second, 0)
    handed(sums, grads)


def conv_back(rows, before, after, mask, w_conv, vectors, normed2, stats, first, count, into=None, lanes=512, chunk=16):
    seqs, length, inner = rows.shape
    seq = lambda *dims: pl.BlockSpec((1, *dims), lambda s, t: (s + first,) + (0,) * len(dims))
    more = () if into is None else (into,)
    return pl.pallas_call(
        functools.partial(conv_back_kernel, chunk=chunk),
        grid=(count, length // lanes),
        in_specs=[
            seq(length, inner),
            seq(BORDER, inner),
            seq(BORDER, inner),
            seq(2, length, LANES),
            held(w_conv.shape),
            vector(inner, 6),
            vector(inner, 7),
            here(inner, lanes, first),
            here(8, lanes, first),
        ]
        + [pl.BlockSpec(memory_space=pl.ANY)] * len(more),
        out_specs=[here(inner, lanes, first), held((2, inner, LANES))],
        input_output_aliases={9: 0} if more else {},
        out_shape=[shape((seqs, inner, length)), shape((2, inner, LANES), F32)],
        scratch_shapes=[
            pltpu.VMEM((length + 2 * BORDER, inner), BF16),
            pltpu.VMEM((KERNEL_TAPS // 2, length, inner), BF16),
            pltpu.VMEM((inner, lanes), F32),
            pltpu.VMEM((inner, lanes), F32),
            pltpu.VMEM((2, inner, LANES), F32),
        ],
        compiler_params=params(2),
        cost_estimate=cost(2 * rows.size * w_conv.size * count // (seqs * inner), 10 * rows.size * count // seqs),
        name="conv_back",
    )(rows, before, after, mask, w_conv, vectors, vectors, normed2, stats, *more)


def leave_kernel(low, w_in, x, g, gain, shift, stats, *rest, chunk):
    out, grads, grad, sums = rest[-4:]
    lanes, width = out.shape[2], out.shape[1]
    cleared(sums)
    grad[...] = dot(w_in[...], low[0])
    mean = stats[0, 0:1, :]
    scale = stats[0, 1:2, :]
    norm = lambda at: (x[0, at, :].astype(F32) - mean) * scale

    def first(i, carry):
        at = rows_at(i, chunk)
        normed = norm(at)
        _, _, p, q = back_first(
            grad[at, :], normed, wide(gain[at, :], lanes), wide(shift[at, :], lanes)
        )
        grad[at, :] = q
        sums[0, at, :] += folded(p * normed)
        sums[1, at, :] += folded(p)
        return carry[0] + q, carry[1] + q * normed

    zero = jnp.zeros((chunk, lanes), F32)
    one, two = each(width // chunk, first, (zero, zero))
    one = jnp.sum(one, axis=0, keepdims=True) * (1.0 / width)
    two = jnp.sum(two, axis=0, keepdims=True) * (1.0 / width)

    def second(i, carry):
        at = rows_at(i, chunk)
        branch = scale * (grad[at, :] - one - norm(at) * two)
        out[0, at, :] = (g[0, at, :].astype(F32) + branch).astype(BF16)
        return carry

    each(width // chunk, second, 0)
    handed(sums, grads)


def leave(low, w_in, x, g, vectors, stats, first, count, into=None, lanes=256, chunk=16):
    seqs, inner, length = low.shape
    width = x.shape[1]
    more = () if into is None else (into,)
    return pl.pallas_call(
        functools.partial(leave_kernel, chunk=chunk),
        grid=(count, length // lanes),
        in_specs=[
            here(inner, lanes, first),
            held((width, inner)),
            here(width, lanes, first),
            here(width, lanes, first),
            vector(width, 0),
            vector(width, 1),
            here(8, lanes, first),
        ]
        + [pl.BlockSpec(memory_space=pl.ANY)] * len(more),
        input_output_aliases={7: 0} if more else {},
        out_specs=[here(width, lanes, first), held((2, width, LANES))],
        out_shape=[shape(x.shape), shape((2, width, LANES), F32)],
        scratch_shapes=[pltpu.VMEM((width, lanes), F32), pltpu.VMEM((2, width, LANES), F32)],
        compiler_params=params(2),
        cost_estimate=cost(2 * low.size * width * count // seqs, (2 * low.size + 6 * x.size) * count // seqs),
        name="leave",
    )(low, w_in, x, g, vectors, vectors, stats, *more)


def finish_kernel(w_out, act3, x, bias, *rest, chunk):
    out, proj = rest[-2:]
    lanes, width = out.shape[2], out.shape[1]
    proj[...] = dot(w_out[...], act3[0])

    def body(i, carry):
        at = rows_at(i, chunk)
        out[0, at, :] = (x[0, at, :].astype(F32) + proj[at, :] + wide(bias[at, :], lanes)).astype(BF16)
        return carry

    each(width // chunk, body, 0)


def finish(w_out_t, act3, x, vectors, first, count, into=None, lanes=512, chunk=32):
    more = () if into is None else (into,)
    seqs, inner, length = act3.shape
    width = x.shape[1]
    return pl.pallas_call(
        functools.partial(finish_kernel, chunk=chunk),
        grid=(count, length // lanes),
        in_specs=[held((width, inner)), here(inner, lanes, first), here(width, lanes, first), vector(width, 2)]
        + [pl.BlockSpec(memory_space=pl.ANY)] * len(more),
        input_output_aliases={4: 0} if more else {},
        out_specs=here(width, lanes, first),
        out_shape=shape(x.shape),
        scratch_shapes=[pltpu.VMEM((width, lanes), F32)],
        compiler_params=params(2),
        cost_estimate=cost(0, 0),
        name="finish",
    )(w_out_t, act3, x, vectors, *more)


def grads_kernel(at, *refs, pair, taps, keep, units):
    refs = list(refs)
    take = lambda n: [refs.pop(0) for _ in range(n)]
    sources = []
    left = right = act2 = rows3 = before = after = mask = got = None
    if pair:
        left, right = take(2)
    if taps:
        act2, rows3, before, after, mask = take(5)
    if keep:
        (got,) = take(1)
    outs = take(2 if keep else len(units))
    sems = refs.pop(-1)
    loads = []

    def load(source, target):
        copy = pltpu.make_async_copy(source, target, sems.at[len(loads)])
        copy.start()
        loads.append(copy)
        return copy

    if pair:
        left_here, right_here = take(2)
        half = left_here.shape[1]
        columns = right_here.shape[1] // pair
        first = [load(left.at[:, pl.ds(pl.multiple_of(at[0] * half, half), half), :], left_here)]
        blocks = []
        for i in range(pair):
            span = pl.ds(i * columns, columns)
            blocks.append(load(right.at[:, span, :], right_here.at[:, span, :]))
    if taps:
        act2_here, whole, mask_here, masked = take(4)
        seqs, length = rows3.shape[0], rows3.shape[1]
        half2 = act2_here.shape[1]
        ready = [load(act2.at[:, pl.ds(pl.multiple_of(at[0] * half2, half2), half2), :], act2_here)]
        for seq in range(seqs):
            ready.append(load(rows3.at[seq], whole.at[seq, pl.ds(BORDER, length), :]))
        ready.append(load(before, whole.at[:, pl.ds(0, BORDER), :]))
        ready.append(load(after, whole.at[:, pl.ds(BORDER + length, BORDER), :]))
        ready.append(load(mask, mask_here))
    if keep:
        got_here, total = take(2)
        got_load = load(got, got_here)

    def give(step, value):
        if not keep:
            place = step
            for out, size in zip(outs, units):
                if place < size:
                    out[place] = value.astype(BF16)
                    return
                place -= size
        if step == 0:
            got_load.wait()
        total[...] = value + got_here[step].astype(F32)
        rows = outs[0].shape[1]
        for place, out in enumerate(outs):
            start = pl.multiple_of((at[1] ^ place) * rows, 8)
            out[step] = total[pl.ds(start, rows), :].astype(BF16)

    for i in range(pair):
        if i == 0:
            first[0].wait()
        blocks[i].wait()
        value = None
        for seq in range(left_here.shape[0]):
            part = dot(left_here[seq], right_here[seq, i * columns : (i + 1) * columns, :], NT)
            value = part if value is None else value + part
        give(i, value)
    for step, tap in enumerate(taps):
        by = (tap - KERNEL_TAPS // 2) * DILATION_STEP
        if step == 0:
            for copy in ready:
                copy.wait()
        value = None
        for seq in range(seqs):
            if by > 0:
                mask_rows(whole.at[seq], mask_here, masked, seq, by)
                rows = masked[...]
            else:
                rows = whole[seq, BORDER - by : BORDER - by + length, :]
            part = dot(act2_here[seq], rows)
            value = part if value is None else value + part
        give(pair + step, value)


def tap_grads_kernel(left, rows3, before, after, mask, out, left_here, whole, mask_here, masked, total, done, sems):
    seqs, length = rows3.shape[0], rows3.shape[1]
    count, size = out.shape[0], left.shape[1] // out.shape[0]

    def copy(place, source, target):
        moving = pltpu.make_async_copy(source, target, sems.at[place])
        moving.start()
        return moving

    loads = [copy(0, left, left_here), copy(1, mask, mask_here)]
    loads.append(copy(2, before, whole.at[:, pl.ds(0, BORDER), :]))
    loads.append(copy(3, after, whole.at[:, pl.ds(BORDER + length, BORDER), :]))
    for seq in range(seqs):
        loads.append(copy(4 + seq, rows3.at[seq], whole.at[seq, pl.ds(BORDER, length), :]))
    for load in loads:
        load.wait()
    stores = []
    for tap in range(KERNEL_TAPS):
        by = (tap - KERNEL_TAPS // 2) * DILATION_STEP
        value = None
        for seq in range(seqs):
            if by > 0:
                mask_rows(whole.at[seq], mask_here, masked, seq, by)
                rows = masked[...]
            else:
                rows = whole[seq, BORDER - by : BORDER - by + length, :]
            part = dot(left_here[seq], rows)
            value = part if value is None else value + part
        total[tap % 2] = value
        last = tap == KERNEL_TAPS - 1
        if tap % 2 == 0 and not last:
            continue
        start = tap // 2 * 2 * size
        height = out.shape[1] - start if last else 2 * size
        fill = jnp.zeros((height - size, total.shape[2]), F32)
        for shard in range(count):
            span = slice(shard * size, (shard + 1) * size)
            below = fill if last else total[1, span, :]
            done[tap // 2, shard, :height, :] = jnp.concatenate([total[0, span, :], below], axis=0).astype(BF16)
            place = 4 + seqs + tap // 2 * count + shard
            stores.append(copy(place, done.at[tap // 2, shard, pl.ds(0, height), :], out.at[shard, pl.ds(start, height), :]))
    for store in stores:
        store.wait()


def tap_grads(count, padded, left, rows3, before, after, mask):
    seqs, length, inner = rows3.shape
    steps = -(-KERNEL_TAPS // 2)
    operands = (left, rows3, before, after, mask)
    return pl.pallas_call(
        tap_grads_kernel,
        in_specs=[pl.BlockSpec(memory_space=pl.ANY)] * len(operands),
        out_specs=pl.BlockSpec(memory_space=pl.ANY),
        out_shape=shape((count, padded, inner)),
        scratch_shapes=[
            pltpu.VMEM(left.shape, BF16),
            pltpu.VMEM((seqs, length + 2 * BORDER, inner), BF16),
            pltpu.VMEM(mask.shape, BF16),
            pltpu.VMEM((length, inner), BF16),
            pltpu.VMEM((2, inner, inner), F32),
            pltpu.VMEM((steps, count, 2 * inner // count, inner), BF16),
            pltpu.SemaphoreType.DMA((4 + seqs + steps * count,)),
        ],
        compiler_params=params(),
        cost_estimate=cost(2 * KERNEL_TAPS * left.size * inner, 4 * left.size + 10 * inner * inner),
        name="tap_grads",
    )(*operands)


def mask_rows(whole, mask, masked, seq, by):
    length, inner = masked.shape
    chunk = 128

    def body(i, carry):
        kept = mask[seq, by // DILATION_STEP - 1, rows_at(i, chunk), :]
        kept = jnp.concatenate([kept] * -(-inner // LANES), axis=1)[:, :inner]
        start = pl.multiple_of(i * chunk + BORDER - by, DILATION_STEP)
        masked[rows_at(i, chunk), :] = whole[pl.ds(start, chunk), :] * kept
        return carry

    each(length // chunk, body, 0, 1)


def grads(at, columns, pair=None, taps=(), conv=(), got=None, units=None):
    operands, scratch = [], []
    count, flops, copies = 0, 0, 0
    if pair is not None:
        left, right = pair
        half = left.shape[1] // 2
        count = right.shape[1] // columns
        operands += [left, right]
        scratch += [pltpu.VMEM((left.shape[0], half, left.shape[2]), BF16), pltpu.VMEM(right.shape, BF16)]
        copies += 1 + count
        flops += left.size * right.shape[1]
    if taps:
        act2, rows3, _, _, mask = conv
        seqs, length, inner = rows3.shape
        half = inner // 2
        operands += conv
        scratch += [
            pltpu.VMEM((seqs, half, length), BF16),
            pltpu.VMEM((seqs, length + 2 * BORDER, inner), BF16),
            pltpu.VMEM(mask.shape, BF16),
            pltpu.VMEM((length, inner), BF16),
        ]
        copies += 4 + seqs
        flops += act2.size * inner * len(taps)
    total = count + len(taps)
    if got is None:
        units = units or (total,)
        dims = [(size, half, columns) for size in units]
    else:
        operands.append(got)
        scratch += [pltpu.VMEM(got.shape, BF16), pltpu.VMEM((half, columns), F32)]
        copies += 1
        dims = [(total, half // 2, columns)] * 2
    scratch.append(pltpu.SemaphoreType.DMA((copies,)))
    return pl.pallas_call(
        functools.partial(grads_kernel, pair=count, taps=taps, keep=got is not None, units=units),
        grid_spec=pltpu.PrefetchScalarGridSpec(
            num_scalar_prefetch=1,
            grid=(1,),
            in_specs=[pl.BlockSpec(memory_space=pl.ANY)] * len(operands),
            out_specs=[held(d) for d in dims],
            scratch_shapes=scratch,
        ),
        out_shape=[shape(d) for d in dims],
        compiler_params=params(1),
        cost_estimate=cost(flops, 2 * sum(o.size for o in operands)),
        name="grads",
    )(at, *operands)


def flip_kernel(w, out):
    for tap in range(w.shape[0]):
        out[tap] = w[tap].T


def flip(w):
    taps, rows, columns = w.shape
    return pl.pallas_call(
        flip_kernel,
        out_shape=shape((taps, columns, rows)),
        compiler_params=params(),
        cost_estimate=cost(0, 4 * w.size),
        name="flip",
    )(w)


def assemble_kernel(at, own, mine, other, natural, turned, whole, *, gap):
    rows, half = own.shape[0], mine.shape[1]
    whole[pl.ds(pl.multiple_of(at[0] * rows, 8), rows), :] = own[...].astype(F32)
    for step in range(mine.shape[0]):
        for pieces, core in ((mine, at[1]), (other, 1 - at[1])):
            start = (at[0] ^ (step + 1)) * rows + core * (rows - half)
            whole[pl.ds(pl.multiple_of(start, 8), half), :] = pieces[step].astype(F32)
    natural[...] = whole[...].astype(BF16)
    turned[...] = natural[...].T


def assemble(at, own, mine, other):
    rows, columns = own.shape
    full = rows * (mine.shape[0] + 1)
    dims = [(full, columns), (columns, full)]
    return pl.pallas_call(
        functools.partial(assemble_kernel, gap=0),
        grid_spec=pltpu.PrefetchScalarGridSpec(
            num_scalar_prefetch=1,
            grid=(1,),
            in_specs=[held(own.shape), held(mine.shape), held(other.shape)],
            out_specs=[held(d) for d in dims],
            scratch_shapes=[pltpu.VMEM((full, columns), F32)],
        ),
        out_shape=[shape(d) for d in dims],
        compiler_params=params(1),
        cost_estimate=cost(0, 6 * full * columns),
        name="assemble",
    )(at, own, mine, other)


def join_kernel(pieces, natural, turned, whole, *, rows):
    count, half = pieces.shape[0], pieces.shape[3]
    for shard in range(count):
        for core in range(2):
            start = shard * rows + core * (rows - half)
            whole[start : start + half, :] = pieces[shard, core, 0].astype(F32)
    natural[0] = whole[...].astype(BF16)
    turned[0] = natural[0].T


def join(pieces, rows):
    count, cores, taps, half, columns = pieces.shape
    full = count * rows
    dims = [(taps, full, columns), (taps, columns, full)]
    return pl.pallas_call(
        functools.partial(join_kernel, rows=rows),
        grid=(taps,),
        in_specs=[pl.BlockSpec((count, cores, 1, half, columns), lambda t: (0, 0, t, 0, 0))],
        out_specs=[pl.BlockSpec((1, *d[1:]), lambda t: (t, 0, 0)) for d in dims],
        out_shape=[shape(d) for d in dims],
        scratch_shapes=[pltpu.VMEM((full, columns), F32)],
        compiler_params=params(1),
        cost_estimate=cost(0, 6 * taps * full * columns),
        name="join",
    )(pieces)


def spread_kernel(at, parts, out, rows, *, sizes):
    count = parts.shape[0]
    for i in range(count):
        rows[pl.ds(at[0] ^ i, 1), :] = parts[i : i + 1, :]
    start, base = 0, 0
    for size in sizes:
        for shard in range(count):
            row = rows[shard : shard + 1, start : start + size]
            out[base : base + size, :] = jnp.broadcast_to(row, (LANES, size)).T
            base += size
        start += size


def spread(at, parts, sizes):
    total = parts.size
    return pl.pallas_call(
        functools.partial(spread_kernel, sizes=sizes),
        grid_spec=pltpu.PrefetchScalarGridSpec(
            num_scalar_prefetch=1,
            grid=(1,),
            in_specs=[held(parts.shape)],
            out_specs=held((total, LANES)),
            scratch_shapes=[pltpu.VMEM(parts.shape, F32)],
        ),
        out_shape=shape((total, LANES), F32),
        compiler_params=params(1),
        cost_estimate=cost(0, 4 * LANES * total),
        name="spread",
    )(at, parts)


def after(value, *others):
    return lax.optimization_barrier((value, *others))[0] if others else value


def swapped(x):
    return lax.ppermute(x, "core", [(0, 1), (1, 0)])


def from_ws(x, bit):
    return lax.ppermute(x, "ws", [(i, i ^ bit) for i in range(lax.axis_size("ws"))])


def neighbours(first, last):
    runs = lax.axis_size("run") * 2
    up = [(i, i + 1) for i in range(runs - 1)]
    down = [(i + 1, i) for i in range(runs - 1)]
    return lax.ppermute(last, ("run", "core"), up), lax.ppermute(first, ("run", "core"), down)


def square():
    return lax.axis_size("ws") == 4 and lax.axis_size("run") == 4


def halved(rows):
    return -(-rows // 16) * 8


def fetched(shard):
    rows = shard.shape[0]
    half = halved(rows)
    own = lax.dynamic_slice_in_dim(shard, lax.axis_index("core") * (rows - half), half, axis=0)
    return [from_ws(own, bit) for bit in (1, 2, 3)]


def whole_weight(at, shard, pieces):
    if pieces is None:
        natural = lax.all_gather(shard, "ws", axis=0, tiled=True)
        return natural, flip(natural[None])[0]
    mine = jnp.stack(pieces)
    return assemble(at, shard, mine, swapped(mine))


def halves_of(shard, *others):
    taps, rows, columns = shard.shape
    half = halved(rows)
    own = lax.dynamic_slice_in_dim(shard, lax.axis_index("core") * (rows - half), half, axis=1)
    pieces = lax.all_gather(after(own, *others), ("ws", "core"), axis=0)
    return pieces.reshape(-1, 2, taps, half, columns)


def summed(*terms):
    total = terms[0].astype(F32)
    for term in terms[1:]:
        total = total + term.astype(F32)
    return total.astype(BF16)


def active(shard):
    return shard >> 1


class Share:
    def __init__(self, first, second):
        self.dims = first.shape
        rows = lambda x: x.reshape(-1, x.shape[-1])
        self.sum, self.second = rows(first), rows(second)

    def land(self, *kernels):
        self.sum = summed(self.sum, *after(self.came, *kernels))
        return self.sum

    def spread(self):
        near = [(2 * i + active(i), 2 * (i ^ 1) + active(i)) for i in range(4)]
        far = lambda bit: [(2 * i + 1 - active(i), 2 * (i ^ bit) + 1 - active(i)) for i in range(4)]
        move = lambda x, pairs: lax.ppermute(x, ("ws", "core"), pairs)
        self.came = (move(self.second, near), move(self.sum, far(2)), move(self.second, far(3)))

    def along(self, x, bits):
        every = []
        for shard in range(4):
            every += [((shard * 4 + i) * 2 + active(shard), (shard * 4 + (i ^ bits)) * 2 + active(shard)) for i in range(4)]
        self.came = (lax.ppermute(x, ("ws", "run", "core"), every),)

    def inward(self):
        self.along(self.sum, 1)

    def middle(self):
        self.along(self.sum, 3)

    def both(self):
        shard, core = lax.axis_index("ws"), lax.axis_index("core")
        pairs = [(2 * i + active(i), 2 * i + 1 - active(i)) for i in range(4)]
        other = lax.ppermute(self.sum, ("ws", "core"), pairs)
        return jnp.where(core == active(shard), self.sum, other).astype(F32).reshape(self.dims)


def plain(low, high, axis):
    whole = jnp.concatenate([low, high], axis=axis)
    owned = lax.psum_scatter(whole, "ws", scatter_dimension=axis, tiled=True)
    return lax.psum(owned, ("run", "core")).astype(F32)


class Small:
    def __init__(self, mine):
        self.sum = mine

    def send(self, axis, bit):
        self.came = lax.ppermute(self.sum, axis, [(i, i ^ bit) for i in range(lax.axis_size(axis))])

    def land(self, *kernels):
        self.sum = self.sum + after(self.came, *kernels)


def totals_of(count, sums1, bias, sums2, sums3):
    every = (sums1[0], sums1[1], bias, sums2[0], sums2[1], sums3[0], sums3[1])
    return jnp.concatenate([s.sum(axis=-1).reshape(count, -1) for s in every], axis=1)


def shards(
    inputs,
    cotangent,
    block_ids,
    first_gain,
    first_shift,
    weight_in,
    second_gain,
    second_shift,
    weight_conv,
    third_gain,
    third_shift,
    weight_out,
    output_bias,
):
    x = inputs.transpose(0, 2, 1)
    g = cotangent.transpose(0, 2, 1)
    count, shard, core = lax.axis_size("ws"), lax.axis_index("ws"), lax.axis_index("core")
    easy = square()
    place = jnp.stack([shard, core])
    owned_vectors = (first_gain, first_shift, output_bias, second_gain, second_shift, third_gain, third_shift)
    sizes = tuple(own.size for own in owned_vectors)
    flat = jnp.concatenate(owned_vectors)
    if easy:
        parts = jnp.stack([flat, *[from_ws(flat, bit) for bit in (1, 2, 3)]]).astype(F32)
        vectors = spread(place, parts, sizes)
    else:
        parts = lax.all_gather(flat, "ws", axis=0).astype(F32)
        vectors = spread(jnp.zeros_like(place), parts, sizes)
    in_pieces = fetched(after(weight_in, parts)) if easy else None
    conv_halves = halves_of(weight_conv) if easy else None
    act1, stats1 = open_block(x, vectors)
    length = block_ids.shape[1]
    ids_before, ids_after = neighbours(block_ids[:, :BORDER], block_ids[:, -BORDER:])
    ids = jnp.concatenate([ids_before, block_ids, ids_after], axis=1)
    same = lambda by: ids[:, BORDER + by : BORDER + by + length] == block_ids
    steps = [DILATION_STEP * (i + 1) for i in range(KERNEL_TAPS // 2)]

    def masks(sign):
        both = jnp.stack([same(sign * by) for by in steps], axis=1)
        return jnp.broadcast_to(both[..., None], (*both.shape, LANES)).astype(BF16)

    mask, mask_back = masks(1), masks(-1)
    if easy:
        mask, mask_back = after((mask, mask_back), act1)
    if easy:
        in_pieces = after(in_pieces, act1, mask, mask_back)
        out_pieces = fetched(after(weight_out, *in_pieces))
    else:
        out_pieces = None
    w_in, w_in_t = whole_weight(place, weight_in, in_pieces)
    act2, rows2, normed2, stats2 = enter(act1, w_in_t, vectors)
    halo2 = neighbours(rows2[:, :BORDER], rows2[:, -BORDER:])
    if easy:
        out_pieces = after(out_pieces, act2)
    w_out, w_out_t = whole_weight(place, weight_out, out_pieces)
    grad_act3, bias_sums = project(w_out, g)
    if easy:
        w_conv, w_conv_t = join(after(conv_halves, grad_act3), weight_conv.shape[1])
    else:
        w_conv = lax.all_gather(weight_conv, "ws", axis=1, tiled=True)
        w_conv_t = flip(w_conv)
    halo2 = after(halo2, grad_act3)
    act3, rows3, sums3 = conv_block(rows2, *halo2, mask, w_conv_t, vectors, grad_act3)
    halo = neighbours(rows3[:, :BORDER], rows3[:, -BORDER:])
    bit = shard & 1
    give, keep = jnp.stack([1 - core, bit]), jnp.stack([core, bit])
    if not easy:
        give, keep = jnp.zeros_like(give), jnp.ones_like(keep)
    seqs = x.shape[0]
    back = lambda rows, seq, number, into: conv_back(
        rows, *halo, mask_back, w_conv, vectors, normed2, stats2, seq, number, into
    )
    close = lambda low, seq, number, into: leave(low, w_in, x, g, vectors, stats1, seq, number, into)
    width, inner = x.shape[1], act2.shape[1]
    if not easy:
        conv = (act2, rows3, *halo, mask_back)
        halves = lambda **kw: [grads(at, inner, **kw)[0] for at in (give, keep)]
        out_grad = plain(*halves(pair=(act3, g)), 1)
        out_grad = out_grad.transpose(1, 0, 2).reshape(-1, width)
        conv_grad = plain(*halves(taps=tuple(range(KERNEL_TAPS)), conv=conv), 1)
        low2, sums2 = back(rows3, 0, seqs, None)
        in_grad = plain(*halves(pair=(act1, low2)), 1)[0]
        input_grad, sums1 = close(low2, 0, seqs, None)
        block_output = finish(w_out_t, act3, x, vectors, 0, seqs)
    else:
        shard_rows = inner // count
        padded = -(-KERNEL_TAPS * shard_rows // LANES) * LANES
        taps = tap_grads(count, padded, act2, rows3, *halo, mask_back)
        (out_send,) = grads(give, inner, pair=(after(act3, taps), g))
        got_out = swapped(out_send)
        taps = lax.psum_scatter(taps.reshape(-1, inner), "ws", scatter_dimension=0, tiled=True)
        out = Share(*grads(keep, inner, pair=(act3, g), got=got_out))
        out.spread()
        low2, sums2 = back(after(rows3, out.sum), 0, seqs, None)
        out.land(low2)
        out.inward()
        (in_send,) = grads(give, inner, pair=(act1, after(low2, out.sum)))
        got_in = swapped(in_send)
        out.land(in_send)
        out.middle()
        got_in = after(got_in, out.sum)
        both = Share(*grads(keep, inner, pair=(act1, low2), got=got_in))
        both.spread()
        out.land(both.sum)
        rows = out.both()
        low2, taps = after((low2, taps), both.sum, out.sum)
        taps = lax.psum_scatter(taps, ("run", "core"), scatter_dimension=0, tiled=True)
        input_grad, sums1 = close(low2, 0, seqs, None)
        small = Small(totals_of(count, sums1, bias_sums, sums2, sums3))
        small.send("core", 1)
        both.land(sums1)
        both.inward()
        small.land(both.sum)
        small.send("ws", 1)
        (w_out_t, act3), taps = after(((w_out_t, act3), taps), both.sum, small.sum, rows)
        taps_sum = lax.all_gather(taps, ("run", "core"), axis=0, tiled=True)
        block_output = finish(w_out_t, act3, x, vectors, 0, seqs)
        small.land(block_output)
        both.land(block_output, small.sum)
        small.send("ws", 2)
        both.middle()
        small.land(both.sum)
        small.send("run", 1)
        small.land()
        small.send("run", 2)
        small.land()
        both.land(small.sum, taps_sum)
        taps = taps_sum[: KERNEL_TAPS * shard_rows].astype(F32)
        conv_grad = taps.reshape(KERNEL_TAPS, shard_rows, inner)
        out_grad = jnp.concatenate([rows[0], rows[1]], axis=1)
        in_grad = both.both().reshape(-1, inner)
        small = small.sum

    if not easy:
        small = lax.psum(totals_of(count, sums1, bias_sums, sums2, sums3), ("ws", "run", "core"))
    small = lax.dynamic_index_in_dim(small, shard, axis=0, keepdims=False)
    at, vector_grads = 0, []
    for size in sizes:
        vector_grads.append(small[at : at + size])
        at += size
    gain1, shift1, bias, gain2, shift2, gain3, shift3 = vector_grads
    return (
        block_output.transpose(0, 2, 1),
        input_grad.transpose(0, 2, 1),
        gain1,
        shift1,
        in_grad,
        gain2,
        shift2,
        conv_grad,
        gain3,
        shift3,
        out_grad,
        bias,
    )


def solution(mesh):
    count, runs = mesh.devices.shape
    split = jax.sharding.Mesh(mesh.devices.reshape(count, runs // 2, 2), ("ws", "run", "core"))
    tokens = P("ws", ("run", "core"), None)
    rows = P("ws", None)
    taps = P(None, "ws", None)
    placed = (tokens, tokens, P("ws", ("run", "core")), P("ws"), P("ws"), rows, P("ws"), P("ws"), taps)
    placed += (P("ws"), P("ws"), rows, P("ws"))
    given = (tokens, tokens, P("ws"), P("ws"), rows, P("ws"), P("ws"), taps, P("ws"), P("ws"), rows, P("ws"))
    return jax.shard_map(shards, mesh=split, in_specs=placed, out_specs=given, check_vma=False)
```

```python
import functools
import jax
import jax.numpy as jnp
from jax import lax
from jax.experimental import pallas as pl
from jax.experimental.pallas import tpu as pltpu
from jax.sharding import PartitionSpec as P

KERNEL_TAPS = 5
DILATION_STEP = 16
EPS = 1e-05
LANES = 128
BORDER = KERNEL_TAPS // 2 * DILATION_STEP
F32 = jnp.float32
BF16 = jnp.bfloat16
VMEM_BYTES = 60 * 2**20

NN = (((1,), (0,)), ((), ()))
NT = (((1,), (1,)), ((), ()))


def params(steps=0):
    return pltpu.CompilerParams(
        dimension_semantics=("arbitrary",) * steps or None, vmem_limit_bytes=VMEM_BYTES
    )


def cost(flops, bytes_accessed):
    return pl.CostEstimate(flops=flops // 16, bytes_accessed=bytes_accessed // 16, transcendentals=0)


def shape(dims, dtype=BF16):
    return jax.ShapeDtypeStruct(dims, dtype)


def dot(left, right, dims=NN):
    return lax.dot_general(left, right, dims, preferred_element_type=F32)


def wide(column, lanes):
    return jnp.concatenate([column] * (lanes // LANES), axis=1)


def folded(values):
    total = values[:, :LANES]
    for at in range(LANES, values.shape[1], LANES):
        total = total + values[:, at : at + LANES]
    return total


def logistic(x):
    return 0.5 * jnp.tanh(0.5 * x) + 0.5


def vector(rows, block):
    return pl.BlockSpec((rows, LANES), lambda *_: (block, 0))


def here(rows, lanes, seq=0):
    return pl.BlockSpec((1, rows, lanes), lambda s, t: (s + seq, 0, t))


def held(dims):
    return pl.BlockSpec(dims, lambda *_: (0,) * len(dims))


def each(count, body, init, unroll=True):
    return lax.fori_loop(0, count, body, init, unroll=unroll)


def rows_at(index, size):
    return pl.ds(pl.multiple_of(index * size, size), size)


def row_stats(load, channels, chunk, lanes, unroll=True):
    steps = channels // chunk
    zero = jnp.zeros((chunk, lanes), F32)
    total = each(steps, lambda i, t: t + load(i), zero, unroll)
    mean = jnp.sum(total, axis=0, keepdims=True) * (1.0 / channels)

    def square(i, t):
        centred = load(i) - mean
        return t + centred * centred

    squares = each(steps, square, zero, unroll)
    spread = jnp.sum(squares, axis=0, keepdims=True) * (1.0 / channels)
    return mean, lax.rsqrt(spread + EPS)


def back_first(u, normed, gain, shift):
    pre = normed * gain + shift
    sigma = logistic(pre)
    p = u * (sigma * (1.0 + pre * (1.0 - sigma)))
    return pre, sigma, p, p * gain


def first_step():
    return (pl.program_id(0) == 0) & (pl.program_id(1) == 0)


def last_step():
    return (pl.program_id(0) == pl.num_programs(0) - 1) & (
        pl.program_id(1) == pl.num_programs(1) - 1
    )


def cleared(sums):
    @pl.when(first_step())
    def _():
        sums[...] = jnp.zeros_like(sums)


def handed(sums, out):
    @pl.when(last_step())
    def _():
        out[...] = sums[...]


def open_kernel(x, gain, shift, act1, stats, *, chunk):
    lanes, width = x.shape[2], x.shape[1]
    load = lambda i: x[0, rows_at(i, chunk), :].astype(F32)
    mean, scale = row_stats(load, width, chunk, lanes)

    def activate(i, carry):
        at = rows_at(i, chunk)
        normed = (load(i) - mean) * scale
        pre = normed * wide(gain[at, :], lanes) + wide(shift[at, :], lanes)
        act1[0, at, :] = (pre * logistic(pre)).astype(BF16)
        return carry

    each(width // chunk, activate, 0)
    stats[0] = jnp.concatenate([mean, scale, jnp.zeros((6, lanes), F32)], axis=0)


def open_block(x, vectors, lanes=512, chunk=32):
    seqs, width, length = x.shape
    return pl.pallas_call(
        functools.partial(open_kernel, chunk=chunk),
        grid=(seqs, length // lanes),
        in_specs=[here(width, lanes), vector(width, 0), vector(width, 1)],
        out_specs=[here(width, lanes), here(8, lanes)],
        out_shape=[shape(x.shape), shape((seqs, 8, length), F32)],
        compiler_params=params(2),
        cost_estimate=cost(40 * x.size, 4 * x.size),
        name="open_block",
    )(x, vectors, vectors)


def enter_kernel(act1, w_in, gain, shift, act2, turned, normed2, stats, proj, *, chunk):
    lanes, inner = act1.shape[2], act2.shape[1]
    proj[...] = dot(w_in[...], act1[0])
    load = lambda i: proj[rows_at(i, chunk), :]
    mean, scale = row_stats(load, inner, chunk, lanes, 5)

    def activate(i, carry):
        at = rows_at(i, chunk)
        normed = (load(i) - mean) * scale
        normed2[0, at, :] = normed
        pre = normed * wide(gain[at, :], lanes) + wide(shift[at, :], lanes)
        act2[0, at, :] = (pre * logistic(pre)).astype(BF16)
        return carry

    each(inner // chunk, activate, 0, 5)
    turned[0] = act2[0].T
    stats[0] = jnp.concatenate([scale, jnp.zeros((7, lanes), F32)], axis=0)


def enter(act1, w_in_t, vectors, lanes=512, chunk=32):
    seqs, width, length = act1.shape
    inner = w_in_t.shape[0]
    return pl.pallas_call(
        functools.partial(enter_kernel, chunk=chunk),
        grid=(seqs, length // lanes),
        in_specs=[here(width, lanes), held((inner, width)), vector(inner, 6), vector(inner, 7)],
        out_specs=[
            here(inner, lanes),
            pl.BlockSpec((1, lanes, inner), lambda s, t: (s, t, 0)),
            here(inner, lanes),
            here(8, lanes),
        ],
        out_shape=[
            shape((seqs, inner, length)),
            shape((seqs, length, inner)),
            shape((seqs, inner, length), F32),
            shape((seqs, 8, length), F32),
        ],
        scratch_shapes=[pltpu.VMEM((inner, lanes), F32)],
        compiler_params=params(2),
        cost_estimate=cost(2 * act1.size * inner, seqs * length * (2 * width + 8 * inner)),
        name="enter",
    )(act1, w_in_t, vectors, vectors)


def extend(rows, before, after, mask, whole, masked, seq, sign):
    length = rows.shape[1]
    whole[:BORDER, :] = before[seq]
    whole[BORDER : BORDER + length, :] = rows[seq]
    whole[BORDER + length :, :] = after[seq]
    inner = rows.shape[2]
    chunk = 128
    for later in range(KERNEL_TAPS // 2):
        by = sign * (later + 1) * DILATION_STEP

        def body(i, carry, later=later, by=by):
            kept = mask[seq, later, rows_at(i, chunk), :]
            kept = jnp.concatenate([kept] * -(-inner // LANES), axis=1)[:, :inner]
            start = pl.multiple_of(i * chunk + BORDER + by, DILATION_STEP)
            masked[later, rows_at(i, chunk), :] = whole[pl.ds(start, chunk), :] * kept
            return carry

        each(length // chunk, body, 0, 1)


def tap_rows(whole, masked, tap, sign, start, count):
    by = (tap - KERNEL_TAPS // 2) * DILATION_STEP
    if by > 0:
        return masked[tap - KERNEL_TAPS // 2 - 1, pl.ds(start, count), :]
    return whole[pl.ds(start + (BORDER + sign * by), count), :]


def conv_kernel(rows, before, after, mask, w_conv, gain, shift, g, w_out, act3, turned, grads, whole, masked, conv, scaled, low, sums, upstream, *, chunk):
    tile = pl.program_id(1)
    lanes, inner = act3.shape[2], act3.shape[1]
    cleared(sums)

    @pl.when(tile == 0)
    def _():
        extend(rows, before, after, mask, whole, masked, 0, 1)

    start = pl.multiple_of(tile * lanes, lanes)
    total = None
    for tap in range(KERNEL_TAPS):
        part = dot(w_conv[tap], tap_rows(whole, masked, tap, 1, start, lanes), NT)
        total = part if total is None else total + part
    conv[...] = total
    upstream[...] = dot(w_out[...], g[0])
    load = lambda i: conv[rows_at(i, chunk), :]
    mean, scale = row_stats(load, inner, chunk, lanes)

    def first(i, carry):
        at = rows_at(i, chunk)
        normed = (load(i) - mean) * scale
        gains = wide(gain[at, :], lanes)
        pre, sigma, p, q = back_first(upstream[at, :], normed, gains, wide(shift[at, :], lanes))
        act3[0, at, :] = (pre * sigma).astype(BF16)
        conv[at, :] = normed
        scaled[at, :] = q
        sums[0, at, :] += folded(p * normed)
        sums[1, at, :] += folded(p)
        return carry[0] + q, carry[1] + q * normed

    zero = jnp.zeros((chunk, lanes), F32)
    one, two = each(inner // chunk, first, (zero, zero))
    one = jnp.sum(one, axis=0, keepdims=True) * (1.0 / inner)
    two = jnp.sum(two, axis=0, keepdims=True) * (1.0 / inner)

    def second(i, carry):
        at = rows_at(i, chunk)
        low[at, :] = (scale * (scaled[at, :] - one - conv[at, :] * two)).astype(BF16)
        return carry

    each(inner // chunk, second, 0)
    turned[0] = low[...].T
    handed(sums, grads)


def conv_block(rows, before, after, mask, w_conv_t, vectors, g, w_out, lanes=512, chunk=16):
    seqs, length, inner = rows.shape
    seq = lambda *dims: pl.BlockSpec((1, *dims), lambda s, t: (s,) + (0,) * len(dims))
    return pl.pallas_call(
        functools.partial(conv_kernel, chunk=chunk),
        grid=(seqs, length // lanes),
        in_specs=[
            seq(length, inner),
            seq(BORDER, inner),
            seq(BORDER, inner),
            seq(2, length, LANES),
            held(w_conv_t.shape),
            vector(inner, 8),
            vector(inner, 9),
            here(g.shape[1], lanes),
            held(w_out.shape),
        ],
        out_specs=[
            here(inner, lanes),
            pl.BlockSpec((1, lanes, inner), lambda s, t: (s, t, 0)),
            held((2, inner, LANES)),
        ],
        out_shape=[
            shape((seqs, inner, length)),
            shape((seqs, length, inner)),
            shape((2, inner, LANES), F32),
        ],
        scratch_shapes=[
            pltpu.VMEM((length + 2 * BORDER, inner), BF16),
            pltpu.VMEM((KERNEL_TAPS // 2, length, inner), BF16),
            pltpu.VMEM((inner, lanes), F32),
            pltpu.VMEM((inner, lanes), F32),
            pltpu.VMEM((inner, lanes), BF16),
            pltpu.VMEM((2, inner, LANES), F32),
            pltpu.VMEM((inner, lanes), F32),
        ],
        compiler_params=params(2),
        cost_estimate=cost(2 * rows.size * w_conv_t.size // inner, 12 * rows.size),
        name="conv_block",
    )(rows, before, after, mask, w_conv_t, vectors, vectors, g, w_out)


def conv_back_kernel(rows, before, after, mask, w_conv, gain, shift, normed2, stats, *rest, chunk):
    out, grads, whole, masked, grad, scaled, sums = rest[-7:]
    tile = pl.program_id(1)
    lanes, inner = out.shape[2], out.shape[1]
    cleared(sums)

    @pl.when(tile == 0)
    def _():
        extend(rows, before, after, mask, whole, masked, 0, -1)

    start = pl.multiple_of(tile * lanes, lanes)
    total = None
    for tap in range(KERNEL_TAPS):
        part = dot(w_conv[tap], tap_rows(whole, masked, tap, -1, start, lanes), NT)
        total = part if total is None else total + part
    grad[...] = total
    scale = stats[0, 0:1, :]

    def first(i, carry):
        at = rows_at(i, chunk)
        normed = normed2[0, at, :]
        _, _, p, q = back_first(
            grad[at, :], normed, wide(gain[at, :], lanes), wide(shift[at, :], lanes)
        )
        scaled[at, :] = q
        sums[0, at, :] += folded(p * normed)
        sums[1, at, :] += folded(p)
        return carry[0] + q, carry[1] + q * normed

    zero = jnp.zeros((chunk, lanes), F32)
    one, two = each(inner // chunk, first, (zero, zero))
    one = jnp.sum(one, axis=0, keepdims=True) * (1.0 / inner)
    two = jnp.sum(two, axis=0, keepdims=True) * (1.0 / inner)

    def second(i, carry):
        at = rows_at(i, chunk)
        out[0, at, :] = (scale * (scaled[at, :] - one - normed2[0, at, :] * two)).astype(BF16)
        return carry

    each(inner // chunk, second, 0)
    handed(sums, grads)


def conv_back(rows, before, after, mask, w_conv, vectors, normed2, stats, first, count, into=None, lanes=512, chunk=16):
    seqs, length, inner = rows.shape
    seq = lambda *dims: pl.BlockSpec((1, *dims), lambda s, t: (s + first,) + (0,) * len(dims))
    more = () if into is None else (into,)
    return pl.pallas_call(
        functools.partial(conv_back_kernel, chunk=chunk),
        grid=(count, length // lanes),
        in_specs=[
            seq(length, inner),
            seq(BORDER, inner),
            seq(BORDER, inner),
            seq(2, length, LANES),
            held(w_conv.shape),
            vector(inner, 6),
            vector(inner, 7),
            here(inner, lanes, first),
            here(8, lanes, first),
        ]
        + [pl.BlockSpec(memory_space=pl.ANY)] * len(more),
        out_specs=[here(inner, lanes, first), held((2, inner, LANES))],
        input_output_aliases={9: 0} if more else {},
        out_shape=[shape((seqs, inner, length)), shape((2, inner, LANES), F32)],
        scratch_shapes=[
            pltpu.VMEM((length + 2 * BORDER, inner), BF16),
            pltpu.VMEM((KERNEL_TAPS // 2, length, inner), BF16),
            pltpu.VMEM((inner, lanes), F32),
            pltpu.VMEM((inner, lanes), F32),
            pltpu.VMEM((2, inner, LANES), F32),
        ],
        compiler_params=params(2),
        cost_estimate=cost(2 * rows.size * w_conv.size * count // (seqs * inner), 10 * rows.size * count // seqs),
        name="conv_back",
    )(rows, before, after, mask, w_conv, vectors, vectors, normed2, stats, *more)


def leave_kernel(low, w_in, x, g, gain, shift, stats, *rest, chunk):
    out, grads, grad, sums = rest[-4:]
    lanes, width = out.shape[2], out.shape[1]
    cleared(sums)
    grad[...] = dot(w_in[...], low[0])
    mean = stats[0, 0:1, :]
    scale = stats[0, 1:2, :]
    norm = lambda at: (x[0, at, :].astype(F32) - mean) * scale

    def first(i, carry):
        at = rows_at(i, chunk)
        normed = norm(at)
        _, _, p, q = back_first(
            grad[at, :], normed, wide(gain[at, :], lanes), wide(shift[at, :], lanes)
        )
        grad[at, :] = q
        sums[0, at, :] += folded(p * normed)
        sums[1, at, :] += folded(p)
        return carry[0] + q, carry[1] + q * normed

    zero = jnp.zeros((chunk, lanes), F32)
    one, two = each(width // chunk, first, (zero, zero))
    one = jnp.sum(one, axis=0, keepdims=True) * (1.0 / width)
    two = jnp.sum(two, axis=0, keepdims=True) * (1.0 / width)

    slope = scale * scale * two
    level = scale * one - mean * slope

    def second(i, carry):
        at = rows_at(i, chunk)
        branch = (scale * grad[at, :] - level) - x[0, at, :].astype(F32) * slope
        passed = g[0, at, :].astype(F32)
        sums[2, at, :] += folded(passed)
        out[0, at, :] = (passed + branch).astype(BF16)
        return carry

    each(width // chunk, second, 0)
    handed(sums, grads)


def leave(low, w_in, x, g, vectors, stats, first, count, into=None, lanes=256, chunk=16):
    seqs, inner, length = low.shape
    width = x.shape[1]
    more = () if into is None else (into,)
    return pl.pallas_call(
        functools.partial(leave_kernel, chunk=chunk),
        grid=(count, length // lanes),
        in_specs=[
            here(inner, lanes, first),
            held((width, inner)),
            here(width, lanes, first),
            here(width, lanes, first),
            vector(width, 0),
            vector(width, 1),
            here(8, lanes, first),
        ]
        + [pl.BlockSpec(memory_space=pl.ANY)] * len(more),
        input_output_aliases={7: 0} if more else {},
        out_specs=[here(width, lanes, first), held((3, width, LANES))],
        out_shape=[shape(x.shape), shape((3, width, LANES), F32)],
        scratch_shapes=[pltpu.VMEM((width, lanes), F32), pltpu.VMEM((3, width, LANES), F32)],
        compiler_params=params(2),
        cost_estimate=cost(2 * low.size * width * count // seqs, (2 * low.size + 6 * x.size) * count // seqs),
        name="leave",
    )(low, w_in, x, g, vectors, vectors, stats, *more)


def finish_kernel(w_out, act3, x, bias, *rest, chunk):
    out, proj = rest[-2:]
    lanes, width = out.shape[2], out.shape[1]
    proj[...] = dot(w_out[...], act3[0])

    def body(i, carry):
        at = rows_at(i, chunk)
        out[0, at, :] = (x[0, at, :].astype(F32) + proj[at, :] + wide(bias[at, :], lanes)).astype(BF16)
        return carry

    each(width // chunk, body, 0)


def finish(w_out_t, act3, x, vectors, first, count, into=None, lanes=512, chunk=32):
    more = () if into is None else (into,)
    seqs, inner, length = act3.shape
    width = x.shape[1]
    return pl.pallas_call(
        functools.partial(finish_kernel, chunk=chunk),
        grid=(count, length // lanes),
        in_specs=[held((width, inner)), here(inner, lanes, first), here(width, lanes, first), vector(width, 2)]
        + [pl.BlockSpec(memory_space=pl.ANY)] * len(more),
        input_output_aliases={4: 0} if more else {},
        out_specs=here(width, lanes, first),
        out_shape=shape(x.shape),
        scratch_shapes=[pltpu.VMEM((width, lanes), F32)],
        compiler_params=params(2),
        cost_estimate=cost(0, 0),
        name="finish",
    )(w_out_t, act3, x, vectors, *more)


def grads_kernel(at, *refs, pair, taps, keep, units):
    refs = list(refs)
    take = lambda n: [refs.pop(0) for _ in range(n)]
    sources = []
    left = right = act2 = rows3 = before = after = mask = got = None
    if pair:
        left, right = take(2)
    if taps:
        act2, rows3, before, after, mask = take(5)
    if keep:
        (got,) = take(1)
    outs = take(2 if keep else len(units))
    sems = refs.pop(-1)
    loads = []

    def load(source, target):
        copy = pltpu.make_async_copy(source, target, sems.at[len(loads)])
        copy.start()
        loads.append(copy)
        return copy

    if pair:
        left_here, right_here = take(2)
        half = left_here.shape[1]
        columns = right_here.shape[1] // pair
        first, blocks = [], []
        for i in range(pair):
            span = pl.ds(i * columns, columns)
            for seq in range(left_here.shape[0]):
                if i == 0:
                    rows = pl.ds(pl.multiple_of(at[0] * half, half), half)
                    first.append(load(left.at[seq, rows, :], left_here.at[seq]))
                blocks.append(load(right.at[seq, span, :], right_here.at[seq, span, :]))
    if taps:
        act2_here, whole, mask_here, masked = take(4)
        seqs, length = rows3.shape[0], rows3.shape[1]
        half2 = act2_here.shape[1]
        ready = [load(act2.at[:, pl.ds(pl.multiple_of(at[0] * half2, half2), half2), :], act2_here)]
        for seq in range(seqs):
            ready.append(load(rows3.at[seq], whole.at[seq, pl.ds(BORDER, length), :]))
        ready.append(load(before, whole.at[:, pl.ds(0, BORDER), :]))
        ready.append(load(after, whole.at[:, pl.ds(BORDER + length, BORDER), :]))
        ready.append(load(mask, mask_here))
    if keep:
        got_here, total = take(2)
        got_load = load(got, got_here)

    def give(step, value):
        if not keep:
            place = step
            for out, size in zip(outs, units):
                if place < size:
                    out[place] = value.astype(BF16)
                    return
                place -= size
        if step == 0:
            got_load.wait()
        total[...] = value + got_here[step].astype(F32)
        rows = outs[0].shape[1]
        for place, out in enumerate(outs):
            start = pl.multiple_of((at[1] ^ place) * rows, 8)
            out[step] = total[pl.ds(start, rows), :].astype(BF16)

    for i in range(pair):
        value = None
        for seq in range(left_here.shape[0]):
            if i == 0:
                first[seq].wait()
            blocks[i * left_here.shape[0] + seq].wait()
            part = dot(left_here[seq], right_here[seq, i * columns : (i + 1) * columns, :], NT)
            value = part if value is None else value + part
        give(i, value)
    for step, tap in enumerate(taps):
        by = (tap - KERNEL_TAPS // 2) * DILATION_STEP
        if step == 0:
            for copy in ready:
                copy.wait()
        value = None
        for seq in range(seqs):
            if by > 0:
                mask_rows(whole.at[seq], mask_here, masked, seq, by)
                rows = masked[...]
            else:
                rows = whole[seq, BORDER - by : BORDER - by + length, :]
            part = dot(act2_here[seq], rows)
            value = part if value is None else value + part
        give(pair + step, value)


def tap_grads_kernel(left, rows3, before, after, mask, out, left_here, whole, mask_here, masked, total, done, sems):
    seqs, length = rows3.shape[0], rows3.shape[1]
    count, size = out.shape[0], left.shape[1] // out.shape[0]

    def copy(place, source, target):
        moving = pltpu.make_async_copy(source, target, sems.at[place])
        moving.start()
        return moving

    loads = [copy(0, before, whole.at[:, pl.ds(0, BORDER), :])]
    loads.append(copy(1, after, whole.at[:, pl.ds(BORDER + length, BORDER), :]))
    for seq in range(seqs):
        loads.append(copy(2 + 2 * seq, rows3.at[seq], whole.at[seq, pl.ds(BORDER, length), :]))
        loads.append(copy(3 + 2 * seq, left.at[seq], left_here.at[seq]))
    loads.append(copy(2 + 2 * seqs, mask, mask_here))
    stores = []
    for tap in range(KERNEL_TAPS):
        by = (tap - KERNEL_TAPS // 2) * DILATION_STEP
        value = None
        for seq in range(seqs):
            if tap == 0:
                for load in loads[: 4 if seq == 0 else 2]:
                    load.wait()
                loads = loads[4 if seq == 0 else 2 :]
            if by > 0:
                for load in loads:
                    load.wait()
                loads = []
                mask_rows(whole.at[seq], mask_here, masked, seq, by)
                rows = masked[...]
            else:
                rows = whole[seq, BORDER - by : BORDER - by + length, :]
            part = dot(left_here[seq], rows)
            value = part if value is None else value + part
        total[tap % 2] = value
        last = tap == KERNEL_TAPS - 1
        if tap % 2 == 0 and not last:
            continue
        start = tap // 2 * 2 * size
        height = out.shape[1] - start if last else 2 * size
        fill = jnp.zeros((height - size, total.shape[2]), F32)
        for shard in range(count):
            span = slice(shard * size, (shard + 1) * size)
            below = fill if last else total[1, span, :]
            done[tap // 2, shard, :height, :] = jnp.concatenate([total[0, span, :], below], axis=0).astype(BF16)
            place = 3 + 2 * seqs + tap // 2 * count + shard
            stores.append(copy(place, done.at[tap // 2, shard, pl.ds(0, height), :], out.at[shard, pl.ds(start, height), :]))
    for store in stores:
        store.wait()


def tap_grads(count, padded, left, rows3, before, after, mask):
    seqs, length, inner = rows3.shape
    steps = -(-KERNEL_TAPS // 2)
    operands = (left, rows3, before, after, mask)
    return pl.pallas_call(
        tap_grads_kernel,
        in_specs=[pl.BlockSpec(memory_space=pl.ANY)] * len(operands),
        out_specs=pl.BlockSpec(memory_space=pl.ANY),
        out_shape=shape((count, padded, inner)),
        scratch_shapes=[
            pltpu.VMEM(left.shape, BF16),
            pltpu.VMEM((seqs, length + 2 * BORDER, inner), BF16),
            pltpu.VMEM(mask.shape, BF16),
            pltpu.VMEM((length, inner), BF16),
            pltpu.VMEM((2, inner, inner), F32),
            pltpu.VMEM((steps, count, 2 * inner // count, inner), BF16),
            pltpu.SemaphoreType.DMA((3 + 2 * seqs + steps * count,)),
        ],
        compiler_params=params(),
        cost_estimate=cost(2 * KERNEL_TAPS * left.size * inner, 4 * left.size + 10 * inner * inner),
        name="tap_grads",
    )(*operands)


def mask_rows(whole, mask, masked, seq, by):
    length, inner = masked.shape
    chunk = 128

    def body(i, carry):
        kept = mask[seq, by // DILATION_STEP - 1, rows_at(i, chunk), :]
        kept = jnp.concatenate([kept] * -(-inner // LANES), axis=1)[:, :inner]
        start = pl.multiple_of(i * chunk + BORDER - by, DILATION_STEP)
        masked[rows_at(i, chunk), :] = whole[pl.ds(start, chunk), :] * kept
        return carry

    each(length // chunk, body, 0, 1)


def grads(at, columns, pair=None, taps=(), conv=(), got=None, units=None):
    operands, scratch = [], []
    count, flops, copies = 0, 0, 0
    if pair is not None:
        left, right = pair
        half = left.shape[1] // 2
        count = right.shape[1] // columns
        operands += [left, right]
        scratch += [pltpu.VMEM((left.shape[0], half, left.shape[2]), BF16), pltpu.VMEM(right.shape, BF16)]
        copies += left.shape[0] * (1 + count)
        flops += left.size * right.shape[1]
    if taps:
        act2, rows3, _, _, mask = conv
        seqs, length, inner = rows3.shape
        half = inner // 2
        operands += conv
        scratch += [
            pltpu.VMEM((seqs, half, length), BF16),
            pltpu.VMEM((seqs, length + 2 * BORDER, inner), BF16),
            pltpu.VMEM(mask.shape, BF16),
            pltpu.VMEM((length, inner), BF16),
        ]
        copies += 4 + seqs
        flops += act2.size * inner * len(taps)
    total = count + len(taps)
    if got is None:
        units = units or (total,)
        dims = [(size, half, columns) for size in units]
    else:
        operands.append(got)
        scratch += [pltpu.VMEM(got.shape, BF16), pltpu.VMEM((half, columns), F32)]
        copies += 1
        dims = [(total, half // 2, columns)] * 2
    scratch.append(pltpu.SemaphoreType.DMA((copies,)))
    return pl.pallas_call(
        functools.partial(grads_kernel, pair=count, taps=taps, keep=got is not None, units=units),
        grid_spec=pltpu.PrefetchScalarGridSpec(
            num_scalar_prefetch=1,
            grid=(1,),
            in_specs=[pl.BlockSpec(memory_space=pl.ANY)] * len(operands),
            out_specs=[held(d) for d in dims],
            scratch_shapes=scratch,
        ),
        out_shape=[shape(d) for d in dims],
        compiler_params=params(1),
        cost_estimate=cost(flops, 2 * sum(o.size for o in operands)),
        name="grads",
    )(at, *operands)


def flip_kernel(w, out):
    for tap in range(w.shape[0]):
        out[tap] = w[tap].T


def flip(w):
    taps, rows, columns = w.shape
    return pl.pallas_call(
        flip_kernel,
        out_shape=shape((taps, columns, rows)),
        compiler_params=params(),
        cost_estimate=cost(0, 4 * w.size),
        name="flip",
    )(w)


def assemble_kernel(at, own, mine, other, natural, *rest):
    whole = rest[-1]
    rows, half = own.shape[0], mine.shape[1]
    whole[pl.ds(pl.multiple_of(at[0] * rows, 8), rows), :] = own[...].astype(F32)
    for step in range(mine.shape[0]):
        for pieces, core in ((mine, at[1]), (other, 1 - at[1])):
            start = (at[0] ^ (step + 1)) * rows + core * (rows - half)
            whole[pl.ds(pl.multiple_of(start, 8), half), :] = pieces[step].astype(F32)
    natural[...] = whole[...].astype(BF16)
    if len(rest) == 2:
        rest[0][...] = natural[...].T


def assemble(at, own, mine, other, turned=True):
    rows, columns = own.shape
    full = rows * (mine.shape[0] + 1)
    dims = [(full, columns), (columns, full)][: 1 + turned]
    return pl.pallas_call(
        assemble_kernel,
        grid_spec=pltpu.PrefetchScalarGridSpec(
            num_scalar_prefetch=1,
            grid=(1,),
            in_specs=[held(own.shape), held(mine.shape), held(other.shape)],
            out_specs=[held(d) for d in dims],
            scratch_shapes=[pltpu.VMEM((full, columns), F32)],
        ),
        out_shape=[shape(d) for d in dims],
        compiler_params=params(1),
        cost_estimate=cost(0, 6 * full * columns),
        name="assemble",
    )(at, own, mine, other)


def join_kernel(pieces, natural, turned, whole, *, rows):
    count, half = pieces.shape[0], pieces.shape[3]
    for shard in range(count):
        for core in range(2):
            start = shard * rows + core * (rows - half)
            whole[start : start + half, :] = pieces[shard, core, 0].astype(F32)
    natural[0] = whole[...].astype(BF16)
    turned[0] = natural[0].T


def join(pieces, rows):
    count, cores, taps, half, columns = pieces.shape
    full = count * rows
    dims = [(taps, full, columns), (taps, columns, full)]
    return pl.pallas_call(
        functools.partial(join_kernel, rows=rows),
        grid=(taps,),
        in_specs=[pl.BlockSpec((count, cores, 1, half, columns), lambda t: (0, 0, t, 0, 0))],
        out_specs=[pl.BlockSpec((1, *d[1:]), lambda t: (t, 0, 0)) for d in dims],
        out_shape=[shape(d) for d in dims],
        scratch_shapes=[pltpu.VMEM((full, columns), F32)],
        compiler_params=params(1),
        cost_estimate=cost(0, 6 * taps * full * columns),
        name="join",
    )(pieces)


def spread_kernel(at, parts, out, rows, *, sizes):
    count = parts.shape[0]
    for i in range(count):
        rows[pl.ds(at[0] ^ i, 1), :] = parts[i : i + 1, :]
    start, base = 0, 0
    for size in sizes:
        for shard in range(count):
            row = rows[shard : shard + 1, start : start + size]
            out[base : base + size, :] = jnp.broadcast_to(row, (LANES, size)).T
            base += size
        start += size


def spread(at, parts, sizes):
    total = parts.size
    return pl.pallas_call(
        functools.partial(spread_kernel, sizes=sizes),
        grid_spec=pltpu.PrefetchScalarGridSpec(
            num_scalar_prefetch=1,
            grid=(1,),
            in_specs=[held(parts.shape)],
            out_specs=held((total, LANES)),
            scratch_shapes=[pltpu.VMEM(parts.shape, F32)],
        ),
        out_shape=shape((total, LANES), F32),
        compiler_params=params(1),
        cost_estimate=cost(0, 4 * LANES * total),
        name="spread",
    )(at, parts)


def after(value, *others):
    return lax.optimization_barrier((value, *others))[0] if others else value


def swapped(x):
    return lax.ppermute(x, "core", [(0, 1), (1, 0)])


def from_ws(x, bit):
    return lax.ppermute(x, "ws", [(i, i ^ bit) for i in range(lax.axis_size("ws"))])


def neighbours(first, last):
    runs = lax.axis_size("run") * 2
    up = [(i, i + 1) for i in range(runs - 1)]
    down = [(i + 1, i) for i in range(runs - 1)]
    return lax.ppermute(last, ("run", "core"), up), lax.ppermute(first, ("run", "core"), down)


def square():
    return lax.axis_size("ws") == 4 and lax.axis_size("run") == 4


def halved(rows):
    return -(-rows // 16) * 8


def fetched(shard):
    rows = shard.shape[0]
    half = halved(rows)
    own = lax.dynamic_slice_in_dim(shard, lax.axis_index("core") * (rows - half), half, axis=0)
    return [from_ws(own, bit) for bit in (1, 2, 3)]


def whole_weight(at, shard, pieces, turned=True):
    if pieces is None:
        natural = lax.all_gather(shard, "ws", axis=0, tiled=True)
        return [natural, flip(natural[None])[0]][: 1 + turned]
    mine = jnp.stack(pieces)
    return assemble(at, shard, mine, swapped(mine), turned)


def halves_of(shard, *others):
    taps, rows, columns = shard.shape
    half = halved(rows)
    own = lax.dynamic_slice_in_dim(shard, lax.axis_index("core") * (rows - half), half, axis=1)
    pieces = lax.all_gather(after(own, *others), ("ws", "core"), axis=0)
    return pieces.reshape(-1, 2, taps, half, columns)


def summed(*terms):
    total = terms[0].astype(F32)
    for term in terms[1:]:
        total = total + term.astype(F32)
    return total.astype(BF16)


def active(shard):
    return shard >> 1


class Share:
    def __init__(self, first, second):
        self.dims = first.shape
        rows = lambda x: x.reshape(-1, x.shape[-1])
        self.sum, self.second = rows(first), rows(second)

    def land(self, *kernels):
        self.sum = summed(self.sum, *after(self.came, *kernels))
        return self.sum

    def spread(self):
        near = [(2 * i + active(i), 2 * (i ^ 1) + active(i)) for i in range(4)]
        far = lambda bit: [(2 * i + 1 - active(i), 2 * (i ^ bit) + 1 - active(i)) for i in range(4)]
        move = lambda x, pairs: lax.ppermute(x, ("ws", "core"), pairs)
        self.came = (move(self.second, near), move(self.sum, far(2)), move(self.second, far(3)))

    def along(self, x, bits):
        every = []
        for shard in range(4):
            every += [((shard * 4 + i) * 2 + active(shard), (shard * 4 + (i ^ bits)) * 2 + active(shard)) for i in range(4)]
        self.came = (lax.ppermute(x, ("ws", "run", "core"), every),)

    def inward(self):
        self.along(self.sum, 1)

    def middle(self):
        self.along(self.sum, 3)

    def both(self):
        shard, core = lax.axis_index("ws"), lax.axis_index("core")
        pairs = [(2 * i + active(i), 2 * i + 1 - active(i)) for i in range(4)]
        other = lax.ppermute(self.sum, ("ws", "core"), pairs)
        return jnp.where(core == active(shard), self.sum, other).astype(F32).reshape(self.dims)


def plain(low, high, axis):
    whole = jnp.concatenate([low, high], axis=axis)
    owned = lax.psum_scatter(whole, "ws", scatter_dimension=axis, tiled=True)
    return lax.psum(owned, ("run", "core")).astype(F32)


class Small:
    def __init__(self, mine):
        self.sum = mine

    def send(self, axis, bit):
        self.came = lax.ppermute(self.sum, axis, [(i, i ^ bit) for i in range(lax.axis_size(axis))])

    def land(self, *kernels):
        self.sum = self.sum + after(self.came, *kernels)


def totals_of(count, sums1, sums2, sums3):
    every = (sums1[0], sums1[1], sums1[2], sums2[0], sums2[1], sums3[0], sums3[1])
    return jnp.concatenate([s.sum(axis=-1).reshape(count, -1) for s in every], axis=1)


def shards(
    inputs,
    cotangent,
    block_ids,
    first_gain,
    first_shift,
    weight_in,
    second_gain,
    second_shift,
    weight_conv,
    third_gain,
    third_shift,
    weight_out,
    output_bias,
):
    x = inputs.transpose(0, 2, 1)
    g = cotangent.transpose(0, 2, 1)
    count, shard, core = lax.axis_size("ws"), lax.axis_index("ws"), lax.axis_index("core")
    easy = square()
    place = jnp.stack([shard, core])
    owned_vectors = (first_gain, first_shift, output_bias, second_gain, second_shift, third_gain, third_shift)
    sizes = tuple(own.size for own in owned_vectors)
    flat = jnp.concatenate(owned_vectors)
    if easy:
        parts = jnp.stack([flat, *[from_ws(flat, bit) for bit in (1, 2, 3)]]).astype(F32)
        vectors = spread(place, parts, sizes)
    else:
        parts = lax.all_gather(flat, "ws", axis=0).astype(F32)
        vectors = spread(jnp.zeros_like(place), parts, sizes)
    in_pieces = fetched(after(weight_in, parts)) if easy else None
    conv_halves = halves_of(weight_conv) if easy else None
    act1, stats1 = open_block(x, vectors)
    length = block_ids.shape[1]
    ids_before, ids_after = neighbours(block_ids[:, :BORDER], block_ids[:, -BORDER:])
    ids = jnp.concatenate([ids_before, block_ids, ids_after], axis=1)
    same = lambda by: ids[:, BORDER + by : BORDER + by + length] == block_ids
    steps = [DILATION_STEP * (i + 1) for i in range(KERNEL_TAPS // 2)]

    def masks(sign):
        both = jnp.stack([same(sign * by) for by in steps], axis=1)
        return jnp.broadcast_to(both[..., None], (*both.shape, LANES)).astype(BF16)

    mask, mask_back = masks(1), masks(-1)
    if easy:
        mask, mask_back = after((mask, mask_back), act1)
    if easy:
        in_pieces = after(in_pieces, act1, mask, mask_back)
        out_pieces = fetched(after(weight_out, *in_pieces))
    else:
        out_pieces = None
    w_in, w_in_t = whole_weight(place, weight_in, in_pieces)
    act2, rows2, normed2, stats2 = enter(act1, w_in_t, vectors)
    halo2 = neighbours(rows2[:, :BORDER], rows2[:, -BORDER:])
    if easy:
        out_pieces = after(out_pieces, act2)
    (w_out,) = whole_weight(place, weight_out, out_pieces, False)
    if easy:
        w_conv, w_conv_t = join(after(conv_halves, w_out), weight_conv.shape[1])
    else:
        w_conv = lax.all_gather(weight_conv, "ws", axis=1, tiled=True)
        w_conv_t = flip(w_conv)
    halo2 = after(halo2, w_conv_t)
    act3, rows3, sums3 = conv_block(rows2, *halo2, mask, w_conv_t, vectors, g, w_out)
    halo = neighbours(rows3[:, :BORDER], rows3[:, -BORDER:])
    bit = shard & 1
    give, keep = jnp.stack([1 - core, bit]), jnp.stack([core, bit])
    if not easy:
        give, keep = jnp.zeros_like(give), jnp.ones_like(keep)
    seqs = x.shape[0]
    back = lambda rows, seq, number, into: conv_back(
        rows, *halo, mask_back, w_conv, vectors, normed2, stats2, seq, number, into
    )
    close = lambda low, seq, number, into: leave(low, w_in, x, g, vectors, stats1, seq, number, into)
    width, inner = x.shape[1], act2.shape[1]
    if not easy:
        conv = (act2, rows3, *halo, mask_back)
        halves = lambda **kw: [grads(at, inner, **kw)[0] for at in (give, keep)]
        out_grad = plain(*halves(pair=(act3, g)), 1)
        out_grad = out_grad.transpose(1, 0, 2).reshape(-1, width)
        conv_grad = plain(*halves(taps=tuple(range(KERNEL_TAPS)), conv=conv), 1)
        low2, sums2 = back(rows3, 0, seqs, None)
        in_grad = plain(*halves(pair=(act1, low2)), 1)[0]
        input_grad, sums1 = close(low2, 0, seqs, None)
        block_output = finish(flip(w_out[None])[0], act3, x, vectors, 0, seqs)
    else:
        shard_rows = inner // count
        padded = -(-KERNEL_TAPS * shard_rows // LANES) * LANES
        taps = tap_grads(count, padded, act2, rows3, *halo, mask_back)
        (out_send,) = grads(give, inner, pair=(after(act3, taps), g))
        got_out = swapped(out_send)
        taps = lax.psum_scatter(taps.reshape(-1, inner), "ws", scatter_dimension=0, tiled=True)
        out = Share(*grads(keep, inner, pair=(act3, g), got=got_out))
        out.spread()
        low2, sums2 = back(after(rows3, out.sum), 0, seqs, None)
        out.land(low2)
        out.inward()
        (in_send,) = grads(give, inner, pair=(act1, after(low2, out.sum)))
        got_in = swapped(in_send)
        out.land(in_send)
        out.middle()
        got_in = after(got_in, out.sum)
        both = Share(*grads(keep, inner, pair=(act1, low2), got=got_in))
        both.spread()
        out.land(both.sum)
        rows = out.both()
        w_out_t = flip(after(w_out, both.sum)[None])[0]
        low2, taps = after((low2, taps), both.sum, out.sum, w_out_t)
        taps = lax.psum_scatter(taps, ("run", "core"), scatter_dimension=0, tiled=True)
        input_grad, sums1 = close(low2, 0, seqs, None)
        small = Small(totals_of(count, sums1, sums2, sums3))
        small.send("core", 1)
        both.land(sums1)
        both.inward()
        small.land(both.sum)
        small.send("ws", 1)
        (w_out_t, act3), taps = after(((w_out_t, act3), taps), both.sum, small.sum, rows)
        taps_sum = lax.all_gather(taps, ("run", "core"), axis=0, tiled=True)
        block_output = finish(w_out_t, act3, x, vectors, 0, seqs)
        small.land(block_output)
        both.land(block_output, small.sum)
        small.send("ws", 2)
        both.middle()
        small.land(both.sum)
        small.send("run", 1)
        small.land()
        small.send("run", 2)
        small.land()
        taps = taps_sum[: KERNEL_TAPS * shard_rows].astype(F32)
        conv_grad = taps.reshape(KERNEL_TAPS, shard_rows, inner)
        out_grad = jnp.concatenate([rows[0], rows[1]], axis=1)
        both.land(small.sum, conv_grad, out_grad)
        in_grad = both.both().reshape(-1, inner)
        small = small.sum

    if not easy:
        small = lax.psum(totals_of(count, sums1, sums2, sums3), ("ws", "run", "core"))
    small = lax.dynamic_index_in_dim(small, shard, axis=0, keepdims=False)
    at, vector_grads = 0, []
    for size in sizes:
        vector_grads.append(small[at : at + size])
        at += size
    gain1, shift1, bias, gain2, shift2, gain3, shift3 = vector_grads
    return (
        block_output.transpose(0, 2, 1),
        input_grad.transpose(0, 2, 1),
        gain1,
        shift1,
        in_grad,
        gain2,
        shift2,
        conv_grad,
        gain3,
        shift3,
        out_grad,
        bias,
    )


def solution(mesh):
    count, runs = mesh.devices.shape
    split = jax.sharding.Mesh(mesh.devices.reshape(count, runs // 2, 2), ("ws", "run", "core"))
    tokens = P("ws", ("run", "core"), None)
    rows = P("ws", None)
    taps = P(None, "ws", None)
    placed = (tokens, tokens, P("ws", ("run", "core")), P("ws"), P("ws"), rows, P("ws"), P("ws"), taps)
    placed += (P("ws"), P("ws"), rows, P("ws"))
    given = (tokens, tokens, P("ws"), P("ws"), rows, P("ws"), P("ws"), taps, P("ws"), P("ws"), rows, P("ws"))
    return jax.shard_map(shards, mesh=split, in_specs=placed, out_specs=given, check_vma=False)
```

```python
import functools
import jax
import jax.numpy as jnp
from jax import lax
from jax.experimental import pallas as pl
from jax.experimental.pallas import tpu as pltpu
from jax.sharding import PartitionSpec as P

KERNEL_TAPS = 5
DILATION_STEP = 16
EPS = 1e-05
LANES = 128
BORDER = KERNEL_TAPS // 2 * DILATION_STEP
F32 = jnp.float32
BF16 = jnp.bfloat16
VMEM_BYTES = 60 * 2**20

NN = (((1,), (0,)), ((), ()))
NT = (((1,), (1,)), ((), ()))


def params(steps=0):
    return pltpu.CompilerParams(
        dimension_semantics=("arbitrary",) * steps or None, vmem_limit_bytes=VMEM_BYTES
    )


def cost(flops, bytes_accessed):
    return pl.CostEstimate(flops=flops // 16, bytes_accessed=bytes_accessed // 16, transcendentals=0)


def shape(dims, dtype=BF16):
    return jax.ShapeDtypeStruct(dims, dtype)


def dot(left, right, dims=NN):
    return lax.dot_general(left, right, dims, preferred_element_type=F32)


def wide(column, lanes):
    return jnp.concatenate([column] * (lanes // LANES), axis=1)


def folded(values):
    total = values[:, :LANES]
    for at in range(LANES, values.shape[1], LANES):
        total = total + values[:, at : at + LANES]
    return total


def logistic(x):
    return 0.5 * jnp.tanh(0.5 * x) + 0.5


def vector(rows, block):
    return pl.BlockSpec((rows, LANES), lambda *_: (block, 0))


def here(rows, lanes, seq=0):
    return pl.BlockSpec((1, rows, lanes), lambda s, t: (s + seq, 0, t))


def held(dims):
    return pl.BlockSpec(dims, lambda *_: (0,) * len(dims))


def each(count, body, init, unroll=True):
    return lax.fori_loop(0, count, body, init, unroll=unroll)


def rows_at(index, size):
    return pl.ds(pl.multiple_of(index * size, size), size)


def row_stats(load, channels, chunk, lanes, unroll=True):
    steps = channels // chunk
    zero = jnp.zeros((chunk, lanes), F32)
    total = each(steps, lambda i, t: t + load(i), zero, unroll)
    mean = jnp.sum(total, axis=0, keepdims=True) * (1.0 / channels)

    def square(i, t):
        centred = load(i) - mean
        return t + centred * centred

    squares = each(steps, square, zero, unroll)
    spread = jnp.sum(squares, axis=0, keepdims=True) * (1.0 / channels)
    return mean, lax.rsqrt(spread + EPS)


def back_first(u, normed, gain, shift):
    pre = normed * gain + shift
    sigma = logistic(pre)
    p = u * (sigma * (1.0 + pre * (1.0 - sigma)))
    return pre, sigma, p, p * gain


def first_step():
    return (pl.program_id(0) == 0) & (pl.program_id(1) == 0)


def last_step():
    return (pl.program_id(0) == pl.num_programs(0) - 1) & (
        pl.program_id(1) == pl.num_programs(1) - 1
    )


def cleared(sums):
    @pl.when(first_step())
    def _():
        sums[...] = jnp.zeros_like(sums)


def handed(sums, out):
    @pl.when(last_step())
    def _():
        out[...] = sums[...]


def open_kernel(x, gain, shift, act1, stats, *, chunk):
    lanes, width = x.shape[2], x.shape[1]
    load = lambda i: x[0, rows_at(i, chunk), :].astype(F32)
    mean, scale = row_stats(load, width, chunk, lanes)

    def activate(i, carry):
        at = rows_at(i, chunk)
        normed = (load(i) - mean) * scale
        pre = normed * wide(gain[at, :], lanes) + wide(shift[at, :], lanes)
        act1[0, at, :] = (pre * logistic(pre)).astype(BF16)
        return carry

    each(width // chunk, activate, 0)
    stats[0] = jnp.concatenate([mean, scale, jnp.zeros((6, lanes), F32)], axis=0)


def open_block(x, vectors, lanes=512, chunk=32):
    seqs, width, length = x.shape
    return pl.pallas_call(
        functools.partial(open_kernel, chunk=chunk),
        grid=(seqs, length // lanes),
        in_specs=[here(width, lanes), vector(width, 0), vector(width, 1)],
        out_specs=[here(width, lanes), here(8, lanes)],
        out_shape=[shape(x.shape), shape((seqs, 8, length), F32)],
        compiler_params=params(2),
        cost_estimate=cost(40 * x.size, 4 * x.size),
        name="open_block",
    )(x, vectors, vectors)


def enter_kernel(act1, w_in, gain, shift, act2, turned, normed2, stats, proj, *, chunk):
    lanes, inner = act1.shape[2], act2.shape[1]
    proj[...] = dot(w_in[...], act1[0])
    load = lambda i: proj[rows_at(i, chunk), :]
    mean, scale = row_stats(load, inner, chunk, lanes, 5)

    def activate(i, carry):
        at = rows_at(i, chunk)
        normed = (load(i) - mean) * scale
        normed2[0, at, :] = normed
        pre = normed * wide(gain[at, :], lanes) + wide(shift[at, :], lanes)
        act2[0, at, :] = (pre * logistic(pre)).astype(BF16)
        return carry

    each(inner // chunk, activate, 0, 5)
    turned[0] = act2[0].T
    stats[0] = jnp.concatenate([scale, jnp.zeros((7, lanes), F32)], axis=0)


def enter(act1, w_in_t, vectors, lanes=512, chunk=32):
    seqs, width, length = act1.shape
    inner = w_in_t.shape[0]
    return pl.pallas_call(
        functools.partial(enter_kernel, chunk=chunk),
        grid=(seqs, length // lanes),
        in_specs=[here(width, lanes), held((inner, width)), vector(inner, 6), vector(inner, 7)],
        out_specs=[
            here(inner, lanes),
            pl.BlockSpec((1, lanes, inner), lambda s, t: (s, t, 0)),
            here(inner, lanes),
            here(8, lanes),
        ],
        out_shape=[
            shape((seqs, inner, length)),
            shape((seqs, length, inner)),
            shape((seqs, inner, length), F32),
            shape((seqs, 8, length), F32),
        ],
        scratch_shapes=[pltpu.VMEM((inner, lanes), F32)],
        compiler_params=params(2),
        cost_estimate=cost(2 * act1.size * inner, seqs * length * (2 * width + 8 * inner)),
        name="enter",
    )(act1, w_in_t, vectors, vectors)


def extend(rows, before, after, mask, whole, masked, seq, sign):
    length = rows.shape[1]
    whole[:BORDER, :] = before[seq]
    whole[BORDER : BORDER + length, :] = rows[seq]
    whole[BORDER + length :, :] = after[seq]
    inner = rows.shape[2]
    chunk = 128
    for later in range(KERNEL_TAPS // 2):
        by = sign * (later + 1) * DILATION_STEP

        def body(i, carry, later=later, by=by):
            kept = mask[seq, later, rows_at(i, chunk), :]
            kept = jnp.concatenate([kept] * -(-inner // LANES), axis=1)[:, :inner]
            start = pl.multiple_of(i * chunk + BORDER + by, DILATION_STEP)
            masked[later, rows_at(i, chunk), :] = whole[pl.ds(start, chunk), :] * kept
            return carry

        each(length // chunk, body, 0, 1)


def tap_rows(whole, masked, tap, sign, start, count):
    by = (tap - KERNEL_TAPS // 2) * DILATION_STEP
    if by > 0:
        return masked[tap - KERNEL_TAPS // 2 - 1, pl.ds(start, count), :]
    return whole[pl.ds(start + (BORDER + sign * by), count), :]


def conv_kernel(rows, before, after, mask, w_conv, gain, shift, g, w_out, act3, turned, grads, whole, masked, conv, scaled, low, sums, upstream, *, chunk):
    tile = pl.program_id(1)
    lanes, inner = act3.shape[2], act3.shape[1]
    cleared(sums)

    @pl.when(tile == 0)
    def _():
        extend(rows, before, after, mask, whole, masked, 0, 1)

    start = pl.multiple_of(tile * lanes, lanes)
    total = None
    for tap in range(KERNEL_TAPS):
        part = dot(w_conv[tap], tap_rows(whole, masked, tap, 1, start, lanes), NT)
        total = part if total is None else total + part
    conv[...] = total
    upstream[...] = dot(w_out[...], g[0])
    load = lambda i: conv[rows_at(i, chunk), :]
    mean, scale = row_stats(load, inner, chunk, lanes)

    def first(i, carry):
        at = rows_at(i, chunk)
        normed = (load(i) - mean) * scale
        gains = wide(gain[at, :], lanes)
        pre, sigma, p, q = back_first(upstream[at, :], normed, gains, wide(shift[at, :], lanes))
        act3[0, at, :] = (pre * sigma).astype(BF16)
        conv[at, :] = normed
        scaled[at, :] = q
        sums[0, at, :] += folded(p * normed)
        sums[1, at, :] += folded(p)
        return carry[0] + q, carry[1] + q * normed

    zero = jnp.zeros((chunk, lanes), F32)
    one, two = each(inner // chunk, first, (zero, zero))
    one = jnp.sum(one, axis=0, keepdims=True) * (1.0 / inner)
    two = jnp.sum(two, axis=0, keepdims=True) * (1.0 / inner)

    def second(i, carry):
        at = rows_at(i, chunk)
        low[at, :] = (scale * (scaled[at, :] - one - conv[at, :] * two)).astype(BF16)
        return carry

    each(inner // chunk, second, 0)
    turned[0] = low[...].T
    handed(sums, grads)


def conv_block(rows, before, after, mask, w_conv_t, vectors, g, w_out, lanes=512, chunk=16):
    seqs, length, inner = rows.shape
    seq = lambda *dims: pl.BlockSpec((1, *dims), lambda s, t: (s,) + (0,) * len(dims))
    return pl.pallas_call(
        functools.partial(conv_kernel, chunk=chunk),
        grid=(seqs, length // lanes),
        in_specs=[
            seq(length, inner),
            seq(BORDER, inner),
            seq(BORDER, inner),
            seq(2, length, LANES),
            held(w_conv_t.shape),
            vector(inner, 8),
            vector(inner, 9),
            here(g.shape[1], lanes),
            held(w_out.shape),
        ],
        out_specs=[
            here(inner, lanes),
            pl.BlockSpec((1, lanes, inner), lambda s, t: (s, t, 0)),
            held((2, inner, LANES)),
        ],
        out_shape=[
            shape((seqs, inner, length)),
            shape((seqs, length, inner)),
            shape((2, inner, LANES), F32),
        ],
        scratch_shapes=[
            pltpu.VMEM((length + 2 * BORDER, inner), BF16),
            pltpu.VMEM((KERNEL_TAPS // 2, length, inner), BF16),
            pltpu.VMEM((inner, lanes), F32),
            pltpu.VMEM((inner, lanes), F32),
            pltpu.VMEM((inner, lanes), BF16),
            pltpu.VMEM((2, inner, LANES), F32),
            pltpu.VMEM((inner, lanes), F32),
        ],
        compiler_params=params(2),
        cost_estimate=cost(2 * rows.size * w_conv_t.size // inner, 12 * rows.size),
        name="conv_block",
    )(rows, before, after, mask, w_conv_t, vectors, vectors, g, w_out)


def conv_back_kernel(rows, before, after, mask, w_conv, gain, shift, normed2, stats, *rest, chunk):
    out, grads, whole, masked, grad, scaled, sums = rest[-7:]
    tile = pl.program_id(1)
    lanes, inner = out.shape[2], out.shape[1]
    cleared(sums)

    @pl.when(tile == 0)
    def _():
        extend(rows, before, after, mask, whole, masked, 0, -1)

    start = pl.multiple_of(tile * lanes, lanes)
    total = None
    for tap in range(KERNEL_TAPS):
        part = dot(w_conv[tap], tap_rows(whole, masked, tap, -1, start, lanes), NT)
        total = part if total is None else total + part
    grad[...] = total
    scale = stats[0, 0:1, :]

    def first(i, carry):
        at = rows_at(i, chunk)
        normed = normed2[0, at, :]
        _, _, p, q = back_first(
            grad[at, :], normed, wide(gain[at, :], lanes), wide(shift[at, :], lanes)
        )
        scaled[at, :] = q
        sums[0, at, :] += folded(p * normed)
        sums[1, at, :] += folded(p)
        return carry[0] + q, carry[1] + q * normed

    zero = jnp.zeros((chunk, lanes), F32)
    one, two = each(inner // chunk, first, (zero, zero))
    one = jnp.sum(one, axis=0, keepdims=True) * (1.0 / inner)
    two = jnp.sum(two, axis=0, keepdims=True) * (1.0 / inner)

    def second(i, carry):
        at = rows_at(i, chunk)
        out[0, at, :] = (scale * (scaled[at, :] - one - normed2[0, at, :] * two)).astype(BF16)
        return carry

    each(inner // chunk, second, 0)
    handed(sums, grads)


def conv_back(rows, before, after, mask, w_conv, vectors, normed2, stats, first, count, into=None, lanes=512, chunk=16):
    seqs, length, inner = rows.shape
    seq = lambda *dims: pl.BlockSpec((1, *dims), lambda s, t: (s + first,) + (0,) * len(dims))
    more = () if into is None else (into,)
    return pl.pallas_call(
        functools.partial(conv_back_kernel, chunk=chunk),
        grid=(count, length // lanes),
        in_specs=[
            seq(length, inner),
            seq(BORDER, inner),
            seq(BORDER, inner),
            seq(2, length, LANES),
            held(w_conv.shape),
            vector(inner, 6),
            vector(inner, 7),
            here(inner, lanes, first),
            here(8, lanes, first),
        ]
        + [pl.BlockSpec(memory_space=pl.ANY)] * len(more),
        out_specs=[here(inner, lanes, first), held((2, inner, LANES))],
        input_output_aliases={9: 0} if more else {},
        out_shape=[shape((seqs, inner, length)), shape((2, inner, LANES), F32)],
        scratch_shapes=[
            pltpu.VMEM((length + 2 * BORDER, inner), BF16),
            pltpu.VMEM((KERNEL_TAPS // 2, length, inner), BF16),
            pltpu.VMEM((inner, lanes), F32),
            pltpu.VMEM((inner, lanes), F32),
            pltpu.VMEM((2, inner, LANES), F32),
        ],
        compiler_params=params(2),
        cost_estimate=cost(2 * rows.size * w_conv.size * count // (seqs * inner), 10 * rows.size * count // seqs),
        name="conv_back",
    )(rows, before, after, mask, w_conv, vectors, vectors, normed2, stats, *more)


def leave_kernel(low, w_in, x, g, gain, shift, stats, *rest, chunk):
    out, grads, grad, sums = rest[-4:]
    lanes, width = out.shape[2], out.shape[1]
    cleared(sums)
    grad[...] = dot(w_in[...], low[0])
    mean = stats[0, 0:1, :]
    scale = stats[0, 1:2, :]
    norm = lambda at: (x[0, at, :].astype(F32) - mean) * scale

    def first(i, carry):
        at = rows_at(i, chunk)
        normed = norm(at)
        _, _, p, q = back_first(
            grad[at, :], normed, wide(gain[at, :], lanes), wide(shift[at, :], lanes)
        )
        grad[at, :] = q
        sums[0, at, :] += folded(p * normed)
        sums[1, at, :] += folded(p)
        return carry[0] + q, carry[1] + q * normed

    zero = jnp.zeros((chunk, lanes), F32)
    one, two = each(width // chunk, first, (zero, zero))
    one = jnp.sum(one, axis=0, keepdims=True) * (1.0 / width)
    two = jnp.sum(two, axis=0, keepdims=True) * (1.0 / width)

    slope = scale * scale * two
    level = scale * one - mean * slope

    def second(i, carry):
        at = rows_at(i, chunk)
        branch = (scale * grad[at, :] - level) - x[0, at, :].astype(F32) * slope
        passed = g[0, at, :].astype(F32)
        sums[2, at, :] += folded(passed)
        out[0, at, :] = (passed + branch).astype(BF16)
        return carry

    each(width // chunk, second, 0)
    handed(sums, grads)


def leave(low, w_in, x, g, vectors, stats, first, count, into=None, lanes=256, chunk=16):
    seqs, inner, length = low.shape
    width = x.shape[1]
    more = () if into is None else (into,)
    return pl.pallas_call(
        functools.partial(leave_kernel, chunk=chunk),
        grid=(count, length // lanes),
        in_specs=[
            here(inner, lanes, first),
            held((width, inner)),
            here(width, lanes, first),
            here(width, lanes, first),
            vector(width, 0),
            vector(width, 1),
            here(8, lanes, first),
        ]
        + [pl.BlockSpec(memory_space=pl.ANY)] * len(more),
        input_output_aliases={7: 0} if more else {},
        out_specs=[here(width, lanes, first), held((3, width, LANES))],
        out_shape=[shape(x.shape), shape((3, width, LANES), F32)],
        scratch_shapes=[pltpu.VMEM((width, lanes), F32), pltpu.VMEM((3, width, LANES), F32)],
        compiler_params=params(2),
        cost_estimate=cost(2 * low.size * width * count // seqs, (2 * low.size + 6 * x.size) * count // seqs),
        name="leave",
    )(low, w_in, x, g, vectors, vectors, stats, *more)


def finish_kernel(w_out, act3, x, bias, *rest, chunk):
    out, proj = rest[-2:]
    lanes, width = out.shape[2], out.shape[1]
    proj[...] = dot(w_out[...], act3[0])

    def body(i, carry):
        at = rows_at(i, chunk)
        out[0, at, :] = (x[0, at, :].astype(F32) + proj[at, :] + wide(bias[at, :], lanes)).astype(BF16)
        return carry

    each(width // chunk, body, 0)


def finish(w_out_t, act3, x, vectors, first, count, into=None, lanes=512, chunk=32):
    more = () if into is None else (into,)
    seqs, inner, length = act3.shape
    width = x.shape[1]
    return pl.pallas_call(
        functools.partial(finish_kernel, chunk=chunk),
        grid=(count, length // lanes),
        in_specs=[held((width, inner)), here(inner, lanes, first), here(width, lanes, first), vector(width, 2)]
        + [pl.BlockSpec(memory_space=pl.ANY)] * len(more),
        input_output_aliases={4: 0} if more else {},
        out_specs=here(width, lanes, first),
        out_shape=shape(x.shape),
        scratch_shapes=[pltpu.VMEM((width, lanes), F32)],
        compiler_params=params(2),
        cost_estimate=cost(0, 0),
        name="finish",
    )(w_out_t, act3, x, vectors, *more)


def grads_kernel(at, *refs, pair, taps, keep, units):
    refs = list(refs)
    take = lambda n: [refs.pop(0) for _ in range(n)]
    sources = []
    left = right = act2 = rows3 = before = after = mask = got = None
    if pair:
        left, right = take(2)
    if taps:
        act2, rows3, before, after, mask = take(5)
    if keep:
        (got,) = take(1)
    outs = take(2 if keep else len(units))
    sems = refs.pop(-1)
    loads = []

    def load(source, target):
        copy = pltpu.make_async_copy(source, target, sems.at[len(loads)])
        copy.start()
        loads.append(copy)
        return copy

    if pair:
        left_here, right_here = take(2)
        half = left_here.shape[1]
        columns = right_here.shape[1] // pair
        first, blocks = [], []
        for i in range(pair):
            span = pl.ds(i * columns, columns)
            for seq in range(left_here.shape[0]):
                if i == 0:
                    rows = pl.ds(pl.multiple_of(at[0] * half, half), half)
                    first.append(load(left.at[seq, rows, :], left_here.at[seq]))
                blocks.append(load(right.at[seq, span, :], right_here.at[seq, span, :]))
    if taps:
        act2_here, whole, mask_here, masked = take(4)
        seqs, length = rows3.shape[0], rows3.shape[1]
        half2 = act2_here.shape[1]
        ready = [load(act2.at[:, pl.ds(pl.multiple_of(at[0] * half2, half2), half2), :], act2_here)]
        for seq in range(seqs):
            ready.append(load(rows3.at[seq], whole.at[seq, pl.ds(BORDER, length), :]))
        ready.append(load(before, whole.at[:, pl.ds(0, BORDER), :]))
        ready.append(load(after, whole.at[:, pl.ds(BORDER + length, BORDER), :]))
        ready.append(load(mask, mask_here))
    if keep:
        got_here, total = take(2)
        got_load = load(got, got_here)

    def give(step, value):
        if not keep:
            place = step
            for out, size in zip(outs, units):
                if place < size:
                    out[place] = value.astype(BF16)
                    return
                place -= size
        if step == 0:
            got_load.wait()
        total[...] = value + got_here[step].astype(F32)
        rows = outs[0].shape[1]
        for place, out in enumerate(outs):
            start = pl.multiple_of((at[1] ^ place) * rows, 8)
            out[step] = total[pl.ds(start, rows), :].astype(BF16)

    for i in range(pair):
        value = None
        for seq in range(left_here.shape[0]):
            if i == 0:
                first[seq].wait()
            blocks[i * left_here.shape[0] + seq].wait()
            part = dot(left_here[seq], right_here[seq, i * columns : (i + 1) * columns, :], NT)
            value = part if value is None else value + part
        give(i, value)
    for step, tap in enumerate(taps):
        by = (tap - KERNEL_TAPS // 2) * DILATION_STEP
        if step == 0:
            for copy in ready:
                copy.wait()
        value = None
        for seq in range(seqs):
            if by > 0:
                mask_rows(whole.at[seq], mask_here, masked, seq, by)
                rows = masked[...]
            else:
                rows = whole[seq, BORDER - by : BORDER - by + length, :]
            part = dot(act2_here[seq], rows)
            value = part if value is None else value + part
        give(pair + step, value)


def tap_grads_kernel(left, rows3, before, after, mask, out, left_here, whole, mask_here, masked, total, done, sems):
    seqs, length = rows3.shape[0], rows3.shape[1]
    count, size = out.shape[0], left.shape[1] // out.shape[0]

    def copy(place, source, target):
        moving = pltpu.make_async_copy(source, target, sems.at[place])
        moving.start()
        return moving

    loads = [copy(0, before, whole.at[:, pl.ds(0, BORDER), :])]
    loads.append(copy(1, after, whole.at[:, pl.ds(BORDER + length, BORDER), :]))
    for seq in range(seqs):
        loads.append(copy(2 + 2 * seq, rows3.at[seq], whole.at[seq, pl.ds(BORDER, length), :]))
        loads.append(copy(3 + 2 * seq, left.at[seq], left_here.at[seq]))
    loads.append(copy(2 + 2 * seqs, mask, mask_here))
    stores = []
    for tap in range(KERNEL_TAPS):
        by = (tap - KERNEL_TAPS // 2) * DILATION_STEP
        value = None
        for seq in range(seqs):
            if tap == 0:
                for load in loads[: 4 if seq == 0 else 2]:
                    load.wait()
                loads = loads[4 if seq == 0 else 2 :]
            if by > 0:
                for load in loads:
                    load.wait()
                loads = []
                mask_rows(whole.at[seq], mask_here, masked, seq, by)
                rows = masked[...]
            else:
                rows = whole[seq, BORDER - by : BORDER - by + length, :]
            part = dot(left_here[seq], rows)
            value = part if value is None else value + part
        total[tap % 2] = value
        last = tap == KERNEL_TAPS - 1
        if tap % 2 == 0 and not last:
            continue
        start = tap // 2 * 2 * size
        height = out.shape[1] - start if last else 2 * size
        fill = jnp.zeros((height - size, total.shape[2]), F32)
        for shard in range(count):
            span = slice(shard * size, (shard + 1) * size)
            below = fill if last else total[1, span, :]
            done[tap // 2, shard, :height, :] = jnp.concatenate([total[0, span, :], below], axis=0).astype(BF16)
            place = 3 + 2 * seqs + tap // 2 * count + shard
            stores.append(copy(place, done.at[tap // 2, shard, pl.ds(0, height), :], out.at[shard, pl.ds(start, height), :]))
    for store in stores:
        store.wait()


def tap_grads(count, padded, left, rows3, before, after, mask):
    seqs, length, inner = rows3.shape
    steps = -(-KERNEL_TAPS // 2)
    operands = (left, rows3, before, after, mask)
    return pl.pallas_call(
        tap_grads_kernel,
        in_specs=[pl.BlockSpec(memory_space=pl.ANY)] * len(operands),
        out_specs=pl.BlockSpec(memory_space=pl.ANY),
        out_shape=shape((count, padded, inner)),
        scratch_shapes=[
            pltpu.VMEM(left.shape, BF16),
            pltpu.VMEM((seqs, length + 2 * BORDER, inner), BF16),
            pltpu.VMEM(mask.shape, BF16),
            pltpu.VMEM((length, inner), BF16),
            pltpu.VMEM((2, inner, inner), F32),
            pltpu.VMEM((steps, count, 2 * inner // count, inner), BF16),
            pltpu.SemaphoreType.DMA((3 + 2 * seqs + steps * count,)),
        ],
        compiler_params=params(),
        cost_estimate=cost(2 * KERNEL_TAPS * left.size * inner, 4 * left.size + 10 * inner * inner),
        name="tap_grads",
    )(*operands)


def mask_rows(whole, mask, masked, seq, by):
    length, inner = masked.shape
    chunk = 128

    def body(i, carry):
        kept = mask[seq, by // DILATION_STEP - 1, rows_at(i, chunk), :]
        kept = jnp.concatenate([kept] * -(-inner // LANES), axis=1)[:, :inner]
        start = pl.multiple_of(i * chunk + BORDER - by, DILATION_STEP)
        masked[rows_at(i, chunk), :] = whole[pl.ds(start, chunk), :] * kept
        return carry

    each(length // chunk, body, 0, 1)


def grads(at, columns, pair=None, taps=(), conv=(), got=None, units=None):
    operands, scratch = [], []
    count, flops, copies = 0, 0, 0
    if pair is not None:
        left, right = pair
        half = left.shape[1] // 2
        count = right.shape[1] // columns
        operands += [left, right]
        scratch += [pltpu.VMEM((left.shape[0], half, left.shape[2]), BF16), pltpu.VMEM(right.shape, BF16)]
        copies += left.shape[0] * (1 + count)
        flops += left.size * right.shape[1]
    if taps:
        act2, rows3, _, _, mask = conv
        seqs, length, inner = rows3.shape
        half = inner // 2
        operands += conv
        scratch += [
            pltpu.VMEM((seqs, half, length), BF16),
            pltpu.VMEM((seqs, length + 2 * BORDER, inner), BF16),
            pltpu.VMEM(mask.shape, BF16),
            pltpu.VMEM((length, inner), BF16),
        ]
        copies += 4 + seqs
        flops += act2.size * inner * len(taps)
    total = count + len(taps)
    if got is None:
        units = units or (total,)
        dims = [(size, half, columns) for size in units]
    else:
        operands.append(got)
        scratch += [pltpu.VMEM(got.shape, BF16), pltpu.VMEM((half, columns), F32)]
        copies += 1
        dims = [(total, half // 2, columns)] * 2
    scratch.append(pltpu.SemaphoreType.DMA((copies,)))
    return pl.pallas_call(
        functools.partial(grads_kernel, pair=count, taps=taps, keep=got is not None, units=units),
        grid_spec=pltpu.PrefetchScalarGridSpec(
            num_scalar_prefetch=1,
            grid=(1,),
            in_specs=[pl.BlockSpec(memory_space=pl.ANY)] * len(operands),
            out_specs=[held(d) for d in dims],
            scratch_shapes=scratch,
        ),
        out_shape=[shape(d) for d in dims],
        compiler_params=params(1),
        cost_estimate=cost(flops, 2 * sum(o.size for o in operands)),
        name="grads",
    )(at, *operands)


def flip_kernel(w, out):
    for tap in range(w.shape[0]):
        out[tap] = w[tap].T


def flip(w):
    taps, rows, columns = w.shape
    return pl.pallas_call(
        flip_kernel,
        out_shape=shape((taps, columns, rows)),
        compiler_params=params(),
        cost_estimate=cost(0, 4 * w.size),
        name="flip",
    )(w)


def assemble_kernel(at, own, mine, other, natural, *rest):
    whole = rest[-1]
    rows, half = own.shape[0], mine.shape[1]
    whole[pl.ds(pl.multiple_of(at[0] * rows, 8), rows), :] = own[...].astype(F32)
    for step in range(mine.shape[0]):
        for pieces, core in ((mine, at[1]), (other, 1 - at[1])):
            start = (at[0] ^ (step + 1)) * rows + core * (rows - half)
            whole[pl.ds(pl.multiple_of(start, 8), half), :] = pieces[step].astype(F32)
    natural[...] = whole[...].astype(BF16)
    if len(rest) == 2:
        rest[0][...] = natural[...].T


def assemble(at, own, mine, other, turned=True):
    rows, columns = own.shape
    full = rows * (mine.shape[0] + 1)
    dims = [(full, columns), (columns, full)][: 1 + turned]
    return pl.pallas_call(
        assemble_kernel,
        grid_spec=pltpu.PrefetchScalarGridSpec(
            num_scalar_prefetch=1,
            grid=(1,),
            in_specs=[held(own.shape), held(mine.shape), held(other.shape)],
            out_specs=[held(d) for d in dims],
            scratch_shapes=[pltpu.VMEM((full, columns), F32)],
        ),
        out_shape=[shape(d) for d in dims],
        compiler_params=params(1),
        cost_estimate=cost(0, 6 * full * columns),
        name="assemble",
    )(at, own, mine, other)


def join_kernel(pieces, natural, turned, whole, *, rows):
    count, half = pieces.shape[0], pieces.shape[3]
    for shard in range(count):
        for core in range(2):
            start = shard * rows + core * (rows - half)
            whole[start : start + half, :] = pieces[shard, core, 0].astype(F32)
    natural[0] = whole[...].astype(BF16)
    turned[0] = natural[0].T


def join(pieces, rows):
    count, cores, taps, half, columns = pieces.shape
    full = count * rows
    dims = [(taps, full, columns), (taps, columns, full)]
    return pl.pallas_call(
        functools.partial(join_kernel, rows=rows),
        grid=(taps,),
        in_specs=[pl.BlockSpec((count, cores, 1, half, columns), lambda t: (0, 0, t, 0, 0))],
        out_specs=[pl.BlockSpec((1, *d[1:]), lambda t: (t, 0, 0)) for d in dims],
        out_shape=[shape(d) for d in dims],
        scratch_shapes=[pltpu.VMEM((full, columns), F32)],
        compiler_params=params(1),
        cost_estimate=cost(0, 6 * taps * full * columns),
        name="join",
    )(pieces)


def spread_kernel(at, parts, out, rows, *, sizes):
    count = parts.shape[0]
    for i in range(count):
        rows[pl.ds(at[0] ^ i, 1), :] = parts[i : i + 1, :]
    start, base = 0, 0
    for size in sizes:
        for shard in range(count):
            row = rows[shard : shard + 1, start : start + size]
            out[base : base + size, :] = jnp.broadcast_to(row, (LANES, size)).T
            base += size
        start += size


def spread(at, parts, sizes):
    total = parts.size
    return pl.pallas_call(
        functools.partial(spread_kernel, sizes=sizes),
        grid_spec=pltpu.PrefetchScalarGridSpec(
            num_scalar_prefetch=1,
            grid=(1,),
            in_specs=[held(parts.shape)],
            out_specs=held((total, LANES)),
            scratch_shapes=[pltpu.VMEM(parts.shape, F32)],
        ),
        out_shape=shape((total, LANES), F32),
        compiler_params=params(1),
        cost_estimate=cost(0, 4 * LANES * total),
        name="spread",
    )(at, parts)


def after(value, *others):
    return lax.optimization_barrier((value, *others))[0] if others else value


def swapped(x):
    return lax.ppermute(x, "core", [(0, 1), (1, 0)])


def from_ws(x, bit):
    return lax.ppermute(x, "ws", [(i, i ^ bit) for i in range(lax.axis_size("ws"))])


def neighbours(first, last):
    runs = lax.axis_size("run") * 2
    up = [(i, i + 1) for i in range(runs - 1)]
    down = [(i + 1, i) for i in range(runs - 1)]
    return lax.ppermute(last, ("run", "core"), up), lax.ppermute(first, ("run", "core"), down)


def square():
    return lax.axis_size("ws") == 4 and lax.axis_size("run") == 4


def halved(rows):
    return -(-rows // 16) * 8


def fetched(shard):
    rows = shard.shape[0]
    half = halved(rows)
    own = lax.dynamic_slice_in_dim(shard, lax.axis_index("core") * (rows - half), half, axis=0)
    return [from_ws(own, bit) for bit in (1, 2, 3)]


def whole_weight(at, shard, pieces, turned=True):
    if pieces is None:
        natural = lax.all_gather(shard, "ws", axis=0, tiled=True)
        return [natural, flip(natural[None])[0]][: 1 + turned]
    mine = jnp.stack(pieces)
    return assemble(at, shard, mine, swapped(mine), turned)


def halves_of(shard, *others):
    taps, rows, columns = shard.shape
    half = halved(rows)
    own = lax.dynamic_slice_in_dim(shard, lax.axis_index("core") * (rows - half), half, axis=1)
    pieces = lax.all_gather(after(own, *others), ("ws", "core"), axis=0)
    return pieces.reshape(-1, 2, taps, half, columns)


def summed(*terms):
    total = terms[0].astype(F32)
    for term in terms[1:]:
        total = total + term.astype(F32)
    return total.astype(BF16)


def active(shard):
    return shard >> 1


class Share:
    def __init__(self, first, second):
        self.dims = first.shape
        rows = lambda x: x.reshape(-1, x.shape[-1])
        self.sum, self.second = rows(first), rows(second)

    def land(self, *kernels):
        self.sum = summed(self.sum, *after(self.came, *kernels))
        return self.sum

    def spread(self):
        near = [(2 * i + active(i), 2 * (i ^ 1) + active(i)) for i in range(4)]
        far = lambda bit: [(2 * i + 1 - active(i), 2 * (i ^ bit) + 1 - active(i)) for i in range(4)]
        move = lambda x, pairs: lax.ppermute(x, ("ws", "core"), pairs)
        self.came = (move(self.second, near), move(self.sum, far(2)), move(self.second, far(3)))

    def along(self, x, bits):
        every = []
        for shard in range(4):
            every += [((shard * 4 + i) * 2 + active(shard), (shard * 4 + (i ^ bits)) * 2 + active(shard)) for i in range(4)]
        self.came = (lax.ppermute(x, ("ws", "run", "core"), every),)

    def inward(self):
        self.along(self.sum, 1)

    def middle(self):
        self.along(self.sum, 3)

    def both(self):
        shard, core = lax.axis_index("ws"), lax.axis_index("core")
        pairs = [(2 * i + active(i), 2 * i + 1 - active(i)) for i in range(4)]
        other = lax.ppermute(self.sum, ("ws", "core"), pairs)
        return jnp.where(core == active(shard), self.sum, other).astype(F32).reshape(self.dims)


def plain(low, high, axis):
    whole = jnp.concatenate([low, high], axis=axis)
    owned = lax.psum_scatter(whole, "ws", scatter_dimension=axis, tiled=True)
    return lax.psum(owned, ("run", "core")).astype(F32)


class Small:
    def __init__(self, mine):
        self.sum = mine

    def send(self, axis, bit):
        self.came = lax.ppermute(self.sum, axis, [(i, i ^ bit) for i in range(lax.axis_size(axis))])

    def land(self, *kernels):
        self.sum = self.sum + after(self.came, *kernels)


def totals_of(count, sums1, sums2, sums3):
    every = (sums1[0], sums1[1], sums1[2], sums2[0], sums2[1], sums3[0], sums3[1])
    return jnp.concatenate([s.sum(axis=-1).reshape(count, -1) for s in every], axis=1)


def shards(
    inputs,
    cotangent,
    block_ids,
    first_gain,
    first_shift,
    weight_in,
    second_gain,
    second_shift,
    weight_conv,
    third_gain,
    third_shift,
    weight_out,
    output_bias,
):
    x = inputs.transpose(0, 2, 1)
    g = cotangent.transpose(0, 2, 1)
    count, shard, core = lax.axis_size("ws"), lax.axis_index("ws"), lax.axis_index("core")
    easy = square()
    place = jnp.stack([shard, core])
    owned_vectors = (first_gain, first_shift, output_bias, second_gain, second_shift, third_gain, third_shift)
    sizes = tuple(own.size for own in owned_vectors)
    flat = jnp.concatenate(owned_vectors)
    if easy:
        parts = jnp.stack([flat, *[from_ws(flat, bit) for bit in (1, 2, 3)]]).astype(F32)
        vectors = spread(place, parts, sizes)
    else:
        parts = lax.all_gather(flat, "ws", axis=0).astype(F32)
        vectors = spread(jnp.zeros_like(place), parts, sizes)
    in_pieces = fetched(after(weight_in, parts)) if easy else None
    conv_halves = halves_of(weight_conv) if easy else None
    act1, stats1 = open_block(x, vectors)
    length = block_ids.shape[1]
    ids_before, ids_after = neighbours(block_ids[:, :BORDER], block_ids[:, -BORDER:])
    ids = jnp.concatenate([ids_before, block_ids, ids_after], axis=1)
    same = lambda by: ids[:, BORDER + by : BORDER + by + length] == block_ids
    steps = [DILATION_STEP * (i + 1) for i in range(KERNEL_TAPS // 2)]

    def masks(sign):
        both = jnp.stack([same(sign * by) for by in steps], axis=1)
        return jnp.broadcast_to(both[..., None], (*both.shape, LANES)).astype(BF16)

    mask, mask_back = masks(1), masks(-1)
    if easy:
        mask, mask_back = after((mask, mask_back), act1)
    if easy:
        in_pieces = after(in_pieces, act1, mask, mask_back)
        out_pieces = fetched(after(weight_out, *in_pieces))
    else:
        out_pieces = None
    w_in, w_in_t = whole_weight(place, weight_in, in_pieces)
    act2, rows2, normed2, stats2 = enter(act1, w_in_t, vectors)
    halo2 = neighbours(rows2[:, :BORDER], rows2[:, -BORDER:])
    if easy:
        out_pieces = after(out_pieces, act2)
    (w_out,) = whole_weight(place, weight_out, out_pieces, False)
    if easy:
        w_conv, w_conv_t = join(after(conv_halves, w_out), weight_conv.shape[1])
    else:
        w_conv = lax.all_gather(weight_conv, "ws", axis=1, tiled=True)
        w_conv_t = flip(w_conv)
    halo2 = after(halo2, w_conv_t)
    act3, rows3, sums3 = conv_block(rows2, *halo2, mask, w_conv_t, vectors, g, w_out)
    halo = neighbours(rows3[:, :BORDER], rows3[:, -BORDER:])
    bit = shard & 1
    give, keep = jnp.stack([1 - core, bit]), jnp.stack([core, bit])
    if not easy:
        give, keep = jnp.zeros_like(give), jnp.ones_like(keep)
    seqs = x.shape[0]
    back = lambda rows, seq, number, into: conv_back(
        rows, *halo, mask_back, w_conv, vectors, normed2, stats2, seq, number, into
    )
    close = lambda low, seq, number, into: leave(low, w_in, x, g, vectors, stats1, seq, number, into)
    width, inner = x.shape[1], act2.shape[1]
    if not easy:
        conv = (act2, rows3, *halo, mask_back)
        halves = lambda **kw: [grads(at, inner, **kw)[0] for at in (give, keep)]
        out_grad = plain(*halves(pair=(act3, g)), 1)
        out_grad = out_grad.transpose(1, 0, 2).reshape(-1, width)
        conv_grad = plain(*halves(taps=tuple(range(KERNEL_TAPS)), conv=conv), 1)
        low2, sums2 = back(rows3, 0, seqs, None)
        in_grad = plain(*halves(pair=(act1, low2)), 1)[0]
        input_grad, sums1 = close(low2, 0, seqs, None)
        block_output = finish(flip(w_out[None])[0], act3, x, vectors, 0, seqs)
    else:
        shard_rows = inner // count
        padded = -(-KERNEL_TAPS * shard_rows // LANES) * LANES
        taps = tap_grads(count, padded, act2, rows3, *halo, mask_back)
        (out_send,) = grads(give, inner, pair=(after(act3, taps), g))
        w_out_t = flip(after(w_out, out_send)[None])[0]
        got_out = after(swapped(out_send), w_out_t)
        taps = lax.psum_scatter(taps.reshape(-1, inner), "ws", scatter_dimension=0, tiled=True)
        out = Share(*grads(keep, inner, pair=(act3, g), got=got_out))
        out.spread()
        low2, sums2 = back(after(rows3, out.sum), 0, seqs, None)
        out.land(low2)
        out.inward()
        (in_send,) = grads(give, inner, pair=(act1, after(low2, out.sum)))
        got_in = swapped(in_send)
        out.land(in_send)
        out.middle()
        got_in = after(got_in, out.sum)
        both = Share(*grads(keep, inner, pair=(act1, low2), got=got_in))
        both.spread()
        out.land(both.sum)
        rows = out.both()
        low2, taps = after((low2, taps), both.sum, out.sum)
        taps = lax.psum_scatter(taps, ("run", "core"), scatter_dimension=0, tiled=True)
        input_grad, sums1 = close(low2, 0, seqs, None)
        small = Small(totals_of(count, sums1, sums2, sums3))
        small.send("core", 1)
        both.land(sums1)
        both.inward()
        small.land(both.sum)
        small.send("run", 1)
        small.land()
        small.send("run", 2)
        (w_out_t, act3), taps = after(((w_out_t, act3), taps), both.sum, small.sum, rows)
        taps_sum = lax.all_gather(taps, ("run", "core"), axis=0, tiled=True)
        block_output = finish(w_out_t, act3, x, vectors, 0, seqs)
        small.land(block_output)
        both.land(block_output, small.sum)
        small.send("ws", 1)
        both.middle()
        small.land(both.sum)
        small.send("ws", 2)
        small.land()
        taps = taps_sum[: KERNEL_TAPS * shard_rows].astype(F32)
        conv_grad = taps.reshape(KERNEL_TAPS, shard_rows, inner)
        out_grad = jnp.concatenate([rows[0], rows[1]], axis=1)
        both.land(small.sum, conv_grad, out_grad)
        in_grad = both.both().reshape(-1, inner)
        small = small.sum

    if not easy:
        small = lax.psum(totals_of(count, sums1, sums2, sums3), ("ws", "run", "core"))
    small = lax.dynamic_index_in_dim(small, shard, axis=0, keepdims=False)
    at, vector_grads = 0, []
    for size in sizes:
        vector_grads.append(small[at : at + size])
        at += size
    gain1, shift1, bias, gain2, shift2, gain3, shift3 = vector_grads
    return (
        block_output.transpose(0, 2, 1),
        input_grad.transpose(0, 2, 1),
        gain1,
        shift1,
        in_grad,
        gain2,
        shift2,
        conv_grad,
        gain3,
        shift3,
        out_grad,
        bias,
    )


def solution(mesh):
    count, runs = mesh.devices.shape
    split = jax.sharding.Mesh(mesh.devices.reshape(count, runs // 2, 2), ("ws", "run", "core"))
    tokens = P("ws", ("run", "core"), None)
    rows = P("ws", None)
    taps = P(None, "ws", None)
    placed = (tokens, tokens, P("ws", ("run", "core")), P("ws"), P("ws"), rows, P("ws"), P("ws"), taps)
    placed += (P("ws"), P("ws"), rows, P("ws"))
    given = (tokens, tokens, P("ws"), P("ws"), rows, P("ws"), P("ws"), taps, P("ws"), P("ws"), rows, P("ws"))
    return jax.shard_map(shards, mesh=split, in_specs=placed, out_specs=given, check_vma=False)
```

```python
import functools
import jax
import jax.numpy as jnp
from jax import lax
from jax.experimental import pallas as pl
from jax.experimental.pallas import tpu as pltpu
from jax.sharding import PartitionSpec as P

KERNEL_TAPS = 5
DILATION_STEP = 16
EPS = 1e-05
LANES = 128
BORDER = KERNEL_TAPS // 2 * DILATION_STEP
F32 = jnp.float32
BF16 = jnp.bfloat16
VMEM_BYTES = 60 * 2**20

NN = (((1,), (0,)), ((), ()))
NT = (((1,), (1,)), ((), ()))


def params(steps=0):
    return pltpu.CompilerParams(
        dimension_semantics=("arbitrary",) * steps or None, vmem_limit_bytes=VMEM_BYTES
    )


def cost(flops, bytes_accessed):
    return pl.CostEstimate(flops=flops // 16, bytes_accessed=bytes_accessed // 16, transcendentals=0)


def shape(dims, dtype=BF16):
    return jax.ShapeDtypeStruct(dims, dtype)


def dot(left, right, dims=NN):
    return lax.dot_general(left, right, dims, preferred_element_type=F32)


def wide(column, lanes):
    return jnp.concatenate([column] * (lanes // LANES), axis=1)


def folded(values):
    total = values[:, :LANES]
    for at in range(LANES, values.shape[1], LANES):
        total = total + values[:, at : at + LANES]
    return total


def logistic(x):
    return 0.5 * jnp.tanh(0.5 * x) + 0.5


def vector(rows, block):
    return pl.BlockSpec((rows, LANES), lambda *_: (block, 0))


def here(rows, lanes, seq=0):
    return pl.BlockSpec((1, rows, lanes), lambda s, t: (s + seq, 0, t))


def held(dims):
    return pl.BlockSpec(dims, lambda *_: (0,) * len(dims))


def each(count, body, init, unroll=True):
    return lax.fori_loop(0, count, body, init, unroll=unroll)


def rows_at(index, size):
    return pl.ds(pl.multiple_of(index * size, size), size)


def row_stats(load, channels, chunk, lanes, unroll=True):
    steps = channels // chunk
    zero = jnp.zeros((chunk, lanes), F32)
    total = each(steps, lambda i, t: t + load(i), zero, unroll)
    mean = jnp.sum(total, axis=0, keepdims=True) * (1.0 / channels)

    def square(i, t):
        centred = load(i) - mean
        return t + centred * centred

    squares = each(steps, square, zero, unroll)
    spread = jnp.sum(squares, axis=0, keepdims=True) * (1.0 / channels)
    return mean, lax.rsqrt(spread + EPS)


def back_first(u, normed, gain, shift):
    pre = normed * gain + shift
    sigma = logistic(pre)
    p = u * (sigma * (1.0 + pre * (1.0 - sigma)))
    return pre, sigma, p, p * gain


def first_step():
    return (pl.program_id(0) == 0) & (pl.program_id(1) == 0)


def last_step():
    return (pl.program_id(0) == pl.num_programs(0) - 1) & (
        pl.program_id(1) == pl.num_programs(1) - 1
    )


def cleared(sums):
    @pl.when(first_step())
    def _():
        sums[...] = jnp.zeros_like(sums)


def handed(sums, out):
    @pl.when(last_step())
    def _():
        out[...] = sums[...]


def open_kernel(x, gain, shift, act1, stats, *, chunk):
    lanes, width = x.shape[2], x.shape[1]
    load = lambda i: x[0, rows_at(i, chunk), :].astype(F32)
    mean, scale = row_stats(load, width, chunk, lanes)

    def activate(i, carry):
        at = rows_at(i, chunk)
        normed = (load(i) - mean) * scale
        pre = normed * wide(gain[at, :], lanes) + wide(shift[at, :], lanes)
        act1[0, at, :] = (pre * logistic(pre)).astype(BF16)
        return carry

    each(width // chunk, activate, 0)
    stats[0] = jnp.concatenate([mean, scale, jnp.zeros((6, lanes), F32)], axis=0)


def open_block(x, vectors, lanes=512, chunk=32):
    seqs, width, length = x.shape
    return pl.pallas_call(
        functools.partial(open_kernel, chunk=chunk),
        grid=(seqs, length // lanes),
        in_specs=[here(width, lanes), vector(width, 0), vector(width, 1)],
        out_specs=[here(width, lanes), here(8, lanes)],
        out_shape=[shape(x.shape), shape((seqs, 8, length), F32)],
        compiler_params=params(2),
        cost_estimate=cost(40 * x.size, 4 * x.size),
        name="open_block",
    )(x, vectors, vectors)


def enter_kernel(act1, w_in, gain, shift, act2, turned, normed2, stats, proj, *, chunk):
    lanes, inner = act1.shape[2], act2.shape[1]
    proj[...] = dot(w_in[...], act1[0])
    load = lambda i: proj[rows_at(i, chunk), :]
    mean, scale = row_stats(load, inner, chunk, lanes, 5)

    def activate(i, carry):
        at = rows_at(i, chunk)
        normed = (load(i) - mean) * scale
        normed2[0, at, :] = normed
        pre = normed * wide(gain[at, :], lanes) + wide(shift[at, :], lanes)
        act2[0, at, :] = (pre * logistic(pre)).astype(BF16)
        return carry

    each(inner // chunk, activate, 0, 5)
    turned[0] = act2[0].T
    stats[0] = jnp.concatenate([scale, jnp.zeros((7, lanes), F32)], axis=0)


def enter(act1, w_in_t, vectors, lanes=512, chunk=32):
    seqs, width, length = act1.shape
    inner = w_in_t.shape[0]
    return pl.pallas_call(
        functools.partial(enter_kernel, chunk=chunk),
        grid=(seqs, length // lanes),
        in_specs=[here(width, lanes), held((inner, width)), vector(inner, 6), vector(inner, 7)],
        out_specs=[
            here(inner, lanes),
            pl.BlockSpec((1, lanes, inner), lambda s, t: (s, t, 0)),
            here(inner, lanes),
            here(8, lanes),
        ],
        out_shape=[
            shape((seqs, inner, length)),
            shape((seqs, length, inner)),
            shape((seqs, inner, length), F32),
            shape((seqs, 8, length), F32),
        ],
        scratch_shapes=[pltpu.VMEM((inner, lanes), F32)],
        compiler_params=params(2),
        cost_estimate=cost(2 * act1.size * inner, seqs * length * (2 * width + 8 * inner)),
        name="enter",
    )(act1, w_in_t, vectors, vectors)


def extend(rows, before, after, mask, whole, masked, seq, sign):
    length = rows.shape[1]
    whole[:BORDER, :] = before[seq]
    whole[BORDER : BORDER + length, :] = rows[seq]
    whole[BORDER + length :, :] = after[seq]
    inner = rows.shape[2]
    chunk = 128
    for later in range(KERNEL_TAPS // 2):
        by = sign * (later + 1) * DILATION_STEP

        def body(i, carry, later=later, by=by):
            kept = mask[seq, later, rows_at(i, chunk), :]
            kept = jnp.concatenate([kept] * -(-inner // LANES), axis=1)[:, :inner]
            start = pl.multiple_of(i * chunk + BORDER + by, DILATION_STEP)
            masked[later, rows_at(i, chunk), :] = whole[pl.ds(start, chunk), :] * kept
            return carry

        each(length // chunk, body, 0, 1)


def tap_rows(whole, masked, tap, sign, start, count):
    by = (tap - KERNEL_TAPS // 2) * DILATION_STEP
    if by > 0:
        return masked[tap - KERNEL_TAPS // 2 - 1, pl.ds(start, count), :]
    return whole[pl.ds(start + (BORDER + sign * by), count), :]


def conv_kernel(rows, before, after, mask, w_conv, gain, shift, g, w_out, act3, turned, grads, whole, masked, conv, scaled, low, sums, upstream, *, chunk):
    tile = pl.program_id(1)
    lanes, inner = act3.shape[2], act3.shape[1]
    cleared(sums)

    @pl.when(tile == 0)
    def _():
        extend(rows, before, after, mask, whole, masked, 0, 1)

    start = pl.multiple_of(tile * lanes, lanes)
    total = None
    for tap in range(KERNEL_TAPS):
        part = dot(w_conv[tap], tap_rows(whole, masked, tap, 1, start, lanes), NT)
        total = part if total is None else total + part
    conv[...] = total
    upstream[...] = dot(w_out[...], g[0])
    load = lambda i: conv[rows_at(i, chunk), :]
    mean, scale = row_stats(load, inner, chunk, lanes)

    def first(i, carry):
        at = rows_at(i, chunk)
        normed = (load(i) - mean) * scale
        gains = wide(gain[at, :], lanes)
        pre, sigma, p, q = back_first(upstream[at, :], normed, gains, wide(shift[at, :], lanes))
        act3[0, at, :] = (pre * sigma).astype(BF16)
        conv[at, :] = normed
        scaled[at, :] = q
        sums[0, at, :] += folded(p * normed)
        sums[1, at, :] += folded(p)
        return carry[0] + q, carry[1] + q * normed

    zero = jnp.zeros((chunk, lanes), F32)
    one, two = each(inner // chunk, first, (zero, zero))
    one = jnp.sum(one, axis=0, keepdims=True) * (1.0 / inner)
    two = jnp.sum(two, axis=0, keepdims=True) * (1.0 / inner)

    def second(i, carry):
        at = rows_at(i, chunk)
        low[at, :] = (scale * (scaled[at, :] - one - conv[at, :] * two)).astype(BF16)
        return carry

    each(inner // chunk, second, 0)
    turned[0] = low[...].T
    handed(sums, grads)


def conv_block(rows, before, after, mask, w_conv_t, vectors, g, w_out, lanes=512, chunk=16):
    seqs, length, inner = rows.shape
    seq = lambda *dims: pl.BlockSpec((1, *dims), lambda s, t: (s,) + (0,) * len(dims))
    return pl.pallas_call(
        functools.partial(conv_kernel, chunk=chunk),
        grid=(seqs, length // lanes),
        in_specs=[
            seq(length, inner),
            seq(BORDER, inner),
            seq(BORDER, inner),
            seq(2, length, LANES),
            held(w_conv_t.shape),
            vector(inner, 8),
            vector(inner, 9),
            here(g.shape[1], lanes),
            held(w_out.shape),
        ],
        out_specs=[
            here(inner, lanes),
            pl.BlockSpec((1, lanes, inner), lambda s, t: (s, t, 0)),
            held((2, inner, LANES)),
        ],
        out_shape=[
            shape((seqs, inner, length)),
            shape((seqs, length, inner)),
            shape((2, inner, LANES), F32),
        ],
        scratch_shapes=[
            pltpu.VMEM((length + 2 * BORDER, inner), BF16),
            pltpu.VMEM((KERNEL_TAPS // 2, length, inner), BF16),
            pltpu.VMEM((inner, lanes), F32),
            pltpu.VMEM((inner, lanes), F32),
            pltpu.VMEM((inner, lanes), BF16),
            pltpu.VMEM((2, inner, LANES), F32),
            pltpu.VMEM((inner, lanes), F32),
        ],
        compiler_params=params(2),
        cost_estimate=cost(2 * rows.size * w_conv_t.size // inner, 12 * rows.size),
        name="conv_block",
    )(rows, before, after, mask, w_conv_t, vectors, vectors, g, w_out)


def conv_back_kernel(rows, before, after, mask, w_conv, gain, shift, normed2, stats, *rest, chunk):
    out, grads, whole, masked, grad, scaled, sums = rest[-7:]
    tile = pl.program_id(1)
    lanes, inner = out.shape[2], out.shape[1]
    cleared(sums)

    @pl.when(tile == 0)
    def _():
        extend(rows, before, after, mask, whole, masked, 0, -1)

    start = pl.multiple_of(tile * lanes, lanes)
    total = None
    for tap in range(KERNEL_TAPS):
        part = dot(w_conv[tap], tap_rows(whole, masked, tap, -1, start, lanes), NT)
        total = part if total is None else total + part
    grad[...] = total
    scale = stats[0, 0:1, :]

    def first(i, carry):
        at = rows_at(i, chunk)
        normed = normed2[0, at, :]
        _, _, p, q = back_first(
            grad[at, :], normed, wide(gain[at, :], lanes), wide(shift[at, :], lanes)
        )
        scaled[at, :] = q
        sums[0, at, :] += folded(p * normed)
        sums[1, at, :] += folded(p)
        return carry[0] + q, carry[1] + q * normed

    zero = jnp.zeros((chunk, lanes), F32)
    one, two = each(inner // chunk, first, (zero, zero))
    one = jnp.sum(one, axis=0, keepdims=True) * (1.0 / inner)
    two = jnp.sum(two, axis=0, keepdims=True) * (1.0 / inner)

    def second(i, carry):
        at = rows_at(i, chunk)
        out[0, at, :] = (scale * (scaled[at, :] - one - normed2[0, at, :] * two)).astype(BF16)
        return carry

    each(inner // chunk, second, 0)
    handed(sums, grads)


def conv_back(rows, before, after, mask, w_conv, vectors, normed2, stats, first, count, into=None, lanes=512, chunk=16):
    seqs, length, inner = rows.shape
    seq = lambda *dims: pl.BlockSpec((1, *dims), lambda s, t: (s + first,) + (0,) * len(dims))
    more = () if into is None else (into,)
    return pl.pallas_call(
        functools.partial(conv_back_kernel, chunk=chunk),
        grid=(count, length // lanes),
        in_specs=[
            seq(length, inner),
            seq(BORDER, inner),
            seq(BORDER, inner),
            seq(2, length, LANES),
            held(w_conv.shape),
            vector(inner, 6),
            vector(inner, 7),
            here(inner, lanes, first),
            here(8, lanes, first),
        ]
        + [pl.BlockSpec(memory_space=pl.ANY)] * len(more),
        out_specs=[here(inner, lanes, first), held((2, inner, LANES))],
        input_output_aliases={9: 0} if more else {},
        out_shape=[shape((seqs, inner, length)), shape((2, inner, LANES), F32)],
        scratch_shapes=[
            pltpu.VMEM((length + 2 * BORDER, inner), BF16),
            pltpu.VMEM((KERNEL_TAPS // 2, length, inner), BF16),
            pltpu.VMEM((inner, lanes), F32),
            pltpu.VMEM((inner, lanes), F32),
            pltpu.VMEM((2, inner, LANES), F32),
        ],
        compiler_params=params(2),
        cost_estimate=cost(2 * rows.size * w_conv.size * count // (seqs * inner), 10 * rows.size * count // seqs),
        name="conv_back",
    )(rows, before, after, mask, w_conv, vectors, vectors, normed2, stats, *more)


def leave_kernel(low, w_in, x, g, gain, shift, stats, *rest, chunk):
    out, grads, grad, sums = rest[-4:]
    lanes, width = out.shape[2], out.shape[1]
    cleared(sums)
    grad[...] = dot(w_in[...], low[0])
    mean = stats[0, 0:1, :]
    scale = stats[0, 1:2, :]
    norm = lambda at: (x[0, at, :].astype(F32) - mean) * scale

    def first(i, carry):
        at = rows_at(i, chunk)
        normed = norm(at)
        _, _, p, q = back_first(
            grad[at, :], normed, wide(gain[at, :], lanes), wide(shift[at, :], lanes)
        )
        grad[at, :] = q
        sums[0, at, :] += folded(p * normed)
        sums[1, at, :] += folded(p)
        return carry[0] + q, carry[1] + q * normed

    zero = jnp.zeros((chunk, lanes), F32)
    one, two = each(width // chunk, first, (zero, zero))
    one = jnp.sum(one, axis=0, keepdims=True) * (1.0 / width)
    two = jnp.sum(two, axis=0, keepdims=True) * (1.0 / width)

    slope = scale * scale * two
    level = scale * one - mean * slope

    def second(i, carry):
        at = rows_at(i, chunk)
        branch = (scale * grad[at, :] - level) - x[0, at, :].astype(F32) * slope
        passed = g[0, at, :].astype(F32)
        sums[2, at, :] += folded(passed)
        out[0, at, :] = (passed + branch).astype(BF16)
        return carry

    each(width // chunk, second, 0)
    handed(sums, grads)


def leave(low, w_in, x, g, vectors, stats, first, count, into=None, lanes=256, chunk=16):
    seqs, inner, length = low.shape
    width = x.shape[1]
    more = () if into is None else (into,)
    return pl.pallas_call(
        functools.partial(leave_kernel, chunk=chunk),
        grid=(count, length // lanes),
        in_specs=[
            here(inner, lanes, first),
            held((width, inner)),
            here(width, lanes, first),
            here(width, lanes, first),
            vector(width, 0),
            vector(width, 1),
            here(8, lanes, first),
        ]
        + [pl.BlockSpec(memory_space=pl.ANY)] * len(more),
        input_output_aliases={7: 0} if more else {},
        out_specs=[here(width, lanes, first), held((3, width, LANES))],
        out_shape=[shape(x.shape), shape((3, width, LANES), F32)],
        scratch_shapes=[pltpu.VMEM((width, lanes), F32), pltpu.VMEM((3, width, LANES), F32)],
        compiler_params=params(2),
        cost_estimate=cost(2 * low.size * width * count // seqs, (2 * low.size + 6 * x.size) * count // seqs),
        name="leave",
    )(low, w_in, x, g, vectors, vectors, stats, *more)


def finish_kernel(w_out, act3, x, bias, *rest, chunk):
    out, proj = rest[-2:]
    lanes, width = out.shape[2], out.shape[1]
    proj[...] = dot(w_out[...], act3[0])

    def body(i, carry):
        at = rows_at(i, chunk)
        out[0, at, :] = (x[0, at, :].astype(F32) + proj[at, :] + wide(bias[at, :], lanes)).astype(BF16)
        return carry

    each(width // chunk, body, 0)


def finish(w_out_t, act3, x, vectors, first, count, into=None, lanes=512, chunk=32):
    more = () if into is None else (into,)
    seqs, inner, length = act3.shape
    width = x.shape[1]
    return pl.pallas_call(
        functools.partial(finish_kernel, chunk=chunk),
        grid=(count, length // lanes),
        in_specs=[held((width, inner)), here(inner, lanes, first), here(width, lanes, first), vector(width, 2)]
        + [pl.BlockSpec(memory_space=pl.ANY)] * len(more),
        input_output_aliases={4: 0} if more else {},
        out_specs=here(width, lanes, first),
        out_shape=shape(x.shape),
        scratch_shapes=[pltpu.VMEM((width, lanes), F32)],
        compiler_params=params(2),
        cost_estimate=cost(0, 0),
        name="finish",
    )(w_out_t, act3, x, vectors, *more)


def grads_kernel(at, *refs, pair, taps, keep, units):
    refs = list(refs)
    take = lambda n: [refs.pop(0) for _ in range(n)]
    sources = []
    left = right = act2 = rows3 = before = after = mask = got = None
    if pair:
        left, right = take(2)
    if taps:
        act2, rows3, before, after, mask = take(5)
    if keep:
        (got,) = take(1)
    outs = take(2 if keep else len(units))
    sems = refs.pop(-1)
    loads = []

    def load(source, target):
        copy = pltpu.make_async_copy(source, target, sems.at[len(loads)])
        copy.start()
        loads.append(copy)
        return copy

    if pair:
        left_here, right_here = take(2)
        half = left_here.shape[1]
        columns = right_here.shape[1] // pair
        first, blocks = [], []
        for i in range(pair):
            span = pl.ds(i * columns, columns)
            for seq in range(left_here.shape[0]):
                if i == 0:
                    rows = pl.ds(pl.multiple_of(at[0] * half, half), half)
                    first.append(load(left.at[seq, rows, :], left_here.at[seq]))
                blocks.append(load(right.at[seq, span, :], right_here.at[seq, span, :]))
    if taps:
        act2_here, whole, mask_here, masked = take(4)
        seqs, length = rows3.shape[0], rows3.shape[1]
        half2 = act2_here.shape[1]
        ready = [load(act2.at[:, pl.ds(pl.multiple_of(at[0] * half2, half2), half2), :], act2_here)]
        for seq in range(seqs):
            ready.append(load(rows3.at[seq], whole.at[seq, pl.ds(BORDER, length), :]))
        ready.append(load(before, whole.at[:, pl.ds(0, BORDER), :]))
        ready.append(load(after, whole.at[:, pl.ds(BORDER + length, BORDER), :]))
        ready.append(load(mask, mask_here))
    if keep:
        got_here, total = take(2)
        got_load = load(got, got_here)

    def give(step, value):
        if not keep:
            place = step
            for out, size in zip(outs, units):
                if place < size:
                    out[place] = value.astype(BF16)
                    return
                place -= size
        if step == 0:
            got_load.wait()
        total[...] = value + got_here[step].astype(F32)
        rows = outs[0].shape[1]
        for place, out in enumerate(outs):
            start = pl.multiple_of((at[1] ^ place) * rows, 8)
            out[step] = total[pl.ds(start, rows), :].astype(BF16)

    for i in range(pair):
        value = None
        for seq in range(left_here.shape[0]):
            if i == 0:
                first[seq].wait()
            blocks[i * left_here.shape[0] + seq].wait()
            part = dot(left_here[seq], right_here[seq, i * columns : (i + 1) * columns, :], NT)
            value = part if value is None else value + part
        give(i, value)
    for step, tap in enumerate(taps):
        by = (tap - KERNEL_TAPS // 2) * DILATION_STEP
        if step == 0:
            for copy in ready:
                copy.wait()
        value = None
        for seq in range(seqs):
            if by > 0:
                mask_rows(whole.at[seq], mask_here, masked, seq, by)
                rows = masked[...]
            else:
                rows = whole[seq, BORDER - by : BORDER - by + length, :]
            part = dot(act2_here[seq], rows)
            value = part if value is None else value + part
        give(pair + step, value)


def tap_grads_kernel(left, rows3, before, after, mask, out, left_here, whole, mask_here, masked, total, done, sems):
    seqs, length = rows3.shape[0], rows3.shape[1]
    count, size = out.shape[0], left.shape[1] // out.shape[0]

    def copy(place, source, target):
        moving = pltpu.make_async_copy(source, target, sems.at[place])
        moving.start()
        return moving

    loads = [copy(0, before, whole.at[:, pl.ds(0, BORDER), :])]
    loads.append(copy(1, after, whole.at[:, pl.ds(BORDER + length, BORDER), :]))
    for seq in range(seqs):
        loads.append(copy(2 + 2 * seq, rows3.at[seq], whole.at[seq, pl.ds(BORDER, length), :]))
        loads.append(copy(3 + 2 * seq, left.at[seq], left_here.at[seq]))
    loads.append(copy(2 + 2 * seqs, mask, mask_here))
    stores = []
    for tap in range(KERNEL_TAPS):
        by = (tap - KERNEL_TAPS // 2) * DILATION_STEP
        value = None
        for seq in range(seqs):
            if tap == 0:
                for load in loads[: 4 if seq == 0 else 2]:
                    load.wait()
                loads = loads[4 if seq == 0 else 2 :]
            if by > 0:
                for load in loads:
                    load.wait()
                loads = []
                mask_rows(whole.at[seq], mask_here, masked, seq, by)
                rows = masked[...]
            else:
                rows = whole[seq, BORDER - by : BORDER - by + length, :]
            part = dot(left_here[seq], rows)
            value = part if value is None else value + part
        total[tap % 2] = value
        last = tap == KERNEL_TAPS - 1
        if tap % 2 == 0 and not last:
            continue
        start = tap // 2 * 2 * size
        height = out.shape[1] - start if last else 2 * size
        fill = jnp.zeros((height - size, total.shape[2]), F32)
        for shard in range(count):
            span = slice(shard * size, (shard + 1) * size)
            below = fill if last else total[1, span, :]
            done[tap // 2, shard, :height, :] = jnp.concatenate([total[0, span, :], below], axis=0).astype(BF16)
            place = 3 + 2 * seqs + tap // 2 * count + shard
            stores.append(copy(place, done.at[tap // 2, shard, pl.ds(0, height), :], out.at[shard, pl.ds(start, height), :]))
    for store in stores:
        store.wait()


def tap_grads(count, padded, left, rows3, before, after, mask):
    seqs, length, inner = rows3.shape
    steps = -(-KERNEL_TAPS // 2)
    operands = (left, rows3, before, after, mask)
    return pl.pallas_call(
        tap_grads_kernel,
        in_specs=[pl.BlockSpec(memory_space=pl.ANY)] * len(operands),
        out_specs=pl.BlockSpec(memory_space=pl.ANY),
        out_shape=shape((count, padded, inner)),
        scratch_shapes=[
            pltpu.VMEM(left.shape, BF16),
            pltpu.VMEM((seqs, length + 2 * BORDER, inner), BF16),
            pltpu.VMEM(mask.shape, BF16),
            pltpu.VMEM((length, inner), BF16),
            pltpu.VMEM((2, inner, inner), F32),
            pltpu.VMEM((steps, count, 2 * inner // count, inner), BF16),
            pltpu.SemaphoreType.DMA((3 + 2 * seqs + steps * count,)),
        ],
        compiler_params=params(),
        cost_estimate=cost(2 * KERNEL_TAPS * left.size * inner, 4 * left.size + 10 * inner * inner),
        name="tap_grads",
    )(*operands)


def mask_rows(whole, mask, masked, seq, by):
    length, inner = masked.shape
    chunk = 128

    def body(i, carry):
        kept = mask[seq, by // DILATION_STEP - 1, rows_at(i, chunk), :]
        kept = jnp.concatenate([kept] * -(-inner // LANES), axis=1)[:, :inner]
        start = pl.multiple_of(i * chunk + BORDER - by, DILATION_STEP)
        masked[rows_at(i, chunk), :] = whole[pl.ds(start, chunk), :] * kept
        return carry

    each(length // chunk, body, 0, 1)


def grads(at, columns, pair=None, taps=(), conv=(), got=None, units=None):
    operands, scratch = [], []
    count, flops, copies = 0, 0, 0
    if pair is not None:
        left, right = pair
        half = left.shape[1] // 2
        count = right.shape[1] // columns
        operands += [left, right]
        scratch += [pltpu.VMEM((left.shape[0], half, left.shape[2]), BF16), pltpu.VMEM(right.shape, BF16)]
        copies += left.shape[0] * (1 + count)
        flops += left.size * right.shape[1]
    if taps:
        act2, rows3, _, _, mask = conv
        seqs, length, inner = rows3.shape
        half = inner // 2
        operands += conv
        scratch += [
            pltpu.VMEM((seqs, half, length), BF16),
            pltpu.VMEM((seqs, length + 2 * BORDER, inner), BF16),
            pltpu.VMEM(mask.shape, BF16),
            pltpu.VMEM((length, inner), BF16),
        ]
        copies += 4 + seqs
        flops += act2.size * inner * len(taps)
    total = count + len(taps)
    if got is None:
        units = units or (total,)
        dims = [(size, half, columns) for size in units]
    else:
        operands.append(got)
        scratch += [pltpu.VMEM(got.shape, BF16), pltpu.VMEM((half, columns), F32)]
        copies += 1
        dims = [(total, half // 2, columns)] * 2
    scratch.append(pltpu.SemaphoreType.DMA((copies,)))
    return pl.pallas_call(
        functools.partial(grads_kernel, pair=count, taps=taps, keep=got is not None, units=units),
        grid_spec=pltpu.PrefetchScalarGridSpec(
            num_scalar_prefetch=1,
            grid=(1,),
            in_specs=[pl.BlockSpec(memory_space=pl.ANY)] * len(operands),
            out_specs=[held(d) for d in dims],
            scratch_shapes=scratch,
        ),
        out_shape=[shape(d) for d in dims],
        compiler_params=params(1),
        cost_estimate=cost(flops, 2 * sum(o.size for o in operands)),
        name="grads",
    )(at, *operands)


def flip_kernel(w, out):
    for tap in range(w.shape[0]):
        out[tap] = w[tap].T


def flip(w):
    taps, rows, columns = w.shape
    return pl.pallas_call(
        flip_kernel,
        out_shape=shape((taps, columns, rows)),
        compiler_params=params(),
        cost_estimate=cost(0, 4 * w.size),
        name="flip",
    )(w)


def assemble_kernel(at, own, mine, other, natural, *rest):
    whole = rest[-1]
    rows, half = own.shape[0], mine.shape[1]
    whole[pl.ds(pl.multiple_of(at[0] * rows, 8), rows), :] = own[...].astype(F32)
    for step in range(mine.shape[0]):
        for pieces, core in ((mine, at[1]), (other, 1 - at[1])):
            start = (at[0] ^ (step + 1)) * rows + core * (rows - half)
            whole[pl.ds(pl.multiple_of(start, 8), half), :] = pieces[step].astype(F32)
    natural[...] = whole[...].astype(BF16)
    if len(rest) == 2:
        rest[0][...] = natural[...].T


def assemble(at, own, mine, other, turned=True):
    rows, columns = own.shape
    full = rows * (mine.shape[0] + 1)
    dims = [(full, columns), (columns, full)][: 1 + turned]
    return pl.pallas_call(
        assemble_kernel,
        grid_spec=pltpu.PrefetchScalarGridSpec(
            num_scalar_prefetch=1,
            grid=(1,),
            in_specs=[held(own.shape), held(mine.shape), held(other.shape)],
            out_specs=[held(d) for d in dims],
            scratch_shapes=[pltpu.VMEM((full, columns), F32)],
        ),
        out_shape=[shape(d) for d in dims],
        compiler_params=params(1),
        cost_estimate=cost(0, 6 * full * columns),
        name="assemble",
    )(at, own, mine, other)


def join_kernel(pieces, natural, turned, whole, *, rows):
    count, half = pieces.shape[0], pieces.shape[3]
    for shard in range(count):
        for core in range(2):
            start = shard * rows + core * (rows - half)
            whole[start : start + half, :] = pieces[shard, core, 0].astype(F32)
    natural[0] = whole[...].astype(BF16)
    turned[0] = natural[0].T


def join(pieces, rows):
    count, cores, taps, half, columns = pieces.shape
    full = count * rows
    dims = [(taps, full, columns), (taps, columns, full)]
    return pl.pallas_call(
        functools.partial(join_kernel, rows=rows),
        grid=(taps,),
        in_specs=[pl.BlockSpec((count, cores, 1, half, columns), lambda t: (0, 0, t, 0, 0))],
        out_specs=[pl.BlockSpec((1, *d[1:]), lambda t: (t, 0, 0)) for d in dims],
        out_shape=[shape(d) for d in dims],
        scratch_shapes=[pltpu.VMEM((full, columns), F32)],
        compiler_params=params(1),
        cost_estimate=cost(0, 6 * taps * full * columns),
        name="join",
    )(pieces)


def spread_kernel(at, parts, out, rows, *, sizes):
    count = parts.shape[0]
    for i in range(count):
        rows[pl.ds(at[0] ^ i, 1), :] = parts[i : i + 1, :]
    start, base = 0, 0
    for size in sizes:
        for shard in range(count):
            row = rows[shard : shard + 1, start : start + size]
            out[base : base + size, :] = jnp.broadcast_to(row, (LANES, size)).T
            base += size
        start += size


def spread(at, parts, sizes):
    total = parts.size
    return pl.pallas_call(
        functools.partial(spread_kernel, sizes=sizes),
        grid_spec=pltpu.PrefetchScalarGridSpec(
            num_scalar_prefetch=1,
            grid=(1,),
            in_specs=[held(parts.shape)],
            out_specs=held((total, LANES)),
            scratch_shapes=[pltpu.VMEM(parts.shape, F32)],
        ),
        out_shape=shape((total, LANES), F32),
        compiler_params=params(1),
        cost_estimate=cost(0, 4 * LANES * total),
        name="spread",
    )(at, parts)


def after(value, *others):
    return lax.optimization_barrier((value, *others))[0] if others else value


def swapped(x):
    return lax.ppermute(x, "core", [(0, 1), (1, 0)])


def from_ws(x, bit):
    return lax.ppermute(x, "ws", [(i, i ^ bit) for i in range(lax.axis_size("ws"))])


def neighbours(first, last):
    runs = lax.axis_size("run") * 2
    up = [(i, i + 1) for i in range(runs - 1)]
    down = [(i + 1, i) for i in range(runs - 1)]
    return lax.ppermute(last, ("run", "core"), up), lax.ppermute(first, ("run", "core"), down)


def square():
    return lax.axis_size("ws") == 4 and lax.axis_size("run") == 4


def halved(rows):
    return -(-rows // 16) * 8


def fetched(shard):
    rows = shard.shape[0]
    half = halved(rows)
    own = lax.dynamic_slice_in_dim(shard, lax.axis_index("core") * (rows - half), half, axis=0)
    return [from_ws(own, bit) for bit in (1, 2, 3)]


def whole_weight(at, shard, pieces, turned=True):
    if pieces is None:
        natural = lax.all_gather(shard, "ws", axis=0, tiled=True)
        return [natural, flip(natural[None])[0]][: 1 + turned]
    mine = jnp.stack(pieces)
    return assemble(at, shard, mine, swapped(mine), turned)


def halves_of(shard, *others):
    taps, rows, columns = shard.shape
    half = halved(rows)
    own = lax.dynamic_slice_in_dim(shard, lax.axis_index("core") * (rows - half), half, axis=1)
    pieces = lax.all_gather(after(own, *others), ("ws", "core"), axis=0)
    return pieces.reshape(-1, 2, taps, half, columns)


def summed(*terms):
    total = terms[0].astype(F32)
    for term in terms[1:]:
        total = total + term.astype(F32)
    return total.astype(BF16)


def active(shard):
    return shard >> 1


class Share:
    def __init__(self, first, second):
        self.dims = first.shape
        rows = lambda x: x.reshape(-1, x.shape[-1])
        self.sum, self.second = rows(first), rows(second)

    def land(self, *kernels):
        self.sum = summed(self.sum, *after(self.came, *kernels))
        return self.sum

    def spread(self):
        near = [(2 * i + active(i), 2 * (i ^ 1) + active(i)) for i in range(4)]
        far = lambda bit: [(2 * i + 1 - active(i), 2 * (i ^ bit) + 1 - active(i)) for i in range(4)]
        move = lambda x, pairs: lax.ppermute(x, ("ws", "core"), pairs)
        self.came = (move(self.second, near), move(self.sum, far(2)), move(self.second, far(3)))

    def along(self, x, bits):
        every = []
        for shard in range(4):
            every += [((shard * 4 + i) * 2 + active(shard), (shard * 4 + (i ^ bits)) * 2 + active(shard)) for i in range(4)]
        self.came = (lax.ppermute(x, ("ws", "run", "core"), every),)

    def inward(self):
        self.along(self.sum, 1)

    def middle(self):
        self.along(self.sum, 3)

    def both(self):
        shard, core = lax.axis_index("ws"), lax.axis_index("core")
        pairs = [(2 * i + active(i), 2 * i + 1 - active(i)) for i in range(4)]
        other = lax.ppermute(self.sum, ("ws", "core"), pairs)
        return jnp.where(core == active(shard), self.sum, other).astype(F32).reshape(self.dims)


def plain(low, high, axis):
    whole = jnp.concatenate([low, high], axis=axis)
    owned = lax.psum_scatter(whole, "ws", scatter_dimension=axis, tiled=True)
    return lax.psum(owned, ("run", "core")).astype(F32)


class Small:
    def __init__(self, mine):
        self.sum = mine

    def send(self, axis, bit):
        self.came = lax.ppermute(self.sum, axis, [(i, i ^ bit) for i in range(lax.axis_size(axis))])

    def land(self, *kernels):
        self.sum = self.sum + after(self.came, *kernels)


def totals_of(count, sums1, sums2, sums3):
    every = (sums1[0], sums1[1], sums1[2], sums2[0], sums2[1], sums3[0], sums3[1])
    return jnp.concatenate([s.sum(axis=-1).reshape(count, -1) for s in every], axis=1)


def shards(
    inputs,
    cotangent,
    block_ids,
    first_gain,
    first_shift,
    weight_in,
    second_gain,
    second_shift,
    weight_conv,
    third_gain,
    third_shift,
    weight_out,
    output_bias,
):
    x = inputs.transpose(0, 2, 1)
    g = cotangent.transpose(0, 2, 1)
    count, shard, core = lax.axis_size("ws"), lax.axis_index("ws"), lax.axis_index("core")
    easy = square()
    place = jnp.stack([shard, core])
    owned_vectors = (first_gain, first_shift, output_bias, second_gain, second_shift, third_gain, third_shift)
    sizes = tuple(own.size for own in owned_vectors)
    flat = jnp.concatenate(owned_vectors)
    if easy:
        parts = jnp.stack([flat, *[from_ws(flat, bit) for bit in (1, 2, 3)]]).astype(F32)
        vectors = spread(place, parts, sizes)
    else:
        parts = lax.all_gather(flat, "ws", axis=0).astype(F32)
        vectors = spread(jnp.zeros_like(place), parts, sizes)
    in_pieces = fetched(after(weight_in, parts)) if easy else None
    conv_halves = halves_of(weight_conv) if easy else None
    act1, stats1 = open_block(x, vectors)
    length = block_ids.shape[1]
    ids_before, ids_after = neighbours(block_ids[:, :BORDER], block_ids[:, -BORDER:])
    ids = jnp.concatenate([ids_before, block_ids, ids_after], axis=1)
    same = lambda by: ids[:, BORDER + by : BORDER + by + length] == block_ids
    steps = [DILATION_STEP * (i + 1) for i in range(KERNEL_TAPS // 2)]

    def masks(sign):
        both = jnp.stack([same(sign * by) for by in steps], axis=1)
        return jnp.broadcast_to(both[..., None], (*both.shape, LANES)).astype(BF16)

    mask, mask_back = masks(1), masks(-1)
    if easy:
        mask, mask_back = after((mask, mask_back), act1)
    if easy:
        in_pieces = after(in_pieces, act1, mask, mask_back)
        out_pieces = fetched(after(weight_out, *in_pieces))
    else:
        out_pieces = None
    w_in, w_in_t = whole_weight(place, weight_in, in_pieces)
    act2, rows2, normed2, stats2 = enter(act1, w_in_t, vectors)
    halo2 = neighbours(rows2[:, :BORDER], rows2[:, -BORDER:])
    if easy:
        out_pieces = after(out_pieces, act2)
    (w_out,) = whole_weight(place, weight_out, out_pieces, False)
    if easy:
        w_conv, w_conv_t = join(after(conv_halves, w_out), weight_conv.shape[1])
    else:
        w_conv = lax.all_gather(weight_conv, "ws", axis=1, tiled=True)
        w_conv_t = flip(w_conv)
    halo2 = after(halo2, w_conv_t)
    act3, rows3, sums3 = conv_block(rows2, *halo2, mask, w_conv_t, vectors, g, w_out)
    halo = neighbours(rows3[:, :BORDER], rows3[:, -BORDER:])
    bit = shard & 1
    give, keep = jnp.stack([1 - core, bit]), jnp.stack([core, bit])
    if not easy:
        give, keep = jnp.zeros_like(give), jnp.ones_like(keep)
    seqs = x.shape[0]
    back = lambda rows, seq, number, into: conv_back(
        rows, *halo, mask_back, w_conv, vectors, normed2, stats2, seq, number, into
    )
    close = lambda low, seq, number, into: leave(low, w_in, x, g, vectors, stats1, seq, number, into)
    width, inner = x.shape[1], act2.shape[1]
    if not easy:
        conv = (act2, rows3, *halo, mask_back)
        halves = lambda **kw: [grads(at, inner, **kw)[0] for at in (give, keep)]
        out_grad = plain(*halves(pair=(act3, g)), 1)
        out_grad = out_grad.transpose(1, 0, 2).reshape(-1, width)
        conv_grad = plain(*halves(taps=tuple(range(KERNEL_TAPS)), conv=conv), 1)
        low2, sums2 = back(rows3, 0, seqs, None)
        in_grad = plain(*halves(pair=(act1, low2)), 1)[0]
        input_grad, sums1 = close(low2, 0, seqs, None)
        block_output = finish(flip(w_out[None])[0], act3, x, vectors, 0, seqs)
    else:
        shard_rows = inner // count
        padded = -(-KERNEL_TAPS * shard_rows // LANES) * LANES
        taps = tap_grads(count, padded, act2, rows3, *halo, mask_back)
        (out_send,) = grads(give, inner, pair=(after(act3, taps), g))
        w_out_t = flip(after(w_out, out_send)[None])[0]
        got_out = after(swapped(out_send), w_out_t)
        taps = lax.psum_scatter(taps.reshape(-1, inner), "ws", scatter_dimension=0, tiled=True)
        out = Share(*grads(keep, inner, pair=(act3, g), got=got_out))
        out.spread()
        low2, sums2 = back(after(rows3, out.sum), 0, seqs, None)
        out.land(low2)
        out.inward()
        (in_send,) = grads(give, inner, pair=(act1, after(low2, out.sum)))
        got_in = swapped(in_send)
        out.land(in_send)
        out.middle()
        got_in = after(got_in, out.sum)
        both = Share(*grads(keep, inner, pair=(act1, low2), got=got_in))
        both.spread()
        out.land(both.sum)
        rows = out.both()
        low2, taps = after((low2, taps), both.sum, out.sum)
        taps = lax.psum_scatter(taps, ("run", "core"), scatter_dimension=0, tiled=True)
        input_grad, sums1 = close(low2, 0, seqs, None)
        small = Small(totals_of(count, sums1, sums2, sums3))
        small.send("core", 1)
        both.land(sums1)
        both.inward()
        small.land(both.sum)
        small.send("run", 1)
        small.land()
        small.send("run", 2)
        (w_out_t, act3), taps = after(((w_out_t, act3), taps), both.sum, small.sum, rows)
        taps_sum = lax.all_gather(taps, ("run", "core"), axis=0, tiled=True)
        block_output = finish(w_out_t, act3, x, vectors, 0, seqs)
        small.land(block_output)
        both.land(block_output, small.sum)
        small.send("ws", 1)
        both.middle()
        small.land(both.sum)
        small.send("ws", 2)
        small.land()
        taps = taps_sum[: KERNEL_TAPS * shard_rows].astype(F32)
        conv_grad = taps.reshape(KERNEL_TAPS, shard_rows, inner)
        out_grad = jnp.concatenate([rows[0], rows[1]], axis=1)
        both.land(small.sum, taps_sum, out_grad)
        in_grad = both.both().reshape(-1, inner)
        small = small.sum

    if not easy:
        small = lax.psum(totals_of(count, sums1, sums2, sums3), ("ws", "run", "core"))
    small = lax.dynamic_index_in_dim(small, shard, axis=0, keepdims=False)
    at, vector_grads = 0, []
    for size in sizes:
        vector_grads.append(small[at : at + size])
        at += size
    gain1, shift1, bias, gain2, shift2, gain3, shift3 = vector_grads
    return (
        block_output.transpose(0, 2, 1),
        input_grad.transpose(0, 2, 1),
        gain1,
        shift1,
        in_grad,
        gain2,
        shift2,
        conv_grad,
        gain3,
        shift3,
        out_grad,
        bias,
    )


def solution(mesh):
    count, runs = mesh.devices.shape
    split = jax.sharding.Mesh(mesh.devices.reshape(count, runs // 2, 2), ("ws", "run", "core"))
    tokens = P("ws", ("run", "core"), None)
    rows = P("ws", None)
    taps = P(None, "ws", None)
    placed = (tokens, tokens, P("ws", ("run", "core")), P("ws"), P("ws"), rows, P("ws"), P("ws"), taps)
    placed += (P("ws"), P("ws"), rows, P("ws"))
    given = (tokens, tokens, P("ws"), P("ws"), rows, P("ws"), P("ws"), taps, P("ws"), P("ws"), rows, P("ws"))
    return jax.shard_map(shards, mesh=split, in_specs=placed, out_specs=given, check_vma=False)
```
